32 devices in a mesh: rep: 4 (over y, core), shard: 8 (over z, x).
Axes of the slice: x: 2, y: 2, z: 4, core: 2. Of those that a mesh axis runs over, the one named last changes fastest.
Arguments:
- tokens: bfloat16 [8192, 1280], P(('rep', 'shard')), may hold values from -6 to 6
- lengths: int32 [4, 13], P('rep'), may hold values from 1 to 512, 2048 in all within a row
- parents: int32 [4, 13], P('rep'), may hold values from 0 to 11, as said below
- w_query: bfloat16 [1280, 1280], P('shard'), may hold values from -0.15625 to 0.15625
- w_key: bfloat16 [1280, 1280], P('shard'), may hold values from -0.15625 to 0.15625
- w_value: bfloat16 [1280, 1280], P('shard'), may hold values from -0.15625 to 0.15625
- w_out: bfloat16 [1280, 1280], P('shard'), may hold values from -1 to 1
- w_up: bfloat16 [1280, 1280], P('shard'), may hold values from -0.15625 to 0.15625
- w_down: bfloat16 [1280, 1280], P('shard'), may hold values from -0.15625 to 0.15625
- gain_attn: float32 [1280], replicated, may hold values from 0.1 to 1.9
- gain_ff: float32 [1280], replicated, may hold values from 0.1 to 1.9
- query_scale: float32 [80], replicated, may hold values from 0 to 2
- bias_query: float32 [1280], replicated, may hold values from -3 to 3
- bias_value: float32 [1280], replicated, may hold values from -3 to 3
- bias_out: float32 [1280], replicated, may hold values from -3 to 3
- bias_up: float32 [1280], replicated, may hold values from -3 to 3
- bias_down: float32 [1280], replicated, may hold values from -3 to 3
- cotangent: bfloat16 [8192, 1280], P(('rep', 'shard')), may hold values from -6 to 6
Outputs:
- output: bfloat16 [8192, 1280], P(('rep', 'shard'))
- grad_tokens: bfloat16 [8192, 1280], P(('rep', 'shard'))
- grad_query: float32 [1280, 1280], P('shard')
- grad_key: float32 [1280, 1280], P('shard')
- grad_value: float32 [1280, 1280], P('shard')
- grad_out: float32 [1280, 1280], P('shard')
- grad_up: float32 [1280, 1280], P('shard')
- grad_down: float32 [1280, 1280], P('shard')
- grad_gain_attn: float32 [1280], replicated
- grad_gain_ff: float32 [1280], replicated
- grad_query_scale: float32 [80], replicated
- grad_bias_query: float32 [1280], replicated
- grad_bias_value: float32 [1280], replicated
- grad_bias_out: float32 [1280], replicated
- grad_bias_up: float32 [1280], replicated
- grad_bias_down: float32 [1280], replicated
The draws below stay inside these ranges and needn't reach their ends.
Inputs may be any that keep to these rules, and one draw needn't show every extreme that they name: parents[g, 0] = 0 and parents[g, s] < s for s >= 1; the last segment's parent is the segment before it. `lengths`: each row sums to 2048.
All inputs are finite; a program needn't handle non-finite values.
Results may differ from the reference program's by a relative error of at most 0.02.
Values may be sent and summed in bfloat16 or wider, within the bound.
A program may use at most 256 MiB of HBM per device.

```python
import math
import jax
import jax.numpy as jnp
import numpy as np
from jax import lax

D = 1280
HEADS = 16
HEAD_DIM = 80
FF = 1280
SEGS = 13
TREE = 2048
TOKENS = 8192
N_REP = 4


def draw_parents(key, part):
    key = jax.random.fold_in(key, 11)
    labels = jnp.arange(SEGS, dtype=jnp.int32)
    raw_draw = jax.random.randint(key, (N_REP, SEGS), 0, 1 << 20, dtype=jnp.int32)
    chosen = raw_draw % jnp.maximum(labels, 1)[None, :]
    chosen = jnp.where(labels[None, :] == SEGS - 1, SEGS - 2, chosen)
    return chosen.astype(jnp.int32)


def steps_of(key, shape, cuts, smallest, high):
    loudness, own = 1.0, jax.random.fold_in(key, 6)
    for position, blocks in cuts:
        draws = jnp.exp(jax.random.uniform(jax.random.fold_in(own, position), (blocks,), jnp.float32, smallest / len(cuts), high / len(cuts)))
        loudness = loudness * jnp.repeat(draws, shape[position] // blocks).reshape([-1 if axis == position else 1 for axis in range(len(shape))])
    return loudness


def length_profile(count, total, limit, slope):
    loads = [(1 << 20) // math.isqrt(grade ** slope) + 1 for grade in range(2, count + 1)]
    spare, given = total - limit - (count - 1), [1] * (count - 1)
    while spare > 0:
        free = [i for i in range(count - 1) if given[i] < limit]
        whole, remaining = sum([loads[i] for i in free]), spare
        for i in free:
            extra = min(limit - given[i], max(1, remaining * loads[i] // whole), spare)
            given[i] = given[i] + extra
            spare = spare - extra
    return np.array([limit] + given)


def uneven(rng, number_of, total, limit, skew):
    if number_of == 2:
        one = jax.random.randint(rng, (), max(1, total - limit), min(limit, total - 1) + 1)
        return jnp.stack([one, total - one])
    sizes = jnp.asarray(length_profile(number_of, total, limit, skew), jnp.int32)
    pairs = (number_of - 1) // 2
    donor, taker = sizes[1:1 + 2 * pairs:2], sizes[2:2 + 2 * pairs:2]
    room = jnp.minimum(donor - 1, limit - taker)
    moved = jax.random.randint(jax.random.fold_in(rng, 1), (pairs,), 0, 1 << 20) % (room + 1)
    sizes = sizes.at[1:1 + 2 * pairs:2].set(donor - moved).at[2:2 + 2 * pairs:2].set(taker + moved)
    return sizes[jax.random.permutation(jax.random.fold_in(rng, 2), number_of)]


def noise(rng, shape, width, reach, split=(), held_as=jnp.bfloat16):
    array = width * jax.random.normal(rng, shape, jnp.float32)
    if split:
        array = array * steps_of(rng, shape, split, -0.22, 0.18)
    return jnp.clip(array, -reach, reach).astype(held_as)


def setup_inputs(seed: int = 0) -> dict:
    keys = jax.random.split(jax.random.key(seed), 19)
    return {
        "tokens": noise(keys[0], (TOKENS, D), 1.0, 6.0, ((0, 32),)),
        "lengths": jax.vmap(lambda own: uneven(own, SEGS, TREE, TREE // 4, 2))(jax.random.split(keys[1], N_REP)).reshape((N_REP, SEGS)).astype(jnp.int32),
        "parents": draw_parents(jax.random.fold_in(keys[18], 71), 0),
        "w_query": noise(keys[3], (D, D), D ** -0.5, 0.15625, ((0, 8),)),
        "w_key": noise(keys[4], (D, D), D ** -0.5, 0.15625, ((0, 8),)),
        "w_value": noise(keys[5], (D, D), D ** -0.5, 0.15625, ((0, 8),)),
        "w_out": noise(keys[6], (D, D), (D // 32) ** -0.5, 1.0, ((0, 8),)),
        "w_up": noise(keys[7], (D, FF), D ** -0.5, 0.15625, ((0, 8),)),
        "w_down": noise(keys[8], (FF, D), FF ** -0.5, 0.15625, ((0, 8),)),
        "gain_attn": jnp.clip(1.0 + 0.18 * jax.random.normal(keys[9], (D,), jnp.float32), 0.1, 1.9),
        "gain_ff": jnp.clip(1.0 + 0.18 * jax.random.normal(keys[10], (D,), jnp.float32), 0.1, 1.9),
        "query_scale": jnp.clip(jax.random.uniform(keys[11], (HEAD_DIM,), jnp.float32, 0.0, 2.0), 0.0, 2.0),
        "bias_query": noise(keys[12], (D,), 0.5, 3.0, (), jnp.float32),
        "bias_value": noise(keys[13], (D,), 0.5, 3.0, (), jnp.float32),
        "bias_out": noise(keys[14], (D,), 0.5, 3.0, (), jnp.float32),
        "bias_up": noise(keys[15], (FF,), 0.5, 3.0, (), jnp.float32),
        "bias_down": noise(keys[16], (D,), 0.5, 3.0, (), jnp.float32),
        "cotangent": noise(keys[17], (TOKENS, D), 1.0, 6.0, ((0, 32),)),
    }


@jax.custom_vjp
def low(v):
    return lax.optimization_barrier(v.astype(jnp.bfloat16)).astype(jnp.float32)

@jax.custom_vjp
def low_back(v):
    return v

def low_keep(v):
    return (low(v), None)

def low_pass(kept, grad):
    return (grad,)

def back_keep(v):
    return (v, None)

def back_low(kept, grad):
    return (low(grad),)
low.defvjp(low_keep, low_pass)
low_back.defvjp(back_keep, back_low)
norm_eps = 1e-06
query_base = 1.442695
masked_score = -1e+30
highest = lax.Precision.HIGHEST

def exact_dot(left, right):
    return jnp.dot(left, right, precision=highest)

def rms_scale(values, gain):
    return values * lax.rsqrt(lax.optimization_barrier(jnp.mean(values * values, axis=-1, keepdims=True)) + norm_eps) * gain

def tree_tables(lengths, parents):
    seg_ends = jnp.cumsum(lengths, dtype=jnp.int32)
    segments = lengths.shape[0]
    labels = jnp.arange(segments, dtype=jnp.int32)
    link = ((parents[:, None] == labels[None, :]) & (labels[:, None] > 0)).astype(jnp.float32)
    identity = jnp.eye(segments, dtype=jnp.float32)
    ancestry = identity
    for depth_step in range(segments):
        ancestry = jnp.minimum(identity + exact_dot(link, ancestry), 1.0)
    return (seg_ends, ancestry)

def segment_onehot(positions, seg_ends):
    labels = lax.optimization_barrier(jnp.sum((positions[:, None] >= seg_ends[None, :]).astype(jnp.int32), axis=1))
    return (labels[:, None] == jnp.arange(seg_ends.shape[0], dtype=jnp.int32)[None, :]).astype(jnp.float32)

def allowed_pairs(query_pos, key_pos, seg_ends, ancestry):
    query_reach = exact_dot(segment_onehot(query_pos, seg_ends), ancestry)
    linked = exact_dot(query_reach, segment_onehot(key_pos, seg_ends).T) > 0.5
    return linked & (key_pos[None, :] <= query_pos[:, None])

def attend(queries, key_rows, value_rows, seg_ends, ancestry):
    length = queries.shape[0]
    block_size = min(512, length)
    key_pos = jnp.arange(length, dtype=jnp.int32)

    def one_block(block_in):
        query_block, offset = block_in
        query_pos = offset + jnp.arange(block_size, dtype=jnp.int32)
        allowed = allowed_pairs(query_pos, key_pos, seg_ends, ancestry)
        scores = low_back(jnp.einsum('qhd,khd->hqk', query_block, key_rows, precision=highest))
        scores = jnp.where(allowed[None], scores, masked_score)
        row_max = lax.optimization_barrier(jnp.max(scores, axis=2, keepdims=True))
        exponent = jnp.where(allowed[None], jnp.exp(scores - row_max), 0.0)
        weights = low(exponent / lax.optimization_barrier(jnp.sum(exponent, axis=2, keepdims=True)))
        return jnp.einsum('hqk,khd->qhd', weights, value_rows, precision=highest)
    blocks = queries.reshape(length // block_size, block_size, queries.shape[1], queries.shape[2])
    offsets = jnp.arange(length // block_size, dtype=jnp.int32) * block_size
    mixed_rows = lax.map(jax.checkpoint(one_block), (blocks, offsets))
    return mixed_rows.reshape(length, queries.shape[1] * queries.shape[2])

def group_layer(params, group_in, seg_ends, ancestry):
    w_query, w_key, w_value, w_out, w_up, w_down, gain_attn, gain_ff, query_scale, bias_query, bias_value, bias_out, bias_up, bias_down = params
    length = group_in.shape[0]
    attn_in = low(rms_scale(group_in, gain_attn))
    query_gain = query_base * jax.nn.softplus(query_scale) / math.sqrt(HEAD_DIM)
    query_pre = low_back(exact_dot(attn_in, w_query) + bias_query).reshape(length, HEADS, HEAD_DIM)
    queries = low(query_pre * query_gain)
    key_rows = low(low_back(exact_dot(attn_in, w_key))).reshape(length, HEADS, HEAD_DIM)
    value_rows = low(low_back(exact_dot(attn_in, w_value) + bias_value)).reshape(length, HEADS, HEAD_DIM)
    attn_rows = low(low_back(attend(queries, key_rows, value_rows, seg_ends, ancestry)))
    middle = group_in + low_back(exact_dot(attn_rows, w_out) + bias_out)
    ff_in = low(rms_scale(middle, gain_ff))
    hidden = low(jax.nn.silu(low_back(exact_dot(ff_in, w_up) + bias_up)))
    return middle + low_back(exact_dot(hidden, w_down) + bias_down)

def reference(tokens, lengths, parents, w_query, w_key, w_value, w_out, w_up, w_down, gain_attn, gain_ff, query_scale, bias_query, bias_value, bias_out, bias_up, bias_down, cotangent):
    seg_ends, ancestry = jax.vmap(tree_tables)(lengths, parents)
    params = (w_query.astype(jnp.float32), w_key.astype(jnp.float32), w_value.astype(jnp.float32), w_out.astype(jnp.float32), w_up.astype(jnp.float32), w_down.astype(jnp.float32), gain_attn, gain_ff, query_scale, bias_query, bias_value, bias_out, bias_up, bias_down)
    inputs = tokens.astype(jnp.float32)

    def whole_layer(layer_in, layer_params):
        groups = layer_in.reshape(N_REP, TREE, D)

        def one_group(group_args):
            group_in, group_ends, group_ancestry = group_args
            return group_layer(layer_params, group_in, group_ends, group_ancestry)
        results = lax.map(jax.checkpoint(one_group), (groups, seg_ends, ancestry))
        return results.reshape(N_REP * TREE, D)
    output, pull_back = jax.vjp(whole_layer, inputs, params)
    grad_in, grads = pull_back(cotangent.astype(jnp.float32))
    return (output.astype(jnp.bfloat16), grad_in.astype(jnp.bfloat16), grads[0], grads[1], grads[2], grads[3], grads[4], grads[5], grads[6], grads[7], grads[8], grads[9], grads[10], grads[11], grads[12], grads[13])
```

```python
import functools
import math

import jax
import jax.numpy as jnp
from jax import lax
from jax.experimental import pallas as pl
from jax.experimental.pallas import tpu as pltpu
from jax.sharding import PartitionSpec as P

HEADS = 16
HEAD_DIM = 80
MESH = pl.DeviceIdType.MESH
F32 = jnp.float32
BF16 = jnp.bfloat16

norm_eps = 1e-06
query_base = 1.442695
masked_score = -1e30
LABELS = 16
COPIES = 700
VMEM_BYTES = 64 << 20


def dot(left, right):
    return jnp.dot(left, right, preferred_element_type=F32)


def dot_nt(left, right):
    return lax.dot_general(left, right, (((1,), (1,)), ((), ())), preferred_element_type=F32)


def when(condition, body):
    if condition is True:
        body()
    elif condition is not False:
        pl.when(condition)(body)


class Copy:
    def __init__(self, make, sends, receives):
        self.make, self.sends, self.receives = make, sends, receives

    def start(self):
        when(self.sends, lambda: self.make().start())

    def arrived(self):
        when(self.receives, lambda: self.make().wait_recv())

    def sent(self):
        when(self.sends, lambda: self.make().wait_send())


class Links:
    def __init__(self, send_sems, recv_sems):
        self.send_sems, self.recv_sems, self.used, self.copies = send_sems, recv_sems, 0, []

    def block(self, count):
        first = self.used
        self.used += count
        assert self.used <= COPIES
        return first

    def copy(self, src, dst, device, sends=True, receives=True, index=None, keep=True):
        if index is None:
            index = self.block(1)

        def make():
            return pltpu.make_async_remote_copy(
                src_ref=src,
                dst_ref=dst,
                send_sem=self.send_sems.at[index],
                recv_sem=self.recv_sems.at[index],
                device_id=device,
                device_id_type=MESH,
            )

        made = Copy(make, sends, receives)
        if keep:
            self.copies.append(made)
        return made


def layer_kernel(dims, refs):
    R, S, L, D = dims["R"], dims["S"], dims["L"], dims["D"]
    HG, E, CW, SR, H, SRH = (dims[k] for k in ("HG", "E", "CW", "SR", "H", "SRH"))
    q, U, A, T = S // R, R // 2, R, S * L
    HD = HEAD_DIM
    HALF, DH = L // 2, D // 2
    W = 256
    NW = D // W
    ref = refs
    r, s = lax.axis_index("rep"), lax.axis_index("shard")
    u, c, a, b = r // 2, r % 2, s // q, s % q

    def rho(i):
        return (i % 2) * (R // 2) + i // 2

    def rho_back(j):
        return (j % (R // 2)) * 2 + j // (R // 2)

    def device(r2, a2, b2):
        return (r2, a2 * q + b2)

    def peer(u2, c2, b2):
        return device(u2 * 2 + c2, a, b2)

    def block_of(u2, c2, b2):
        return rho(u2 * 2 + c2) * q + b2

    def rows_of(blk):
        return pl.ds(pl.multiple_of(blk * L, L), L)

    g = r * q + b
    blk = block_of(u, c, b)
    u_off = [(u + d) % U for d in range(U)]
    b_off = [(b + d) % q for d in range(q)]
    u_from = [(u + U - d) % U for d in range(U)]
    b_from = [(b + q - d) % q for d in range(q)]
    home_r, home_a = rho_back(a), rho(r)
    home = device(home_r, home_a, b)
    stays = jnp.logical_and(home_r == r, home_a == a)
    moves = jnp.logical_not(stays)
    sibling = peer(u, 1 - c, b)
    above = device(r, jnp.minimum(a + 1, A - 1), b)
    below = device(r, jnp.maximum(a - 1, 0), b)
    own_half = pl.ds(pl.multiple_of(c * DH, 128), DH)
    other_half = pl.ds(pl.multiple_of((1 - c) * DH, 128), DH)

    links = Links(ref["send_sems"], ref["recv_sems"])

    barrier = pltpu.get_barrier_semaphore()

    def greet(where):
        pl.semaphore_signal(barrier, inc=1, device_id=where, device_id_type=MESH)

    for k in range(1, S):
        g2 = (g + k) % S
        greet(device(g2 // q, a, g2 % q))
    for k in range(1, A):
        greet(device(r, (a + k) % A, b))
    pl.when(moves)(lambda: greet(home))
    pl.semaphore_wait(barrier, S - 1 + A - 1 + jnp.where(moves, 1, 0))

    swaps = []
    for name, there in (("tokens", "tok"), ("tab", "tabs"), ("cotangent", "cot")):
        swaps.append(links.copy(ref[name], ref[there], home, moves, moves))

    local_sems = ref["local_sems"]

    def local(src, dst, n):
        return pltpu.make_async_copy(src, dst, local_sems.at[n])

    def keep_rows():
        kept = [
            local(ref["tokens"], ref["tok"], 0),
            local(ref["tab"], ref["tabs"], 1),
            local(ref["cotangent"], ref["cot"], 2),
        ]
        for copy in kept:
            copy.start()
        for copy in kept:
            copy.wait()

    swaps[0].start()
    swaps[1].start()

    wq, wqt, wcat = ref["wq"], ref["wqt"], ref["wcat"]

    def wq_rows(a2, b2):
        return pl.ds(pl.multiple_of((a2 * q + b2) * SR, 16), SR)

    def near(src, name, n):
        if dims["fits"]:
            return src
        copy = local(src, ref[name], n)
        copy.start()
        copy.wait()
        return ref[name]

    own_wq = local(wcat.at[g], wq.at[wq_rows(a, b)], 3)
    own_wq.start()
    wcat_b = {}
    for db in range(1, q):
        wcat_b[db] = links.copy(
            wcat.at[r * q + b_off[db]], wq.at[wq_rows(a, b)], device(r, a, b_off[db])
        )
        wcat_b[db].start()
    up_q, down_q = {}, {}
    for k in range(A - 1):
        for db in range(q):
            low, high = jnp.maximum(a - k, 0), jnp.minimum(a + k, A - 1)
            slot = wq_rows(low, b_from[db])
            up_q[k, db] = links.copy(
                wq.at[slot], wq.at[slot], above,
                jnp.logical_and(a - k >= 0, a < A - 1), a - 1 - k >= 0,
            )
            slot = wq_rows(high, b_from[db])
            down_q[k, db] = links.copy(
                wq.at[slot], wq.at[slot], below,
                jnp.logical_and(a + k <= A - 1, a > 0), a + 1 + k <= A - 1,
            )
    own_wq.wait()
    up_q[0, 0].start()
    down_q[0, 0].start()

    def wq_pass(k):
        for db in range(q):
            up_q[k, db].arrived()
            down_q[k, db].arrived()
            if k + 1 < A - 1:
                up_q[k + 1, db].start()
                down_q[k + 1, db].start()

    w3 = ref["w3"]
    shards = (ref["w_out"], ref["w_up"], ref["w_down"])

    def shard_rows(a2, b2):
        return pl.ds(pl.multiple_of((a2 * q + b2) * SR, 16), SR)

    def piece_rows(a2, b2, u2):
        if H == 1:
            return shard_rows(a2, b2)
        return pl.ds(pl.multiple_of((a2 * q + b2) * SR + u2 * SRH, 16), SRH)

    own_shards = [local(shards[w], w3.at[w, shard_rows(a, b)], 4 + w) for w in range(3)]
    for copy in own_shards:
        copy.start()
    for copy in own_shards:
        copy.wait()
    pl.when(stays)(keep_rows)
    up_w, down_w, side_w, own_w, core_w, core_own = {}, {}, {}, {}, {}, {}
    slots = [sign * k for k in range(1, A) for sign in (1, -1)]
    for w in range(3):
        for k in range(A - 1):
            low, high = jnp.maximum(a - k, 0), jnp.minimum(a + k, A - 1)
            at = w3.at[w, piece_rows(low, b, u), own_half]
            up_w[w, k] = links.copy(
                at, at, above, jnp.logical_and(a - k >= 0, a < A - 1), a - 1 - k >= 0
            )
            at = w3.at[w, piece_rows(high, b, u), own_half]
            down_w[w, k] = links.copy(
                at, at, below, jnp.logical_and(a + k <= A - 1, a > 0), a + 1 + k <= A - 1
            )
        for slot in slots:
            valid = a + slot <= A - 1 if slot > 0 else a + slot >= 0
            a0 = jnp.clip(a + slot, 0, A - 1)
            at = w3.at[w, piece_rows(a0, b, u), own_half]
            for db in range(1, q):
                side_w[w, slot, 0, db] = links.copy(at, at, peer(u, c, b_off[db]), valid, valid)
            if H > 1:
                for du in range(1, U):
                    side_w[w, slot, du, 0] = links.copy(at, at, peer(u_off[du], c, b), valid, valid)
                    for db in range(1, q):
                        passed = w3.at[w, piece_rows(a0, b_from[db], u), own_half]
                        side_w[w, slot, du, db] = links.copy(
                            passed, passed, peer(u_off[du], c, b), valid, valid
                        )
            at = w3.at[w, pl.ds(pl.multiple_of(a0 * q * SR, 16), q * SR), own_half]
            core_w[w, slot] = links.copy(at, at, sibling, valid, valid)
        for db in range(1, q):
            at = w3.at[w, shard_rows(a, b), own_half]
            own_w[w, db] = links.copy(at, at, peer(u, c, b_off[db]))
            at = w3.at[w, shard_rows(a, b_from[db]), own_half]
            core_own[w, db] = links.copy(at, at, sibling)

    def w3_line(w, k):
        if k < 0:
            up_w[w, 0].start()
            down_w[w, 0].start()
            for db in range(1, q):
                own_w[w, db].start()
            return
        up_w[w, k].arrived()
        down_w[w, k].arrived()
        if k + 1 < A - 1:
            up_w[w, k + 1].start()
            down_w[w, k + 1].start()
        for slot in (-(k + 1), k + 1):
            for (w2, slot2, du, db), moved in side_w.items():
                if (w2, slot2) == (w, slot) and (du == 0 or db == 0):
                    moved.start()

    def w3_side(w, k):
        if k < 0:
            for db in range(1, q):
                own_w[w, db].arrived()
                core_own[w, db].start()
            return
        for slot in (-(k + 1), k + 1):
            for db in range(1, q):
                side_w[w, slot, 0, db].arrived()
                if H > 1:
                    for du in range(1, U):
                        side_w[w, slot, du, db].start()

    def w3_core(w, k):
        for slot in (-(k + 1), k + 1):
            if H > 1:
                for du in range(1, U):
                    side_w[w, slot, du, 0].arrived()
                    for db in range(1, q):
                        side_w[w, slot, du, db].arrived()
            core_w[w, slot].start()

    def w3_whole(w):
        for db in range(1, q):
            core_own[w, db].arrived()
        for slot in slots:
            core_w[w, slot].arrived()

    tok, cot, xa = ref["tok"], ref["cot"], ref["xa"]
    gains = ref["gains"]
    gain_attn, gain_ff = gains[0:1, :], gains[1:2, :]
    STEP = 32

    def unit(x):
        return lax.rsqrt(jnp.mean(x * x, axis=-1, keepdims=True) + norm_eps)

    def half_rows(block, h):
        return pl.ds(pl.multiple_of(block * L + h * HALF, HALF), HALF)

    own_x, pass_x, sib_x = {}, {}, {}
    for h in range(2):
        at = xa.at[half_rows(blk, h)]
        for db in range(1, q):
            own_x[h, 0, db] = links.copy(at, at, peer(u, c, b_off[db]))
        for du in range(1, U):
            own_x[h, du, 0] = links.copy(at, at, peer(u_off[du], c, b))
        for du in range(1, U):
            for db in range(1, q):
                if h == 0:
                    at = xa.at[half_rows(block_of(u, c, b_from[db]), h)]
                    pass_x[h, du, db] = links.copy(at, at, peer(u_off[du], c, b))
                else:
                    at = xa.at[half_rows(block_of(u_from[du], c, b), h)]
                    pass_x[h, du, db] = links.copy(at, at, peer(u, c, b_off[db]))
        for du in range(U):
            for db in range(q):
                at = xa.at[half_rows(block_of(u_from[du], c, b_from[db]), h)]
                sib_x[h, du, db] = links.copy(at, at, sibling)

    swaps[0].arrived()
    for h in range(2):

        def norm_step(i, carried, h=h):
            here = pl.ds(pl.multiple_of(h * HALF + i * STEP, STEP), STEP)
            x = tok[here, :].astype(F32)
            there = pl.ds(pl.multiple_of(blk * L + h * HALF + i * STEP, STEP), STEP)
            row = (x * unit(x) * gain_attn).astype(BF16)
            if dims["fits"]:
                xa[there, :] = row
            else:
                ref["x_rows"][here, :] = row
            return carried

        lax.fori_loop(0, HALF // STEP, norm_step, 0)
        if not dims["fits"]:
            here = pl.ds(h * HALF, HALF)
            out_of = local(ref["x_rows"].at[here], xa.at[half_rows(blk, h)], 7)
            out_of.start()
            out_of.wait()
        for moved in [m for (h2, *_), m in own_x.items() if h2 == h]:
            moved.start()
        sib_x[h, 0, 0].start()

    for db in range(1, q):
        wcat_b[db].arrived()
        up_q[0, db].start()
        down_q[0, db].start()
    swaps[2].start()
    for w in range(3):
        w3_line(w, -1)

    swaps[1].arrived()
    lane = lax.broadcasted_iota(jnp.int32, (LABELS, 128), 1)
    row = lax.broadcasted_iota(jnp.int32, (LABELS, 128), 0)
    lengths = jnp.broadcast_to(ref["tabs"][0:1, :], (LABELS, 128))
    seg_start = jnp.sum(jnp.where(lane < row, lengths, 0.0), axis=1, keepdims=True)
    seg_end = jnp.sum(jnp.where(lane <= row, lengths, 0.0), axis=1, keepdims=True)
    lane = lax.broadcasted_iota(jnp.int32, (128, 128), 1)
    row = lax.broadcasted_iota(jnp.int32, (128, 128), 0)
    parents = jnp.broadcast_to(ref["tabs"][1:2, :], (128, 128))
    segments = dims["segments"]
    is_parent = (parents == row.astype(F32)) & (lane > 0) & (lane < segments)
    reach = jnp.where((lane == row) | is_parent, 1.0, 0.0)
    for _ in range(max(1, (segments - 1).bit_length())):
        reach = jnp.minimum(dot(reach.astype(BF16), reach.astype(BF16)), 1.0)
    blocked = ((1.0 - reach[:LABELS, :LABELS]) * masked_score).astype(BF16)

    for db in range(1, q):
        own_x[0, 0, db].arrived()
        for du in range(1, U):
            pass_x[0, du, db].start()
        sib_x[0, 0, db].start()
    for du in range(1, U):
        own_x[1, du, 0].arrived()
        for db in range(1, q):
            pass_x[1, du, db].start()
        sib_x[1, du, 0].start()
    wq_pass(0)
    for db in range(1, q):
        own_x[1, 0, db].arrived()
        sib_x[1, 0, db].start()
    for du in range(1, U):
        own_x[0, du, 0].arrived()
        sib_x[0, du, 0].start()
    for k in range(1, A - 1):
        wq_pass(k)
    for w in range(3):
        w3_side(w, -1)
    w3_line(0, 0)
    for h in range(2):
        for du in range(1, U):
            for db in range(1, q):
                pass_x[h, du, db].arrived()
                sib_x[h, du, db].start()
    w3_line(1, 0)
    w3_line(2, 0)

    def turn_wq(i, carried):
        here = pl.ds(pl.multiple_of(i * W, W), W)
        wqt[:, here] = wq[here, :].T
        return carried

    lax.fori_loop(0, NW, turn_wq, 0)
    bias_col = jnp.transpose(ref["biascat"][g])[:, 0:1]
    qgain_col = jnp.transpose(ref["qgain"][...])[:, 0:1]
    qkvf, qpre, qt, keys, kt, vals, vt = (
        ref[k] for k in ("qkvf", "qpre", "qt", "keys", "kt", "vals", "vt")
    )

    def project(k, carried):
        for j in range(S):

            def wait_rows(j=j):
                du, db, other = (j // 2) // q, (j // 2) % q, j % 2
                if other:
                    for h in range(2):
                        sib_x[h, du, db].arrived()

            pl.when(k == j)(wait_rows)
        du, db, other = (k // 2) // q, (k // 2) % q, k % 2
        block = block_of((u + U - du) % U, (c + other) % 2, (b + q - db) % q)
        cols = rows_of(block)
        x = near(xa.at[cols], "x_rows", 7)[...]
        qkvf[...] = dot_nt(wqt[...], x) + bias_col
        place = block * L + lax.broadcasted_iota(jnp.int32, (LABELS, L), 1)
        place = place.astype(F32)
        onehot = jnp.where((place >= seg_start) & (place < seg_end), 1.0, 0.0)
        far = dot(blocked, onehot.astype(BF16)).astype(BF16)
        for hd in range(HG):
            head = pl.ds(hd * HD, HD)
            pre = qkvf[head, :]
            qpre[head, cols] = pre
            qt[hd, 0:HD, cols] = (pre * qgain_col[hd * HD : (hd + 1) * HD]).astype(BF16)
            qt[hd, HD : HD + LABELS, cols] = far
            qt[hd, HD + LABELS : 128, cols] = jnp.zeros((128 - HD - LABELS, L), BF16)
            key = qkvf[pl.ds(E + hd * HD, HD), :]
            kt[hd, :, cols] = key.astype(BF16)
            wide = jnp.concatenate([key, onehot, jnp.zeros((128 - HD - LABELS, L), F32)], axis=0)
            keys[hd, cols, :] = wide.T.astype(BF16)
            value = qkvf[pl.ds(2 * E + hd * HD, HD), :]
            vt[hd, :, cols] = value.astype(BF16)
            wide = jnp.concatenate([value, jnp.zeros((128 - HD, L), F32)], axis=0)
            vals[hd, cols, :] = wide.T.astype(BF16)
        return carried

    lax.fori_loop(0, S, project, 0)

    ot, otb, lse, oa = ref["ot"], ref["otb"], ref["lse"], ref["oa"]
    first_o = links.block(S)
    diagonal = lax.broadcasted_iota(jnp.int32, (L, L), 0) <= lax.broadcasted_iota(
        jnp.int32, (L, L), 1
    )
    o_slot = pl.ds(pl.multiple_of(g * E, 16), E)

    def o_copy(block):
        r2, b2 = rho_back(block // q), block % q
        index = first_o + (r2 * q + b2 + S - g) % S
        return links.copy(
            otb.at[:, rows_of(block)], oa.at[o_slot], device(r2, a, b2), index=index, keep=False
        )

    services = {}

    def serve(at, job):
        services.setdefault(at, []).append(job)

    for k in range(A - 1):
        for w in range(3):
            at = min(S - 1, 2 * k + (w + 1) // 2)
            serve(at, functools.partial(w3_side, w, k))
            if k + 1 < A - 1:
                serve(at, functools.partial(w3_line, w, k + 1))
            serve(min(S - 1, at + 1), functools.partial(w3_core, w, k))

    def attend(i, carried):
        cols = rows_of(i)
        query = [qt[hd, :, cols] for hd in range(HG)]

        def key_block(j, state, on_diagonal):
            here = rows_of(j)
            result = []
            for hd in range(HG):
                top, total, acc = state[hd]
                score = dot(keys[hd, here, :], query[hd])
                if on_diagonal:
                    score = jnp.where(diagonal, score, masked_score)
                new_top = jnp.maximum(top, jnp.max(score, axis=0, keepdims=True))
                p = jnp.exp(score - new_top)
                fade = jnp.exp(top - new_top)
                total = total * fade + jnp.sum(p, axis=0, keepdims=True)
                acc = acc * fade + dot(vt[hd, :, here], p.astype(BF16))
                result.append((new_top, total, acc))
            return tuple(result)

        start = tuple(
            (
                jnp.full((1, L), masked_score, F32),
                jnp.zeros((1, L), F32),
                jnp.zeros((HD, L), F32),
            )
            for _ in range(HG)
        )
        state = lax.fori_loop(0, i, functools.partial(key_block, on_diagonal=False), start)
        state = key_block(i, state, True)
        for hd in range(HG):
            top, total, acc = state[hd]
            mixed = acc / total
            head = pl.ds(hd * HD, HD)
            ot[head, cols] = mixed
            otb[head, cols] = mixed.astype(BF16)
            lse[hd, :, cols] = jnp.broadcast_to(top + jnp.log(total), (8, L))

        def keep_block():
            oa[o_slot, :] = otb[:, cols]

        pl.when(i == blk)(keep_block)
        pl.when(i != blk)(lambda: o_copy(i).start())
        for j in sorted(services):

            def run(j=j):
                for job in services[j]:
                    job()

            pl.when(i == j)(run)
        return carried

    lax.fori_loop(0, S, attend, 0)

    def o_arrived(k, carried):
        links.copy(
            otb.at[:, rows_of(0)], oa.at[o_slot], sibling, index=first_o + k, keep=False
        ).make().wait_recv()
        return carried

    lax.fori_loop(1, S, o_arrived, 0)

    def o_sent(i, carried):
        pl.when(i != blk)(lambda: o_copy(i).sent())
        return carried

    otok, mid, ffin, up, hid, outb = (ref[k] for k in ("otok", "mid", "ffin", "up", "hid", "outb"))
    ug, fg, mg, og, mgt = (ref[k] for k in ("ug", "fg", "mg", "og", "mgt"))
    small = ref["small"]

    def tile(n):
        return pl.ds(pl.multiple_of(n * W, W), W)

    def turn_o(n, carried):
        otok[:, tile(n)] = oa[tile(n), :].T
        return carried

    lax.fori_loop(0, NW, turn_o, 0)
    w3_whole(0)

    def out_step(n, carried):
        added = dot(otok[...], w3[0, :, tile(n)]) + gains[2:3, tile(n)]
        mid[:, tile(n)] = tok[:, tile(n)].astype(F32) + added
        return carried

    lax.fori_loop(0, NW, out_step, 0)

    def strip(i):
        return pl.ds(pl.multiple_of(i * STEP, STEP), STEP)

    def ff_norm(i, carried):
        x = mid[strip(i), :]
        ffin[strip(i), :] = (x * unit(x) * gain_ff).astype(BF16)
        return carried

    lax.fori_loop(0, L // STEP, ff_norm, 0)
    w3_whole(1)

    def up_step(n, carried):
        pre = dot(ffin[...], w3[1, :, tile(n)]) + gains[3:4, tile(n)]
        up[:, tile(n)] = pre
        hid[:, tile(n)] = (pre * jax.nn.sigmoid(pre)).astype(BF16)
        return carried

    lax.fori_loop(0, NW, up_step, 0)
    w3_whole(2)

    def down_step(n, carried):
        added = dot(hid[...], w3[2, :, tile(n)]) + gains[4:5, tile(n)]
        outb[:, tile(n)] = (mid[:, tile(n)] + added).astype(BF16)
        return carried

    lax.fori_loop(0, NW, down_step, 0)
    back_out = links.copy(outb, ref["out"], home, moves, moves)
    back_out.start()

    def keep_out():
        ref["out"][...] = outb[...]

    pl.when(stays)(keep_out)
    swaps[2].arrived()
    small[...] = jnp.zeros_like(small)

    def up_back(n, carried):
        pre = up[:, tile(n)]
        gate = jax.nn.sigmoid(pre)
        grad = dot_nt(cot[...], w3[2, tile(n), :]) * gate * (1.0 + pre * (1.0 - gate))
        grad = grad.astype(BF16)
        ug[:, tile(n)] = grad
        small[3:4, tile(n)] = jnp.sum(grad.astype(F32), axis=0, keepdims=True)
        return carried

    lax.fori_loop(0, NW, up_back, 0)

    def ff_back(n, carried):
        fg[:, tile(n)] = dot_nt(ug[...], w3[1, tile(n), :])
        return carried

    lax.fori_loop(0, NW, ff_back, 0)

    def mid_back(i, carried):
        x, grad, above_grad = mid[strip(i), :], fg[strip(i), :], cot[strip(i), :].astype(F32)
        inverse = unit(x)
        normed = x * inverse
        small[1:2, :] += jnp.sum(grad * normed, axis=0, keepdims=True)
        scaled = grad * gain_ff
        mean = jnp.mean(scaled * normed, axis=-1, keepdims=True)
        total = above_grad + inverse * (scaled - normed * mean)
        mg[strip(i), :] = total
        rounded = total.astype(BF16)
        og[strip(i), :] = rounded
        small[2:3, :] += jnp.sum(rounded.astype(F32), axis=0, keepdims=True)
        small[4:5, :] += jnp.sum(above_grad, axis=0, keepdims=True)
        return carried

    lax.fori_loop(0, L // STEP, mid_back, 0)

    dot_t = ref["dot_t"]
    first_m = links.block(S)

    def m_copy(k):
        g2 = (g + k) % S
        at = pl.ds(pl.multiple_of(g2 * E, 16), E)
        return links.copy(
            mgt.at[at], dot_t.at[:, rows_of(blk)], device(g2 // q, a, g2 % q),
            index=first_m + k, keep=False,
        )

    def mixed_step(k, carried):
        at = pl.ds(pl.multiple_of(((g + k) % S) * E, 16), E)
        mgt[at, :] = dot_nt(w3[0, at, :], og[...]).astype(BF16)
        pl.when(k < S)(lambda: m_copy(k).start())
        return carried

    lax.fori_loop(1, S + 1, mixed_step, 0)
    dot_t[:, rows_of(blk)] = mgt[pl.ds(pl.multiple_of(g * E, 16), E), :]

    freed, freed_again = ref["freed"], ref["freed_again"]
    writers = [sibling] + [peer(u, c, v) for v in b_off[1:]] + [peer(v, c, b) for v in u_off[1:]]

    def release(sem):
        for where in writers:
            pl.semaphore_signal(sem, inc=1, device_id=where, device_id_type=MESH)

    for group in (up_w, down_w, side_w, own_w, core_w, core_own):
        for moved in group.values():
            moved.sent()
            links.copies.remove(moved)
    release(freed)

    gp, rc = ref["gp"], ref["rc"]
    rcin = [w3.at[0, :, 0:DH], w3.at[0, :, DH:D], w3.at[1, :, 0:DH]]
    core_g = [links.copy(gp.at[w], rcin[w], sibling) for w in range(3)]

    def weight_grad(w, left, right):
        if left is not None:

            def turn(n, carried):
                oa[tile(n), :] = left[:, tile(n)].T
                return carried

            lax.fori_loop(0, NW, turn, 0)

        def step(n, carried):
            here = pl.ds(pl.multiple_of(n * SR, 16), SR)
            side = oa[here, :]
            gp[w, here, :] = dot(side, right[:, other_half]).astype(BF16)
            rc[w, n // q, n % q] = dot(side, right[:, own_half]).astype(BF16)
            return carried

        lax.fori_loop(0, S, step, 0)

    weight_grad(0, None, og)
    pl.semaphore_wait(freed, len(writers))
    core_g[0].start()
    weight_grad(2, hid, cot)
    core_g[2].start()
    weight_grad(1, ffin, ug)
    core_g[1].start()

    def m_arrived(k, carried):
        m_copy(k).arrived()
        return carried

    lax.fori_loop(1, S, m_arrived, 0)

    A2 = A // 2
    u_rows = [pl.ds(pl.multiple_of(v * SRH, 16), SRH) for v in u_off]
    my_rows = u_rows[0]
    qm, um = q - 1, U - 1

    def t1b(w, db, a2):
        at = ((w * qm + db - 1) * A2 + a2) * SR
        assert at + SR <= D
        return w3.at[1, at : at + SR, DH:D]

    def t1u(w, du, a2, b2):
        at = (((w * um + du - 1) * A2 + a2) * q + b2) * SRH
        assert at + SRH <= D
        return w3.at[2, at : at + SRH, 0:DH]

    def t2b(w, db, a2):
        at = ((w * qm + db - 1) * A2 + a2) * SRH
        return w3.at[2, at : at + SRH, DH:D]

    def t2u(w, du, a2):
        at = (3 * qm * A2 + (w * um + du - 1) * A2 + a2) * SRH
        assert at + SRH <= D
        return w3.at[2, at : at + SRH, DH:D]

    first_b, first_u, second_b, second_u = {}, {}, {}, {}
    for w in range(3):
        for a2 in range(A2):
            for db in range(1, q):
                to = peer(u, c, b_off[db])
                first_b[w, db, a2] = links.copy(rc.at[w, a2, b_off[db]], t1b(w, db, a2), to)
                second_b[w, db, a2] = links.copy(
                    rc.at[w, A2 + a2, b_off[db], my_rows], t2b(w, db, a2), to
                )
            if H > 1:
                for du in range(1, U):
                    to = peer(u_off[du], c, b)
                    for b2 in range(q):
                        first_u[w, du, a2, b2] = links.copy(
                            rc.at[w, A2 + a2, b2, u_rows[du]], t1u(w, du, a2, b2), to
                        )
                    second_u[w, du, a2] = links.copy(
                        rc.at[w, a2, b, u_rows[du]], t2u(w, du, a2), to
                    )

    def add_into(target, *more):
        total = target[...].astype(F32)
        for other in more:
            total = total + other[...].astype(F32)
        target[...] = total.astype(BF16)

    def core_sum(w):
        core_g[w].arrived()

        def step(n, carried):
            a2, b2 = n // q, n % q
            here = pl.ds(pl.multiple_of(n * SR, 16), SR)
            add_into(rc.at[w, a2, b2], rcin[w].at[here])
            return carried

        lax.fori_loop(0, S, step, 0)
        for key, moved in list(first_b.items()) + list(first_u.items()):
            if key[0] == w:
                moved.start()

    def side_sum_1(w):
        for db in range(1, q):
            for a2 in range(A2):
                first_b[w, db, a2].arrived()
                add_into(rc.at[w, a2, b], t1b(w, db, a2))
        if H > 1:
            for du in range(1, U):
                for a2 in range(A2):
                    for b2 in range(q):
                        first_u[w, du, a2, b2].arrived()
                        add_into(rc.at[w, A2 + a2, b2, my_rows], t1u(w, du, a2, b2))
        for key, moved in list(second_b.items()) + list(second_u.items()):
            if key[0] == w:
                moved.start()

    def side_sum_2(w):
        for db in range(1, q):
            for a2 in range(A2):
                second_b[w, db, a2].arrived()
                add_into(rc.at[w, A2 + a2, b, my_rows], t2b(w, db, a2))
        if H > 1:
            for du in range(1, U):
                for a2 in range(A2):
                    second_u[w, du, a2].arrived()
                    add_into(rc.at[w, a2, b, my_rows], t2u(w, du, a2))

    cu = ref["cu"]
    up_g, down_g = {}, {}
    for d in range(A):
        at = rc.at[:, d, b, my_rows]
        if d > 0:
            slot = jnp.where(a + 1 == d, A, d)
            up_g[d] = links.copy(at, cu.at[slot], above, a < d, jnp.logical_and(a > 0, a <= d))
        if d < A - 1:
            down_g[d] = links.copy(
                at, cu.at[d], below, a > d, jnp.logical_and(a < A - 1, a >= d)
            )

    def line_sum(d):
        def from_below():
            up_g[d].make().wait_recv()
            slot = jnp.where(a == d, A, d)
            other = near(cu.at[slot], "c_rows", 7)
            for w in range(3):
                add_into(rc.at[w, d, b, my_rows], other.at[w])

        def from_above():
            down_g[d].make().wait_recv()
            other = near(cu.at[d], "c_rows", 7)
            for w in range(3):
                add_into(rc.at[w, d, b, my_rows], other.at[w])

        if d > 0:
            pl.when(jnp.logical_and(a > 0, a <= d))(from_below)
            up_g[d].start()
        if d < A - 1:
            pl.when(jnp.logical_and(a < A - 1, a >= d))(from_above)
            down_g[d].start()

    line_order = sorted(range(A), key=lambda d: -abs(2 * d - (A - 1)))

    delta, dqt, dqkvt = ref["delta"], ref["dqt"], ref["dqkvt"]
    for hd in range(HG):
        head = slice(hd * HD, (hd + 1) * HD)
        total = jnp.sum(dot_t[head, :].astype(F32) * ot[head, :], axis=0, keepdims=True)
        delta[hd, :, :] = jnp.broadcast_to(total, (8, T))
    dqt[...] = jnp.zeros_like(dqt)
    back_services = {}
    for w, at in ((2, 0), (1, 1), (0, 1)):
        back_services.setdefault(at, []).append(functools.partial(core_sum, w))
    for w, at in ((2, 2), (1, 3), (0, 4)):
        back_services.setdefault(min(at, S - 1), []).append(functools.partial(side_sum_1, w))
    for w, at in ((2, 4), (1, 5), (0, 6)):
        back_services.setdefault(min(at, S - 1), []).append(functools.partial(side_sum_2, w))

    def attend_back(j, carried):
        here = rows_of(j)

        def query_block(i, state, on_diagonal):
            cols = rows_of(i)
            result = []
            for hd in range(HG):
                dk, dv = state[hd]
                head = pl.ds(hd * HD, HD)
                score = dot(keys[hd, here, :], qt[hd, :, cols])
                if on_diagonal:
                    score = jnp.where(diagonal, score, masked_score)
                p = jnp.exp(score - lse[hd, 0:1, cols])
                d_out = dot_t[head, cols]
                dp = dot(vals[hd, here, 0:HD], d_out)
                ds = (p * (dp - delta[hd, 0:1, cols])).astype(BF16)
                dv = dv + dot_nt(d_out, p.astype(BF16))
                dk = dk + dot_nt(qt[hd, 0:HD, cols], ds)
                dqt[head, cols] += dot(kt[hd, :, here], ds)
                result.append((dk, dv))
            return tuple(result)

        zero = jnp.zeros((HD, L), F32)
        state = query_block(j, tuple((zero, zero) for _ in range(HG)), True)
        state = lax.fori_loop(j + 1, S, functools.partial(query_block, on_diagonal=False), state)
        for hd in range(HG):
            dk, dv = state[hd]
            dqkvt[pl.ds(E + hd * HD, HD), here] = dk.astype(BF16)
            dqkvt[pl.ds(2 * E + hd * HD, HD), here] = dv.astype(BF16)
        for n in sorted(back_services):

            def run(n=n):
                for job in back_services[n]:
                    job()

            pl.when(j == n)(run)
        return carried

    lax.fori_loop(0, S, attend_back, 0)
    if CW > 3 * E:
        dqkvt[3 * E :, :] = jnp.zeros((CW - 3 * E, T), BF16)

    def query_part(i, carried):
        cols = rows_of(i)
        dqkvt[0:E, cols] = (dqt[:, cols] * qgain_col[0:E]).astype(BF16)
        return carried + jnp.sum(dqt[:, cols] * qpre[:, cols], axis=1, keepdims=True)

    scale_terms = lax.fori_loop(0, S, query_part, jnp.zeros((E, 1), F32))

    ags, arc = ref["ags"], ref["arc"]

    def slot_of(n, rows):
        page, row = divmod(n * HALF, D)
        return w3.at[page, row : row + rows]

    order = [(u2, b2) for u2 in range(U) for b2 in range(q)]
    slots_used = 2 * U * q
    core_a = {}
    for n, (u2, b2) in enumerate(order):
        core_a[u2, b2] = links.copy(ags.at[u2, b2], slot_of(2 * n, L), sibling)
    dtok = ref["dtok"]
    release(freed_again)
    pl.semaphore_wait(freed_again, len(writers))

    def partial_rows(m, carried, others):
        block = block_of(m // q, 1 - c if others else c, m % q)
        dtok[...] = dqkvt[:, rows_of(block)].T
        for k in range(NW):
            at = slice(k * W, (k + 1) * W)
            part = dot_nt(dtok[...], wq[at, :]).astype(BF16)
            if others:
                ags[m // q, m % q, :, at] = part
            else:
                arc[m // q, m % q, :, at] = part
        if others:
            for j, key in enumerate(order):
                pl.when(m == j)(core_a[key].start)
        return carried

    lax.fori_loop(0, U * q, functools.partial(partial_rows, others=True), 0)
    lax.fori_loop(0, U * q, functools.partial(partial_rows, others=False), 0)

    HA, HB = pl.ds(0, HALF), pl.ds(HALF, HALF)
    afb, afu, asb, asu, landing = {}, {}, {}, {}, {}

    def land(key):
        nonlocal slots_used
        landing[key] = slot_of(slots_used, HALF)
        slots_used += 1
        assert slots_used * HALF <= 3 * D
        return landing[key]

    for db in range(1, q):
        to = peer(u, c, b_off[db])
        for u2 in range(U):
            afb[db, u2] = links.copy(arc.at[u2, b_off[db], HA], land(("fb", db, u2)), to)
        asb[db] = links.copy(arc.at[u, b_off[db], HB], land(("sb", db)), to)
    for du in range(1, U):
        to = peer(u_off[du], c, b)
        for b2 in range(q):
            afu[du, b2] = links.copy(arc.at[u_off[du], b2, HB], land(("fu", du, b2)), to)
        asu[du] = links.copy(arc.at[u_off[du], b, HA], land(("su", du)), to)

    def add_rows(target, other, count):
        def step(i, carried):
            add_into(target.at[strip(i)], other.at[strip(i)])
            return carried

        lax.fori_loop(0, count // STEP, step, 0)

    for u2, b2 in order:
        core_a[u2, b2].arrived()

        add_rows(arc.at[u2, b2], slot_of(2 * order.index((u2, b2)), L), L)
    for moved in list(afb.values()) + list(afu.values()):
        moved.start()

    gq, cqu, gall = ref["gq"], ref["cqu"], ref["gall"]

    def qkv_grad(n, carried):
        gq[tile(n), :] = dot(dqkvt[...], near(xa.at[:, tile(n)], "x_cols", 7)[...]).T.astype(BF16)
        return carried

    lax.fori_loop(0, NW, qkv_grad, 0)
    QR = q * SR
    up_gq, down_gq = {}, {}
    for d in range(A):
        at = gq.at[pl.ds(d * QR, QR)]
        if d > 0:
            slot = jnp.where(a + 1 == d, A, d)
            up_gq[d] = links.copy(at, cqu.at[slot], above, a < d, jnp.logical_and(a > 0, a <= d))
        if d < A - 1:
            down_gq[d] = links.copy(
                at, cqu.at[d], below, a > d, jnp.logical_and(a < A - 1, a >= d)
            )

    def line_sum_q(d):
        at = gq.at[pl.ds(d * QR, QR)]

        def from_below():
            up_gq[d].make().wait_recv()
            add_into(at, cqu.at[jnp.where(a == d, A, d)])

        def from_above():
            down_gq[d].make().wait_recv()
            add_into(at, cqu.at[d])

        if d > 0:
            pl.when(jnp.logical_and(a > 0, a <= d))(from_below)
            up_gq[d].start()
        if d < A - 1:
            pl.when(jnp.logical_and(a < A - 1, a >= d))(from_above)
            down_gq[d].start()

    for d in line_order:
        line_sum_q(d)

    for db in range(1, q):
        for u2 in range(U):
            afb[db, u2].arrived()
            add_rows(arc.at[u2, b, HA], landing["fb", db, u2], HALF)
    for du in range(1, U):
        for b2 in range(q):
            afu[du, b2].arrived()
            add_rows(arc.at[u, b2, HB], landing["fu", du, b2], HALF)
    for moved in list(asb.values()) + list(asu.values()):
        moved.start()

    for d in line_order:
        line_sum(d)

    ones = jnp.ones((8, T), BF16)
    head_sums = dot_nt(ones, dqkvt[...])
    small[pl.ds(8 + g, 1), 0:CW] = head_sums[0:1]
    small[5:6, 0:E] = jnp.transpose(jnp.broadcast_to(scale_terms, (E, 128)))[0:1, :]

    for db in range(1, q):
        asb[db].arrived()
        add_rows(arc.at[u, b, HB], landing["sb", db], HALF)
    for du in range(1, U):
        asu[du].arrived()
        add_rows(arc.at[u, b, HA], landing["su", du], HALF)

    def tok_back(i, carried):
        x, grad = tok[strip(i), :].astype(F32), arc[u, b, strip(i)].astype(F32)
        inverse = unit(x)
        normed = x * inverse
        small[0:1, :] += jnp.sum(grad * normed, axis=0, keepdims=True)
        scaled = grad * gain_attn
        mean = jnp.mean(scaled * normed, axis=-1, keepdims=True)
        ref["gtb"][strip(i), :] = (mg[strip(i), :] + inverse * (scaled - normed * mean)).astype(BF16)
        return carried

    lax.fori_loop(0, L // STEP, tok_back, 0)
    back_tok = links.copy(ref["gtb"], ref["gtok"], home, moves, moves)
    back_tok.start()

    def keep_tok():
        ref["gtok"][...] = ref["gtb"][...]

    pl.when(stays)(keep_tok)

    stages = [
        [sibling],
        [peer(u, c, b_off[db]) for db in range(1, q)],
        [peer(u_off[du], c, b) for du in range(1, U)],
        [device(r, (a + k) % A, b) for k in range(1, A)],
    ]
    stages = [stage for stage in stages if stage]
    sums, landed = ref["sums"], ref["landed"]
    count, moved_small = 0, []
    for n, stage in enumerate(stages):
        moved_small.append(
            [links.copy(sums.at[n], landed.at[count + k], to) for k, to in enumerate(stage)]
        )
        count += len(stage)

    def small_stage(n):
        for moved in moved_small[n]:
            moved.arrived()
        total = sums[n]
        first = sum(len(stage) for stage in stages[:n])
        for k in range(len(stages[n])):
            total = total + landed[first + k]
        return total

    sums[0] = small[...]
    for moved in moved_small[0]:
        moved.start()

    wide = {}
    for db in range(1, q):
        at = gq.at[pl.ds(pl.multiple_of(a * QR + b_off[db] * SR, 16), SR)]
        wide[db] = links.copy(at, gall.at[g], device(r, a, b_off[db]))
        wide[db].start()
    gall[g] = gq[pl.ds(pl.multiple_of(a * QR + b * SR, 16), SR), :]
    go = ref["go"]
    piece = rc.at[:, a, b, my_rows]
    spread = []
    if H > 1:
        at = go.at[:, my_rows, own_half]
        for du in range(U):
            for dc in range(2):
                if du or dc:
                    spread.append(links.copy(piece, at, peer(u_off[du], (c + dc) % 2, b)))
    else:
        partials = [
            links.copy(piece, ref["ru"].at[du - 1], peer(u_off[du], c, b)) for du in range(1, U)
        ]
        for moved in partials:
            moved.start()
        for moved in partials:
            moved.arrived()
        for moved in partials:
            moved.sent()
            links.copies.remove(moved)
        for k in range(U - 1):
            other = near(ref["ru"].at[k], "c_rows", 7)
            for w in range(3):
                add_into(rc.at[w, a, b, my_rows], other.at[w])
        spread.append(links.copy(piece, go.at[:, :, own_half], sibling))
    for moved in spread:
        moved.start()
    go[:, my_rows, own_half] = piece[...]

    if len(stages) > 1:
        sums[1] = small_stage(0)
        for moved in moved_small[1]:
            moved.start()
    q_across, q_core = [], []
    for db in range(1, q):
        wide[db].arrived()
    here = pl.ds(r * q, q)
    for du in range(1, U):
        q_across.append(links.copy(gall.at[here], gall.at[here], peer(u_off[du], c, b)))
        q_across[-1].start()
    for du in range(U):
        here = pl.ds((u_from[du] * 2 + c) * q, q)
        q_core.append(links.copy(gall.at[here], gall.at[here], sibling))
    q_core[0].start()
    for n in range(1, len(stages) - 1):
        sums[n + 1] = small_stage(n)
        for moved in moved_small[n + 1]:
            moved.start()
    for moved in spread:
        moved.arrived()
    for du in range(1, U):
        q_across[du - 1].arrived()
        q_core[du].start()
    ref["g_small"][...] = small_stage(len(stages) - 1)
    for moved in q_core:
        moved.arrived()
    for g2 in range(S):
        mine = gall[g2]
        for n, name in enumerate(("g_query", "g_key", "g_value")):
            ref[name][:, g2 * E : (g2 + 1) * E] = mine[:, n * E : (n + 1) * E].astype(F32)
    back_out.arrived()
    back_tok.arrived()

    lax.fori_loop(0, S, o_sent, 0)

    def m_sent(k, carried):
        m_copy(k).sent()
        return carried

    lax.fori_loop(1, S, m_sent, 0)
    for moved in links.copies:
        moved.sent()


def shards(
    R,
    S,
    tokens,
    lengths,
    parents,
    w_query,
    w_key,
    w_value,
    w_out,
    w_up,
    w_down,
    gain_attn,
    gain_ff,
    query_scale,
    bias_query,
    bias_value,
    bias_out,
    bias_up,
    bias_down,
    cotangent,
):
    L, D = tokens.shape
    SR = w_query.shape[0]
    HG = HEADS // S
    E = HG * HEAD_DIM
    CW = -(-3 * E // 128) * 128
    q, U, A, T = S // R, R // 2, R, S * L
    H = U if SR % (16 * U) == 0 else 1
    SRH = SR // H
    DH = D // 2
    NS = 8 + S
    segments = lengths.shape[1]
    dims = dict(R=R, S=S, L=L, D=D, HG=HG, E=E, CW=CW, SR=SR, H=H, SRH=SRH, segments=segments)

    tab = jnp.pad(
        jnp.concatenate([lengths, parents], axis=0).astype(F32), ((0, 6), (0, 128 - segments))
    )
    by_group = [w.reshape(SR, S, E) for w in (w_query, w_key, w_value)]
    wcat = jnp.pad(jnp.concatenate(by_group, axis=2), ((0, 0), (0, 0), (0, CW - 3 * E)))
    wcat = wcat.transpose(1, 0, 2)
    bias_rows = [bias_query.reshape(S, E), jnp.zeros((S, E), F32), bias_value.reshape(S, E)]
    biascat = jnp.pad(jnp.concatenate(bias_rows, axis=1), ((0, 0), (0, CW - 3 * E)))
    biascat = jnp.broadcast_to(biascat[:, None, :], (S, 8, CW))
    query_gain = query_base * jax.nn.softplus(query_scale) / math.sqrt(HEAD_DIM)
    qgain = jnp.pad(jnp.tile(query_gain, HG), (0, CW - E), constant_values=1.0)
    qgain = jnp.broadcast_to(qgain[None, :], (8, CW))
    zero_row = jnp.zeros_like(gain_attn)
    gains = jnp.stack(
        [gain_attn, gain_ff, bias_out, bias_up, bias_down, zero_row, zero_row, zero_row]
    )

    operands = dict(
        tokens=tokens, cotangent=cotangent, tab=tab, wcat=wcat, w_out=w_out, w_up=w_up,
        w_down=w_down, biascat=biascat, qgain=qgain, gains=gains,
    )
    outputs = dict(
        out=((L, D), BF16), gtok=((L, D), BF16), g_query=((SR, D), F32), g_key=((SR, D), F32),
        g_value=((SR, D), F32), go=((3, SR, D), BF16),
        g_small=((NS, D), F32),
    )
    um = max(U - 1, 1)
    peers = 1 + (q - 1) + (U - 1) + (A - 1)
    scratch = dict(
        tok=((L, D), BF16), cot=((L, D), BF16), tabs=((8, 128), F32),
        wq=((D, CW), BF16), w3=((3, D, D), BF16), xa=((T, D), BF16),
        qkvf=((CW, L), F32), qpre=((E, T), F32), qt=((HG, 128, T), BF16),
        keys=((HG, T, 128), BF16), kt=((HG, HEAD_DIM, T), BF16),
        vals=((HG, T, 128), BF16), vt=((HG, HEAD_DIM, T), BF16),
        ot=((E, T), F32), otb=((E, T), BF16), lse=((HG, 8, T), F32), oa=((D, L), BF16),
        otok=((L, D), BF16), mid=((L, D), F32), ffin=((L, D), BF16), up=((L, D), F32),
        hid=((L, D), BF16), outb=((L, D), BF16),
        mg=((L, D), F32), og=((L, D), BF16), mgt=((D, L), BF16), dot_t=((E, T), BF16),
        small=((NS, D), F32), gp=((3, D, DH), BF16),
        rc=((3, A, q, SR, DH), BF16),
        cu=((A + 1, 3, SRH, DH), BF16), delta=((HG, 8, T), F32), dqkvt=((CW, T), BF16),
        ags=((U, q, L, D), BF16), arc=((U, q, L, D), BF16),
        dtok=((L, CW), BF16),
        gq=((D, CW), BF16), cqu=((A + 1, q * SR, CW), BF16),
        gall=((S, SR, CW), BF16),
        sums=((5, NS, D), F32), landed=((peers, NS, D), F32),
    )
    if H == 1:
        scratch["ru"] = ((um, 3, SR, DH), BF16)
    held = [jax.ShapeDtypeStruct(*v) for v in (outputs | scratch).values()]
    dims["fits"] = sum(v.size * v.dtype.itemsize for v in held) <= VMEM_BYTES - (2 << 20)
    results = len(outputs)
    distant = () if dims["fits"] else ("xa", "cu", "ru")
    for name in distant:
        outputs[name] = scratch.pop(name)
    if distant:
        scratch["x_rows"] = ((L, D), BF16)
        scratch["x_cols"] = ((T, 256), BF16)
        scratch["c_rows"] = ((3, SRH, DH), BF16)
    names = list(operands) + list(outputs) + list(scratch)
    names += ["send_sems", "recv_sems", "local_sems", "freed", "freed_again"]

    def kernel(*refs):
        named = dict(zip(names, refs))
        for later, earlier in (("fg", "up"), ("dqt", "ot"), ("ug", "otok"), ("gtb", "ffin")):
            named[later] = named[earlier]
        named["wqt"] = named["dqkvt"].at[:, 0:D]
        layer_kernel(dims, named)

    whole = pl.BlockSpec(memory_space=pltpu.VMEM)
    far = ("tokens", "cotangent", "wcat", "w_out", "w_up", "w_down")
    made = pl.pallas_call(
        kernel,
        out_shape=[jax.ShapeDtypeStruct(*shape) for shape in outputs.values()],
        in_specs=[pl.BlockSpec(memory_space=pl.ANY) if k in far else whole for k in operands],
        out_specs=[pl.BlockSpec(memory_space=pl.ANY) if k in distant else whole for k in outputs],
        scratch_shapes=[pltpu.VMEM(*shape) for shape in scratch.values()]
        + [pltpu.SemaphoreType.DMA((COPIES,))] * 2
        + [pltpu.SemaphoreType.DMA((8,))]
        + [pltpu.SemaphoreType.REGULAR] * 2,
        compiler_params=pltpu.CompilerParams(
            collective_id=0, has_side_effects=True, vmem_limit_bytes=VMEM_BYTES
        ),
    )(*operands.values())
    out, gtok, g_query, g_key, g_value, go, g_small = made[:results]
    g_out, g_up, g_down = (go[w].astype(F32) for w in range(3))
    scale = jnp.sum(g_small[5, :E].reshape(HG, HEAD_DIM), axis=0)
    scale = scale * query_base * jax.nn.sigmoid(query_scale) / math.sqrt(HEAD_DIM)
    by_head = g_small[8:, : 3 * E]
    return (
        out,
        gtok,
        g_query,
        g_key,
        g_value,
        g_out,
        g_up,
        g_down,
        g_small[0],
        g_small[1],
        scale,
        by_head[:, :E].reshape(D),
        by_head[:, 2 * E :].reshape(D),
        g_small[2],
        g_small[3],
        g_small[4],
    )


def solution(mesh):
    rows, line, copied = P(("rep", "shard"), None), P("shard", None), P()
    in_specs = (rows, P("rep", None), P("rep", None)) + (line,) * 6 + (copied,) * 8 + (rows,)
    out_specs = (rows, rows) + (line,) * 6 + (copied,) * 8
    body = functools.partial(shards, mesh.shape["rep"], mesh.shape["shard"])
    return jax.shard_map(
        body, mesh=mesh, in_specs=in_specs, out_specs=out_specs, check_vma=False
    )
```

```python
import functools
import math

import jax
import jax.numpy as jnp
from jax import lax
from jax.experimental import pallas as pl
from jax.experimental.pallas import tpu as pltpu
from jax.sharding import PartitionSpec as P

HEADS = 16
HEAD_DIM = 80
MESH = pl.DeviceIdType.MESH
F32 = jnp.float32
BF16 = jnp.bfloat16

norm_eps = 1e-06
query_base = 1.442695
masked_score = -1e30
LABELS = 16
VMEM_BYTES = 64 << 20


def dot(left, right):
    return jnp.dot(left, right, preferred_element_type=F32)


def dot_nt(left, right):
    return lax.dot_general(left, right, (((1,), (1,)), ((), ())), preferred_element_type=F32)


def when(condition, body):
    if condition is True:
        body()
    elif condition is not False:
        pl.when(condition)(body)


class Copy:
    def __init__(self, make, sends, receives):
        self.make, self.sends, self.receives = make, sends, receives

    def start(self):
        when(self.sends, lambda: self.make().start())

    def arrived(self):
        when(self.receives, lambda: self.make().wait_recv())

    def sent(self):
        when(self.sends, lambda: self.make().wait_send())


class Links:
    def __init__(self, send_sems, recv_sems):
        self.send_sems, self.recv_sems, self.used, self.copies = send_sems, recv_sems, 0, []

    def block(self, count):
        first = self.used
        self.used += count
        return first

    def copy(self, src, dst, device, sends=True, receives=True, index=None, keep=True):
        if index is None:
            index = self.block(1)

        def make():
            return pltpu.make_async_remote_copy(
                src_ref=src,
                dst_ref=dst,
                send_sem=self.send_sems.at[index],
                recv_sem=self.recv_sems.at[index],
                device_id=device,
                device_id_type=MESH,
            )

        made = Copy(make, sends, receives)
        if keep:
            self.copies.append(made)
        return made


def layer_kernel(dims, refs):
    R, S, L, D = dims["R"], dims["S"], dims["L"], dims["D"]
    HG, E, CW, SR, H, SRH = (dims[k] for k in ("HG", "E", "CW", "SR", "H", "SRH"))
    q, U, A, T = S // R, R // 2, R, S * L
    HD = HEAD_DIM
    HALF, DH = L // 2, D // 2
    W = 256
    NW = D // W
    ref = refs
    r, s = lax.axis_index("rep"), lax.axis_index("shard")
    u, c, a, b = r // 2, r % 2, s // q, s % q

    def rho(i):
        return (i % 2) * (R // 2) + i // 2

    def rho_back(j):
        return (j % (R // 2)) * 2 + j // (R // 2)

    def device(r2, a2, b2):
        return (r2, a2 * q + b2)

    def peer(u2, c2, b2):
        return device(u2 * 2 + c2, a, b2)

    def block_of(u2, c2, b2):
        return rho(u2 * 2 + c2) * q + b2

    def rows_of(blk):
        return pl.ds(pl.multiple_of(blk * L, L), L)

    g = r * q + b
    blk = block_of(u, c, b)
    u_off = [(u + d) % U for d in range(U)]
    b_off = [(b + d) % q for d in range(q)]
    u_from = [(u + U - d) % U for d in range(U)]
    b_from = [(b + q - d) % q for d in range(q)]
    home_r, home_a = rho_back(a), rho(r)
    home = device(home_r, home_a, b)
    stays = jnp.logical_and(home_r == r, home_a == a)
    moves = jnp.logical_not(stays)
    sibling = peer(u, 1 - c, b)
    above = device(r, jnp.minimum(a + 1, A - 1), b)
    below = device(r, jnp.maximum(a - 1, 0), b)
    own_half = pl.ds(pl.multiple_of(c * DH, 128), DH)
    other_half = pl.ds(pl.multiple_of((1 - c) * DH, 128), DH)

    links = Links(ref["send_sems"], ref["recv_sems"])

    barrier = pltpu.get_barrier_semaphore()

    def greet(where):
        pl.semaphore_signal(barrier, inc=1, device_id=where, device_id_type=MESH)

    for k in range(1, S):
        g2 = (g + k) % S
        greet(device(g2 // q, a, g2 % q))
    for k in range(1, A):
        greet(device(r, (a + k) % A, b))
    pl.when(moves)(lambda: greet(home))
    pl.semaphore_wait(barrier, S - 1 + A - 1 + jnp.where(moves, 1, 0))

    swaps = []
    for name, there in (("tokens", "tok"), ("tab", "tabs"), ("cotangent", "cot")):
        swaps.append(links.copy(ref[name], ref[there], home, moves, moves))

    local_sems = ref["local_sems"]

    def local(src, dst, n):
        return pltpu.make_async_copy(src, dst, local_sems.at[n])

    def keep_rows():
        kept = [
            local(ref["tokens"], ref["tok"], 0),
            local(ref["tab"], ref["tabs"], 1),
            local(ref["cotangent"], ref["cot"], 2),
        ]
        for copy in kept:
            copy.start()
        for copy in kept:
            copy.wait()

    swaps[0].start()
    swaps[1].start()

    wq, wqt, wcat = ref["wq"], ref["wqt"], ref["wcat"]

    def wq_rows(a2, b2):
        return pl.ds(pl.multiple_of((a2 * q + b2) * SR, 16), SR)

    def near(src, name, n):
        if dims["fits"] or name == "q_rows":
            return src
        copy = local(src, ref[name], n)
        copy.start()
        copy.wait()
        return ref[name]

    own_wq = local(wcat.at[g], wq.at[wq_rows(a, b)], 3)
    own_wq.start()
    wcat_b = {}
    for db in range(1, q):
        wcat_b[db] = links.copy(
            wcat.at[r * q + b_off[db]], wq.at[wq_rows(a, b)], device(r, a, b_off[db])
        )
        wcat_b[db].start()
    up_q, down_q = {}, {}
    for k in range(A - 1):
        for db in range(q):
            low, high = jnp.maximum(a - k, 0), jnp.minimum(a + k, A - 1)
            slot = wq_rows(low, b_from[db])
            up_q[k, db] = links.copy(
                wq.at[slot], wq.at[slot], above,
                jnp.logical_and(a - k >= 0, a < A - 1), a - 1 - k >= 0,
            )
            slot = wq_rows(high, b_from[db])
            down_q[k, db] = links.copy(
                wq.at[slot], wq.at[slot], below,
                jnp.logical_and(a + k <= A - 1, a > 0), a + 1 + k <= A - 1,
            )
    own_wq.wait()
    up_q[0, 0].start()
    down_q[0, 0].start()

    def wq_pass(k):
        for db in range(q):
            up_q[k, db].arrived()
            down_q[k, db].arrived()
            if k + 1 < A - 1:
                up_q[k + 1, db].start()
                down_q[k + 1, db].start()

    w3 = ref["w3"]
    shards = (ref["w_out"], ref["w_up"], ref["w_down"])

    def shard_rows(a2, b2):
        return pl.ds(pl.multiple_of((a2 * q + b2) * SR, 16), SR)

    def piece_rows(a2, b2, u2):
        if H == 1:
            return shard_rows(a2, b2)
        return pl.ds(pl.multiple_of((a2 * q + b2) * SR + u2 * SRH, 16), SRH)

    own_shards = [local(shards[w], w3.at[w, shard_rows(a, b)], 4 + w) for w in range(3)]
    for copy in own_shards:
        copy.start()
    for copy in own_shards:
        copy.wait()
    pl.when(stays)(keep_rows)
    up_w, down_w, side_w, own_w, core_w, core_own = {}, {}, {}, {}, {}, {}
    slots = [sign * k for k in range(1, A) for sign in (1, -1)]
    for w in range(3):
        for k in range(A - 1):
            low, high = jnp.maximum(a - k, 0), jnp.minimum(a + k, A - 1)
            at = w3.at[w, piece_rows(low, b, u), own_half]
            up_w[w, k] = links.copy(
                at, at, above, jnp.logical_and(a - k >= 0, a < A - 1), a - 1 - k >= 0
            )
            at = w3.at[w, piece_rows(high, b, u), own_half]
            down_w[w, k] = links.copy(
                at, at, below, jnp.logical_and(a + k <= A - 1, a > 0), a + 1 + k <= A - 1
            )
        for slot in slots:
            valid = a + slot <= A - 1 if slot > 0 else a + slot >= 0
            a0 = jnp.clip(a + slot, 0, A - 1)
            at = w3.at[w, piece_rows(a0, b, u), own_half]
            for db in range(1, q):
                side_w[w, slot, 0, db] = links.copy(at, at, peer(u, c, b_off[db]), valid, valid)
            if H > 1:
                for du in range(1, U):
                    side_w[w, slot, du, 0] = links.copy(at, at, peer(u_off[du], c, b), valid, valid)
                    for db in range(1, q):
                        if (slot + w) % 2:
                            passed = w3.at[w, piece_rows(a0, b_from[db], u), own_half]
                            to = peer(u_off[du], c, b)
                        else:
                            passed = w3.at[w, piece_rows(a0, b, u_from[du]), own_half]
                            to = peer(u, c, b_off[db])
                        side_w[w, slot, du, db] = links.copy(passed, passed, to, valid, valid)
            at = w3.at[w, pl.ds(pl.multiple_of(a0 * q * SR, 16), q * SR), own_half]
            core_w[w, slot] = links.copy(at, at, sibling, valid, valid)
        for db in range(1, q):
            at = w3.at[w, shard_rows(a, b), own_half]
            own_w[w, db] = links.copy(at, at, peer(u, c, b_off[db]))
            at = w3.at[w, shard_rows(a, b_from[db]), own_half]
            core_own[w, db] = links.copy(at, at, sibling)

    for moved in own_w.values():
        moved.start()

    def w3_line(w, k):
        if k < 0:
            up_w[w, 0].start()
            down_w[w, 0].start()
            return
        up_w[w, k].arrived()
        down_w[w, k].arrived()
        if k + 1 < A - 1:
            up_w[w, k + 1].start()
            down_w[w, k + 1].start()
        for slot in (-(k + 1), k + 1):
            for (w2, slot2, du, db), moved in side_w.items():
                if (w2, slot2) == (w, slot) and (du == 0 or db == 0):
                    moved.start()

    def w3_side(w, k):
        if k < 0:
            for db in range(1, q):
                own_w[w, db].arrived()
                core_own[w, db].start()
            return
        for slot in (-(k + 1), k + 1):
            for db in range(1, q):
                side_w[w, slot, 0, db].arrived()
            if H > 1:
                for du in range(1, U):
                    side_w[w, slot, du, 0].arrived()
                    for db in range(1, q):
                        side_w[w, slot, du, db].start()

    def w3_core(w, k):
        for slot in (-(k + 1), k + 1):
            if H > 1:
                for du in range(1, U):
                    for db in range(1, q):
                        side_w[w, slot, du, db].arrived()
            core_w[w, slot].start()

    def w3_whole(w):
        for db in range(1, q):
            core_own[w, db].arrived()
        for slot in slots:
            core_w[w, slot].arrived()

    tok, cot, xa = ref["tok"], ref["cot"], ref["xa"]
    gains = ref["gains"]
    gain_attn, gain_ff = gains[0:1, :], gains[1:2, :]
    STEP = 32

    def unit(x):
        return lax.rsqrt(jnp.mean(x * x, axis=-1, keepdims=True) + norm_eps)

    def half_rows(block, h):
        return pl.ds(pl.multiple_of(block * L + h * HALF, HALF), HALF)

    own_x, pass_x, sib_x = {}, {}, {}
    for h in range(2):
        at = xa.at[half_rows(blk, h)]
        for db in range(1, q):
            own_x[h, 0, db] = links.copy(at, at, peer(u, c, b_off[db]))
        for du in range(1, U):
            own_x[h, du, 0] = links.copy(at, at, peer(u_off[du], c, b))
        for du in range(1, U):
            for db in range(1, q):
                if h == 0:
                    at = xa.at[half_rows(block_of(u, c, b_from[db]), h)]
                    pass_x[h, du, db] = links.copy(at, at, peer(u_off[du], c, b))
                else:
                    at = xa.at[half_rows(block_of(u_from[du], c, b), h)]
                    pass_x[h, du, db] = links.copy(at, at, peer(u, c, b_off[db]))
        for du in range(U):
            for db in range(q):
                at = xa.at[half_rows(block_of(u_from[du], c, b_from[db]), h)]
                sib_x[h, du, db] = links.copy(at, at, sibling)

    swaps[0].arrived()
    for h in range(2):

        def norm_step(i, carried, h=h):
            here = pl.ds(pl.multiple_of(h * HALF + i * STEP, STEP), STEP)
            x = tok[here, :].astype(F32)
            there = pl.ds(pl.multiple_of(blk * L + h * HALF + i * STEP, STEP), STEP)
            row = (x * unit(x) * gain_attn).astype(BF16)
            if dims["fits"]:
                xa[there, :] = row
            else:
                ref["x_rows"][here, :] = row
            return carried

        lax.fori_loop(0, HALF // STEP, norm_step, 0)
        if not dims["fits"]:
            here = pl.ds(h * HALF, HALF)
            out_of = local(ref["x_rows"].at[here], xa.at[half_rows(blk, h)], 7)
            out_of.start()
            out_of.wait()
        for moved in [m for (h2, *_), m in own_x.items() if h2 == h]:
            moved.start()
        sib_x[h, 0, 0].start()

    for db in range(1, q):
        wcat_b[db].arrived()
        up_q[0, db].start()
        down_q[0, db].start()

    swaps[1].arrived()
    lane = lax.broadcasted_iota(jnp.int32, (LABELS, 128), 1)
    row = lax.broadcasted_iota(jnp.int32, (LABELS, 128), 0)
    lengths = jnp.broadcast_to(ref["tabs"][0:1, :], (LABELS, 128))
    seg_start = jnp.sum(jnp.where(lane < row, lengths, 0.0), axis=1, keepdims=True)
    seg_end = jnp.sum(jnp.where(lane <= row, lengths, 0.0), axis=1, keepdims=True)
    lane = lax.broadcasted_iota(jnp.int32, (128, 128), 1)
    row = lax.broadcasted_iota(jnp.int32, (128, 128), 0)
    parents = jnp.broadcast_to(ref["tabs"][1:2, :], (128, 128))
    segments = dims["segments"]
    is_parent = (parents == row.astype(F32)) & (lane > 0) & (lane < segments)
    reach = jnp.where((lane == row) | is_parent, 1.0, 0.0)
    for _ in range(max(1, (segments - 1).bit_length())):
        reach = jnp.minimum(dot(reach.astype(BF16), reach.astype(BF16)), 1.0)
    blocked = ((1.0 - reach[:LABELS, :LABELS]) * masked_score).astype(BF16)

    for db in range(1, q):
        own_x[0, 0, db].arrived()
        for du in range(1, U):
            pass_x[0, du, db].start()
        sib_x[0, 0, db].start()
    for du in range(1, U):
        own_x[1, du, 0].arrived()
        for db in range(1, q):
            pass_x[1, du, db].start()
        sib_x[1, du, 0].start()
    wq_pass(0)
    for db in range(1, q):
        own_x[1, 0, db].arrived()
        sib_x[1, 0, db].start()
    for du in range(1, U):
        own_x[0, du, 0].arrived()
        sib_x[0, du, 0].start()
    for w in range(3):
        w3_side(w, -1)
    for k in range(1, A - 2):
        wq_pass(k)
    for w in range(3):
        w3_line(w, -1)
    for h in range(2):
        for du in range(1, U):
            for db in range(1, q):
                pass_x[h, du, db].arrived()
                sib_x[h, du, db].start()
    wq_pass(A - 2)

    def turn_wq(i, carried):
        here = pl.ds(pl.multiple_of(i * W, W), W)
        wqt[:, here] = wq[here, :].T
        return carried

    lax.fori_loop(0, NW, turn_wq, 0)
    bias_col = jnp.transpose(ref["biascat"][g])[:, 0:1]
    qgain_col = jnp.transpose(ref["qgain"][...])[:, 0:1]
    qkvf, qpre, qt, keys, kt, vals, vt = (
        ref[k] for k in ("qkvf", "qpre", "qt", "keys", "kt", "vals", "vt")
    )

    def project(k, carried):
        for j in range(S):

            def wait_rows(j=j):
                du, db, other = (j // 2) // q, (j // 2) % q, j % 2
                if other:
                    for h in range(2):
                        sib_x[h, du, db].arrived()

            pl.when(k == j)(wait_rows)
        du, db, other = (k // 2) // q, (k // 2) % q, k % 2
        block = block_of((u + U - du) % U, (c + other) % 2, (b + q - db) % q)
        cols = rows_of(block)
        x = near(xa.at[cols], "x_rows", 7)[...]
        qkvf[...] = dot_nt(wqt[...], x) + bias_col
        place = block * L + lax.broadcasted_iota(jnp.int32, (LABELS, L), 1)
        place = place.astype(F32)
        onehot = jnp.where((place >= seg_start) & (place < seg_end), 1.0, 0.0)
        far = dot(blocked, onehot.astype(BF16)).astype(BF16)
        for hd in range(HG):
            head = pl.ds(hd * HD, HD)
            pre = qkvf[head, :]
            qpre[head, cols] = pre
            qt[hd, 0:HD, cols] = (pre * qgain_col[hd * HD : (hd + 1) * HD]).astype(BF16)
            qt[hd, HD : HD + LABELS, cols] = far
            qt[hd, HD + LABELS : 128, cols] = jnp.zeros((128 - HD - LABELS, L), BF16)
            key = qkvf[pl.ds(E + hd * HD, HD), :]
            kt[hd, :, cols] = key.astype(BF16)
            wide = jnp.concatenate([key, onehot, jnp.zeros((128 - HD - LABELS, L), F32)], axis=0)
            keys[hd, cols, :] = wide.T.astype(BF16)
            value = qkvf[pl.ds(2 * E + hd * HD, HD), :]
            vt[hd, :, cols] = value.astype(BF16)
            wide = jnp.concatenate([value, jnp.zeros((128 - HD, L), F32)], axis=0)
            vals[hd, cols, :] = wide.T.astype(BF16)
        return carried

    lax.fori_loop(0, S, project, 0)

    ot, otb, lse, oa = ref["ot"], ref["otb"], ref["lse"], ref["oa"]
    first_o = links.block(S)
    o_slot = pl.ds(pl.multiple_of(g * E, 16), E)

    def o_copy(block):
        r2, b2 = rho_back(block // q), block % q
        index = first_o + (r2 * q + b2 + S - g) % S
        return links.copy(
            otb.at[:, rows_of(block)], oa.at[o_slot], device(r2, a, b2), index=index, keep=False
        )

    PAIR = 2
    SQ = PAIR * L
    diagonal = lax.broadcasted_iota(jnp.int32, (SQ, SQ), 0) <= lax.broadcasted_iota(
        jnp.int32, (SQ, SQ), 1
    )
    for w in range(3):
        w3_line(w, 0)

    def after_block(i):
        for w in range(3):
            if i == 1:
                w3_side(w, 0)
            elif i == 2 and A > 2:
                w3_line(w, 1)
            elif i == 3 and A > 2:
                w3_side(w, 1)
                w3_core(w, 0)

    def wide_rows(i):
        return pl.ds(pl.multiple_of(i * SQ, SQ), SQ)

    def attend(i, carried):
        cols = wide_rows(i)
        query = [qt[hd, :, cols] for hd in range(HG)]

        def key_block(j, state, on_diagonal):
            here = wide_rows(j)
            result = []
            for hd in range(HG):
                top, total, acc = state[hd]
                score = dot(keys[hd, here, :], query[hd])
                if on_diagonal:
                    score = jnp.where(diagonal, score, masked_score)
                new_top = jnp.maximum(top, jnp.max(score, axis=0, keepdims=True))
                p = jnp.exp(score - new_top)
                fade = jnp.exp(top - new_top)
                total = total * fade + jnp.sum(p, axis=0, keepdims=True)
                acc = acc * fade + dot(vt[hd, :, here], p.astype(BF16))
                result.append((new_top, total, acc))
            return tuple(result)

        start = tuple(
            (
                jnp.full((1, SQ), masked_score, F32),
                jnp.zeros((1, SQ), F32),
                jnp.zeros((HD, SQ), F32),
            )
            for _ in range(HG)
        )
        state = lax.fori_loop(0, i, functools.partial(key_block, on_diagonal=False), start)
        state = key_block(i, state, True)
        for hd in range(HG):
            top, total, acc = state[hd]
            mixed = acc / total
            head = pl.ds(hd * HD, HD)
            ot[head, cols] = mixed
            otb[head, cols] = mixed.astype(BF16)
            lse[hd, :, cols] = jnp.broadcast_to(top + jnp.log(total), (8, SQ))
        for k in range(PAIR):
            block = i * PAIR + k

            def keep_block(block=block):
                oa[o_slot, :] = otb[:, rows_of(block)]

            pl.when(block == blk)(keep_block)
            pl.when(block != blk)(lambda block=block: o_copy(block).start())
        for j in range(1, 4):
            pl.when(i == j)(functools.partial(after_block, j))
        return carried

    lax.fori_loop(0, S // PAIR, attend, 0)
    if A > 2:
        for w in range(3):
            w3_line(w, 2)
    swaps[2].start()

    def o_arrived(k, carried):
        links.copy(
            otb.at[:, rows_of(0)], oa.at[o_slot], sibling, index=first_o + k, keep=False
        ).make().wait_recv()
        return carried

    lax.fori_loop(1, S, o_arrived, 0)
    for w in range(3):
        if A > 2:
            w3_core(w, 1)
            w3_side(w, 2)
        else:
            w3_side(w, 0)
            w3_core(w, 0)

    def o_sent(i, carried):
        pl.when(i != blk)(lambda: o_copy(i).sent())
        return carried

    otok, mid, ffin, up, hid, outb = (ref[k] for k in ("otok", "mid", "ffin", "up", "hid", "outb"))
    ug, fg, mg, og, mgt = (ref[k] for k in ("ug", "fg", "mg", "og", "mgt"))
    small = ref["small"]

    def tile(n):
        return pl.ds(pl.multiple_of(n * W, W), W)

    def turn_o(n, carried):
        otok[:, tile(n)] = oa[tile(n), :].T
        return carried

    lax.fori_loop(0, NW, turn_o, 0)
    for w in range(3):
        if A > 2:
            w3_core(w, 2)
        for k in range(3, A - 1):
            w3_line(w, k)
            w3_side(w, k)
            w3_core(w, k)
    w3_whole(0)

    def out_step(n, carried):
        added = dot(otok[...], w3[0, :, tile(n)]) + gains[2:3, tile(n)]
        mid[:, tile(n)] = tok[:, tile(n)].astype(F32) + added
        return carried

    lax.fori_loop(0, NW, out_step, 0)

    def strip(i):
        return pl.ds(pl.multiple_of(i * STEP, STEP), STEP)

    def ff_norm(i, carried):
        x = mid[strip(i), :]
        ffin[strip(i), :] = (x * unit(x) * gain_ff).astype(BF16)
        return carried

    lax.fori_loop(0, L // STEP, ff_norm, 0)
    w3_whole(1)

    def up_step(n, carried):
        pre = dot(ffin[...], w3[1, :, tile(n)]) + gains[3:4, tile(n)]
        up[:, tile(n)] = pre
        hid[:, tile(n)] = (pre * jax.nn.sigmoid(pre)).astype(BF16)
        return carried

    lax.fori_loop(0, NW, up_step, 0)
    w3_whole(2)

    def down_step(n, carried):
        added = dot(hid[...], w3[2, :, tile(n)]) + gains[4:5, tile(n)]
        outb[:, tile(n)] = (mid[:, tile(n)] + added).astype(BF16)
        return carried

    lax.fori_loop(0, NW, down_step, 0)
    back_out = links.copy(outb, ref["out"], home, moves, moves)
    back_out.start()

    def keep_out():
        kept = local(outb, ref["out"], 0)
        kept.start()
        kept.wait()

    pl.when(stays)(keep_out)
    swaps[2].arrived()
    small[...] = jnp.zeros_like(small)

    def up_back(n, carried):
        pre = up[:, tile(n)]
        gate = jax.nn.sigmoid(pre)
        grad = dot_nt(cot[...], w3[2, tile(n), :]) * gate * (1.0 + pre * (1.0 - gate))
        grad = grad.astype(BF16)
        ug[:, tile(n)] = grad
        small[3:4, tile(n)] = jnp.sum(grad.astype(F32), axis=0, keepdims=True)
        return carried

    lax.fori_loop(0, NW, up_back, 0)

    def ff_back(n, carried):
        fg[:, tile(n)] = dot_nt(ug[...], w3[1, tile(n), :])
        return carried

    lax.fori_loop(0, NW, ff_back, 0)

    def mid_back(i, carried):
        x, grad, above_grad = mid[strip(i), :], fg[strip(i), :], cot[strip(i), :].astype(F32)
        inverse = unit(x)
        normed = x * inverse
        small[1:2, :] += jnp.sum(grad * normed, axis=0, keepdims=True)
        scaled = grad * gain_ff
        mean = jnp.mean(scaled * normed, axis=-1, keepdims=True)
        total = above_grad + inverse * (scaled - normed * mean)
        mg[strip(i), :] = total
        rounded = total.astype(BF16)
        og[strip(i), :] = rounded
        small[2:3, :] += jnp.sum(rounded.astype(F32), axis=0, keepdims=True)
        small[4:5, :] += jnp.sum(above_grad, axis=0, keepdims=True)
        return carried

    lax.fori_loop(0, L // STEP, mid_back, 0)

    dot_t = ref["dot_t"]
    first_m = links.block(S)

    def m_copy(k):
        g2 = (g + k) % S
        at = pl.ds(pl.multiple_of(g2 * E, 16), E)
        return links.copy(
            mgt.at[at], dot_t.at[:, rows_of(blk)], device(g2 // q, a, g2 % q),
            index=first_m + k, keep=False,
        )

    def mixed_step(k, carried):
        at = pl.ds(pl.multiple_of(((g + k) % S) * E, 16), E)
        mgt[at, :] = dot_nt(w3[0, at, :], og[...]).astype(BF16)
        pl.when(k < S)(lambda: m_copy(k).start())
        return carried

    lax.fori_loop(1, S + 1, mixed_step, 0)
    dot_t[:, rows_of(blk)] = mgt[pl.ds(pl.multiple_of(g * E, 16), E), :]

    freed, freed_again = ref["freed"], ref["freed_again"]
    writers = [sibling] + [peer(u, c, v) for v in b_off[1:]] + [peer(v, c, b) for v in u_off[1:]]

    def release(sem):
        for where in writers:
            pl.semaphore_signal(sem, inc=1, device_id=where, device_id_type=MESH)

    for group in (up_w, down_w, side_w, own_w, core_w, core_own):
        for moved in group.values():
            moved.sent()
            links.copies.remove(moved)
    release(freed)

    gp, rc = ref["gp"], ref["rc"]
    rcin = [w3.at[0, :, 0:DH], w3.at[0, :, DH:D], w3.at[1, :, 0:DH]]
    core_g = [links.copy(gp.at[w], rcin[w], sibling) for w in range(3)]

    def weight_grad(w, left, right):
        if left is not None:

            def turn(n, carried):
                oa[tile(n), :] = left[:, tile(n)].T
                return carried

            lax.fori_loop(0, NW, turn, 0)

        def step(n, carried):
            here = pl.ds(pl.multiple_of(n * SR, 16), SR)
            side = oa[here, :]
            gp[w, here, :] = dot(side, right[:, other_half]).astype(BF16)
            rc[w, n // q, n % q] = dot(side, right[:, own_half]).astype(BF16)
            return carried

        lax.fori_loop(0, S, step, 0)

    weight_grad(0, None, og)
    pl.semaphore_wait(freed, len(writers))
    core_g[0].start()
    weight_grad(2, hid, cot)
    core_g[2].start()
    weight_grad(1, ffin, ug)
    core_g[1].start()

    def m_arrived(k, carried):
        m_copy(k).arrived()
        return carried

    lax.fori_loop(1, S, m_arrived, 0)

    A2 = A // 2
    u_rows = [pl.ds(pl.multiple_of(v * SRH, 16), SRH) for v in u_off]
    my_rows = u_rows[0]
    qm, um = q - 1, U - 1

    def t1b(w, db, a2):
        at = ((w * qm + db - 1) * A2 + a2) * SR
        assert at + SR <= D
        return w3.at[1, at : at + SR, DH:D]

    def t1u(w, du, a2, b2):
        at = (((w * um + du - 1) * A2 + a2) * q + b2) * SRH
        assert at + SRH <= D
        return w3.at[2, at : at + SRH, 0:DH]

    def t2b(w, db, a2):
        at = ((w * qm + db - 1) * A2 + a2) * SRH
        return w3.at[2, at : at + SRH, DH:D]

    def t2u(w, du, a2):
        at = (3 * qm * A2 + (w * um + du - 1) * A2 + a2) * SRH
        assert at + SRH <= D
        return w3.at[2, at : at + SRH, DH:D]

    first_b, first_u, second_b, second_u = {}, {}, {}, {}
    for w in range(3):
        for a2 in range(A2):
            for db in range(1, q):
                to = peer(u, c, b_off[db])
                first_b[w, db, a2] = links.copy(rc.at[w, a2, b_off[db]], t1b(w, db, a2), to)
                second_b[w, db, a2] = links.copy(
                    rc.at[w, A2 + a2, b_off[db], my_rows], t2b(w, db, a2), to
                )
            if H > 1:
                for du in range(1, U):
                    to = peer(u_off[du], c, b)
                    for b2 in range(q):
                        first_u[w, du, a2, b2] = links.copy(
                            rc.at[w, A2 + a2, b2, u_rows[du]], t1u(w, du, a2, b2), to
                        )
                    second_u[w, du, a2] = links.copy(
                        rc.at[w, a2, b, u_rows[du]], t2u(w, du, a2), to
                    )

    def add_into(target, *more):
        total = target[...].astype(F32)
        for other in more:
            total = total + other[...].astype(F32)
        target[...] = total.astype(BF16)

    def core_sum(w):
        core_g[w].arrived()

        def step(n, carried):
            a2, b2 = n // q, n % q
            here = pl.ds(pl.multiple_of(n * SR, 16), SR)
            add_into(rc.at[w, a2, b2], rcin[w].at[here])
            return carried

        lax.fori_loop(0, S, step, 0)
        for key, moved in list(first_b.items()) + list(first_u.items()):
            if key[0] == w:
                moved.start()

    def side_sum_1(w):
        for db in range(1, q):
            for a2 in range(A2):
                first_b[w, db, a2].arrived()
                add_into(rc.at[w, a2, b], t1b(w, db, a2))
        if H > 1:
            for du in range(1, U):
                for a2 in range(A2):
                    for b2 in range(q):
                        first_u[w, du, a2, b2].arrived()
                        add_into(rc.at[w, A2 + a2, b2, my_rows], t1u(w, du, a2, b2))
        for key, moved in list(second_b.items()) + list(second_u.items()):
            if key[0] == w:
                moved.start()

    def side_sum_2(w):
        for db in range(1, q):
            for a2 in range(A2):
                second_b[w, db, a2].arrived()
                add_into(rc.at[w, A2 + a2, b, my_rows], t2b(w, db, a2))
        if H > 1:
            for du in range(1, U):
                for a2 in range(A2):
                    second_u[w, du, a2].arrived()
                    add_into(rc.at[w, a2, b, my_rows], t2u(w, du, a2))

    class Line:
        def __init__(self, part, landed):
            self.part, self.landed = part, landed
            self.first_up, self.first_down = links.block(A), links.block(A)

        def copy(self, d, upward):
            slot = jnp.where(d == a + 1, A, d) if upward else d
            return links.copy(
                self.part(d),
                self.landed(slot),
                above if upward else below,
                index=(self.first_up if upward else self.first_down) + d,
                keep=False,
            )

        def begin(self):
            for k in range(1, A):
                pl.when(a == 0)(lambda k=k: self.copy(A - k, True).make().start())
                pl.when(a == A - 1)(lambda k=k: self.copy(k - 1, False).make().start())

        def step(self, t):
            for upward in (True, False):
                d = A - 1 + a - t if upward else a + t - (A - 1)
                if upward:
                    takes = (a > 0) & (d >= a) & (d <= A - 1)
                    passes = takes & (d > a)
                    slot = jnp.where(d == a, A, d)
                else:
                    takes = (a < A - 1) & (d <= a) & (d >= 0)
                    passes = takes & (d < a)
                    slot = d
                d = jnp.clip(d, 0, A - 1)
                slot = jnp.clip(slot, 0, A)

                def take(d=d, upward=upward, slot=slot):
                    self.copy(d, upward).make().wait_recv()
                    add_into(self.part(d), near(self.landed(slot), self.near_name, 7))

                pl.when(takes)(take)
                pl.when(passes)(lambda d=d, upward=upward: self.copy(d, upward).make().start())

        def finish(self):
            for d in range(A):
                pl.when(a < d)(lambda d=d: self.copy(d, True).make().wait_send())
                pl.when(a > d)(lambda d=d: self.copy(d, False).make().wait_send())

    cu = ref["cu"]
    lines = []
    for w in range(3):
        lines.append(
            Line(
                lambda d, w=w: rc.at[w, d, b, my_rows],
                lambda slot, w=w: cu.at[slot, w],
            )
        )
        lines[-1].near_name = "c_rows"

    delta, dqt, dqkvt = ref["delta"], ref["dqt"], ref["dqkvt"]
    for hd in range(HG):
        head = slice(hd * HD, (hd + 1) * HD)
        total = jnp.sum(dot_t[head, :].astype(F32) * ot[head, :], axis=0, keepdims=True)
        delta[hd, :, :] = jnp.broadcast_to(total, (8, T))
    dqt[...] = jnp.zeros_like(dqt)
    core_sum(0)

    def after_back(j):
        if j == 0:
            core_sum(1)
            core_sum(2)
        elif j == 1:
            side_sum_1(0)
        elif j == 2:
            side_sum_1(1)
            side_sum_2(0)
            lines[0].begin()
        elif j == 3:
            side_sum_1(2)
            side_sum_2(1)
            lines[1].begin()

    def attend_back(j, carried):
        here = wide_rows(j)

        def query_block(i, state, on_diagonal):
            cols = wide_rows(i)
            result = []
            for hd in range(HG):
                dk, dv = state[hd]
                head = pl.ds(hd * HD, HD)
                score = dot(keys[hd, here, :], qt[hd, :, cols])
                if on_diagonal:
                    score = jnp.where(diagonal, score, masked_score)
                p = jnp.exp(score - lse[hd, 0:1, cols])
                d_out = dot_t[head, cols]
                dp = dot(vals[hd, here, 0:HD], d_out)
                ds = (p * (dp - delta[hd, 0:1, cols])).astype(BF16)
                dv = dv + dot_nt(d_out, p.astype(BF16))
                dk = dk + dot_nt(qt[hd, 0:HD, cols], ds)
                dqt[head, cols] += dot(kt[hd, :, here], ds)
                result.append((dk, dv))
            return tuple(result)

        zero = jnp.zeros((HD, SQ), F32)
        state = query_block(j, tuple((zero, zero) for _ in range(HG)), True)
        state = lax.fori_loop(j + 1, S // PAIR, functools.partial(query_block, on_diagonal=False), state)
        for hd in range(HG):
            dk, dv = state[hd]
            dqkvt[pl.ds(E + hd * HD, HD), here] = dk.astype(BF16)
            dqkvt[pl.ds(2 * E + hd * HD, HD), here] = dv.astype(BF16)
        for n in range(4):
            pl.when(j == n)(functools.partial(after_back, n))
        return carried

    lax.fori_loop(0, S // PAIR, attend_back, 0)
    if CW > 3 * E:
        dqkvt[3 * E :, :] = jnp.zeros((CW - 3 * E, T), BF16)

    def query_part(i, carried):
        cols = rows_of(i)
        dqkvt[0:E, cols] = (dqt[:, cols] * qgain_col[0:E]).astype(BF16)
        return carried + jnp.sum(dqt[:, cols] * qpre[:, cols], axis=1, keepdims=True)

    scale_terms = lax.fori_loop(0, S, query_part, jnp.zeros((E, 1), F32))

    gq, cqu, gall = ref["gq"], ref["cqu"], ref["gall"]

    def qkv_grad(n, carried):
        gq[tile(n), :] = dot(dqkvt[...], near(xa.at[:, tile(n)], "x_cols", 7)[...]).T.astype(BF16)
        return carried

    lax.fori_loop(0, NW, qkv_grad, 0)
    QR = q * SR
    line_q = Line(
        lambda d: gq.at[pl.ds(pl.multiple_of(d * QR, 16), QR)], lambda slot: cqu.at[slot]
    )
    line_q.near_name = "q_rows"
    line_q.begin()

    for group in (own_x, pass_x, sib_x):
        for moved in group.values():
            moved.sent()
            links.copies.remove(moved)

    ags, arc = ref["ags"], ref["arc"]

    def slot_of(n, rows):
        page, row = divmod(n * HALF, D)
        return w3.at[page, row : row + rows]

    order = [(u2, b2) for u2 in range(U) for b2 in range(q)]
    slots_used = 2 * U * q
    core_a = {}
    for n, (u2, b2) in enumerate(order):
        core_a[u2, b2] = links.copy(ags.at[pl.ds(n * L, L)], slot_of(2 * n, L), sibling)
    dtok = ref["dtok"]
    side_sum_2(2)
    lines[2].begin()
    release(freed_again)
    pl.semaphore_wait(freed_again, len(writers))

    def partial_rows(m, carried, others):
        block = block_of(m // q, 1 - c if others else c, m % q)
        dtok[...] = dqkvt[:, rows_of(block)].T
        for k in range(NW):
            at = slice(k * W, (k + 1) * W)
            part = dot_nt(dtok[...], wq[at, :]).astype(BF16)
            target = ags if others else arc
            target[rows_of(m), at] = part
        if others:
            for j, key in enumerate(order):
                pl.when(m == j)(core_a[key].start)
        return carried

    lax.fori_loop(0, U * q, functools.partial(partial_rows, others=True), 0)
    lax.fori_loop(0, U * q, functools.partial(partial_rows, others=False), 0)


    def part(u2, b2, h):
        return arc.at[half_rows(u2 * q + b2, h)]

    afb, afu, asb, asu, landing = {}, {}, {}, {}, {}

    def land(key):
        nonlocal slots_used
        landing[key] = slot_of(slots_used, HALF)
        slots_used += 1
        assert slots_used * HALF <= 3 * D
        return landing[key]

    for db in range(1, q):
        to = peer(u, c, b_off[db])
        for u2 in range(U):
            afb[db, u2] = links.copy(part(u2, b_off[db], 0), land(("fb", db, u2)), to)
        asb[db] = links.copy(part(u, b_off[db], 1), land(("sb", db)), to)
    for du in range(1, U):
        to = peer(u_off[du], c, b)
        for b2 in range(q):
            afu[du, b2] = links.copy(part(u_off[du], b2, 1), land(("fu", du, b2)), to)
        asu[du] = links.copy(part(u_off[du], b, 0), land(("su", du)), to)

    def add_rows(target, other, count):
        def step(i, carried):
            add_into(target.at[strip(i)], other.at[strip(i)])
            return carried

        lax.fori_loop(0, count // STEP, step, 0)

    for u2, b2 in order:
        core_a[u2, b2].arrived()

        add_rows(arc.at[rows_of(u2 * q + b2)], slot_of(2 * order.index((u2, b2)), L), L)
    for moved in list(afb.values()) + list(afu.values()):
        moved.start()

    for db in range(1, q):
        for u2 in range(U):
            afb[db, u2].arrived()
            add_rows(part(u2, b, 0), landing["fb", db, u2], HALF)
    for du in range(1, U):
        for b2 in range(q):
            afu[du, b2].arrived()
            add_rows(part(u, b2, 1), landing["fu", du, b2], HALF)
    for moved in list(asb.values()) + list(asu.values()):
        moved.start()
    line_q.step(1)
    for t in range(1, A):
        for line in lines:
            line.step(t)
        if t > 1:
            line_q.step(t)

    ones = jnp.ones((8, T), BF16)
    head_sums = dot_nt(ones, dqkvt[...])
    small[pl.ds(8 + g, 1), 0:CW] = head_sums[0:1]
    small[5:6, 0:E] = jnp.transpose(jnp.broadcast_to(scale_terms, (E, 128)))[0:1, :]

    for db in range(1, q):
        asb[db].arrived()
        add_rows(part(u, b, 1), landing["sb", db], HALF)
    for du in range(1, U):
        asu[du].arrived()
        add_rows(part(u, b, 0), landing["su", du], HALF)

    def tok_back(i, carried):
        x = tok[strip(i), :].astype(F32)
        grad = arc[pl.ds(pl.multiple_of((u * q + b) * L + i * STEP, STEP), STEP), :].astype(F32)
        inverse = unit(x)
        normed = x * inverse
        small[0:1, :] += jnp.sum(grad * normed, axis=0, keepdims=True)
        scaled = grad * gain_attn
        mean = jnp.mean(scaled * normed, axis=-1, keepdims=True)
        ref["gtb"][strip(i), :] = (mg[strip(i), :] + inverse * (scaled - normed * mean)).astype(BF16)
        return carried

    lax.fori_loop(0, L // STEP, tok_back, 0)
    back_tok = links.copy(ref["gtb"], ref["gtok"], home, moves, moves)
    back_tok.start()

    def keep_tok():
        kept = local(ref["gtb"], ref["gtok"], 0)
        kept.start()
        kept.wait()

    pl.when(stays)(keep_tok)

    stages = [
        [sibling],
        [peer(u, c, b_off[db]) for db in range(1, q)],
        [peer(u_off[du], c, b) for du in range(1, U)],
        [device(r, (a + k) % A, b) for k in range(1, A)],
    ]
    stages = [stage for stage in stages if stage]
    sums, landed = ref["sums"], ref["landed"]
    count, moved_small = 0, []
    for n, stage in enumerate(stages):
        moved_small.append(
            [links.copy(sums.at[n], landed.at[count + k], to) for k, to in enumerate(stage)]
        )
        count += len(stage)

    def small_stage(n):
        for moved in moved_small[n]:
            moved.arrived()
        total = sums[n]
        first = sum(len(stage) for stage in stages[:n])
        for k in range(len(stages[n])):
            total = total + landed[first + k]
        return total

    sums[0] = small[...]
    for moved in moved_small[0]:
        moved.start()

    wide = {}
    for db in range(1, q):
        at = gq.at[pl.ds(pl.multiple_of(a * QR + b_off[db] * SR, 16), SR)]
        wide[db] = links.copy(at, gall.at[g], device(r, a, b_off[db]))
        wide[db].start()
    gall[g] = gq[pl.ds(pl.multiple_of(a * QR + b * SR, 16), SR), :]
    go = ref["go"]
    piece = rc.at[:, a, b, my_rows]
    spread = []
    if H > 1:
        at = go.at[:, my_rows, own_half]
        for du in range(U):
            for dc in range(2):
                if du or dc:
                    spread.append(links.copy(piece, at, peer(u_off[du], (c + dc) % 2, b)))
    else:
        partials = [
            links.copy(piece, ref["ru"].at[du - 1], peer(u_off[du], c, b)) for du in range(1, U)
        ]
        for moved in partials:
            moved.start()
        for moved in partials:
            moved.arrived()
        for moved in partials:
            moved.sent()
            links.copies.remove(moved)
        for k in range(U - 1):
            for w in range(3):
                add_into(rc.at[w, a, b, my_rows], near(ref["ru"].at[k, w], "c_rows", 7))
        spread.append(links.copy(piece, go.at[:, :, own_half], sibling))
    for moved in spread:
        moved.start()
    go[:, my_rows, own_half] = piece[...]

    if len(stages) > 1:
        sums[1] = small_stage(0)
        for moved in moved_small[1]:
            moved.start()
    q_across, q_core = [], []
    for db in range(1, q):
        wide[db].arrived()
    here = pl.ds(r * q, q)
    for du in range(1, U):
        q_across.append(links.copy(gall.at[here], gall.at[here], peer(u_off[du], c, b)))
        q_across[-1].start()
    for du in range(U):
        here = pl.ds((u_from[du] * 2 + c) * q, q)
        q_core.append(links.copy(gall.at[here], gall.at[here], sibling))
    q_core[0].start()
    for n in range(1, len(stages) - 1):
        sums[n + 1] = small_stage(n)
        for moved in moved_small[n + 1]:
            moved.start()
    for moved in spread:
        moved.arrived()
    for du in range(1, U):
        q_across[du - 1].arrived()
        q_core[du].start()
    ref["g_small"][...] = small_stage(len(stages) - 1)
    for moved in q_core:
        moved.arrived()
    unpacked = [ref[name].at[pl.ds(0, SR)] for name in ("mid", "up", "mg")]
    for g2 in range(S):
        mine = gall[g2]
        for n in range(3):
            unpacked[n][:, g2 * E : (g2 + 1) * E] = mine[:, n * E : (n + 1) * E].astype(F32)
    written = [
        local(unpacked[n], ref[name], n) for n, name in enumerate(("g_query", "g_key", "g_value"))
    ]
    for copy in written:
        copy.start()
    for copy in written:
        copy.wait()
    back_out.arrived()
    back_tok.arrived()

    lax.fori_loop(0, S, o_sent, 0)

    def m_sent(k, carried):
        m_copy(k).sent()
        return carried

    lax.fori_loop(1, S, m_sent, 0)
    for line in lines + [line_q]:
        line.finish()
    for moved in links.copies:
        moved.sent()
    return links.used


def shards(
    R,
    S,
    tokens,
    lengths,
    parents,
    w_query,
    w_key,
    w_value,
    w_out,
    w_up,
    w_down,
    gain_attn,
    gain_ff,
    query_scale,
    bias_query,
    bias_value,
    bias_out,
    bias_up,
    bias_down,
    cotangent,
):
    L, D = tokens.shape
    SR = w_query.shape[0]
    HG = HEADS // S
    E = HG * HEAD_DIM
    CW = -(-3 * E // 128) * 128
    q, U, A, T = S // R, R // 2, R, S * L
    H = U if SR % (16 * U) == 0 else 1
    SRH = SR // H
    DH = D // 2
    NS = 8 + S
    segments = lengths.shape[1]
    dims = dict(R=R, S=S, L=L, D=D, HG=HG, E=E, CW=CW, SR=SR, H=H, SRH=SRH, segments=segments)

    tab = jnp.pad(
        jnp.concatenate([lengths, parents], axis=0).astype(F32), ((0, 6), (0, 128 - segments))
    )
    by_group = [w.reshape(SR, S, E) for w in (w_query, w_key, w_value)]
    wcat = jnp.pad(jnp.concatenate(by_group, axis=2), ((0, 0), (0, 0), (0, CW - 3 * E)))
    wcat = wcat.transpose(1, 0, 2)
    bias_rows = [bias_query.reshape(S, E), jnp.zeros((S, E), F32), bias_value.reshape(S, E)]
    biascat = jnp.pad(jnp.concatenate(bias_rows, axis=1), ((0, 0), (0, CW - 3 * E)))
    biascat = jnp.broadcast_to(biascat[:, None, :], (S, 8, CW))
    query_gain = query_base * jax.nn.softplus(query_scale) / math.sqrt(HEAD_DIM)
    qgain = jnp.pad(jnp.tile(query_gain, HG), (0, CW - E), constant_values=1.0)
    qgain = jnp.broadcast_to(qgain[None, :], (8, CW))
    zero_row = jnp.zeros_like(gain_attn)
    gains = jnp.stack(
        [gain_attn, gain_ff, bias_out, bias_up, bias_down, zero_row, zero_row, zero_row]
    )

    operands = dict(
        tokens=tokens, cotangent=cotangent, tab=tab, wcat=wcat, w_out=w_out, w_up=w_up,
        w_down=w_down, biascat=biascat, qgain=qgain, gains=gains,
    )
    outputs = dict(
        out=((L, D), BF16), gtok=((L, D), BF16), g_query=((SR, D), F32), g_key=((SR, D), F32),
        g_value=((SR, D), F32), go=((3, SR, D), BF16),
        g_small=((NS, D), F32),
    )
    um = max(U - 1, 1)
    peers = 1 + (q - 1) + (U - 1) + (A - 1)
    scratch = dict(
        tok=((L, D), BF16), cot=((L, D), BF16), tabs=((8, 128), F32),
        wq=((D, CW), BF16), w3=((3, D, D), BF16), xa=((T, D), BF16),
        qkvf=((CW, L), F32), qpre=((E, T), F32), qt=((HG, 128, T), BF16),
        keys=((HG, T, 128), BF16), kt=((HG, HEAD_DIM, T), BF16),
        vals=((HG, T, 128), BF16), vt=((HG, HEAD_DIM, T), BF16),
        ot=((E, T), F32), otb=((E, T), BF16), lse=((HG, 8, T), F32), oa=((D, L), BF16),
        otok=((L, D), BF16), mid=((L, D), F32), ffin=((L, D), BF16), up=((L, D), F32),
        hid=((L, D), BF16), outb=((L, D), BF16),
        mg=((L, D), F32), og=((L, D), BF16), mgt=((D, L), BF16), dot_t=((E, T), BF16),
        small=((NS, D), F32), gp=((3, D, DH), BF16),
        rc=((3, A, q, SR, DH), BF16),
        cu=((A + 1, 3, SRH, DH), BF16), delta=((HG, 8, T), F32), dqkvt=((CW, T), BF16),
        ags=((T // 2, D), BF16), arc=((T // 2, D), BF16),
        dtok=((L, CW), BF16),
        gq=((D, CW), BF16), cqu=((A + 1, q * SR, CW), BF16),
        gall=((S, SR, CW), BF16),
        sums=((5, NS, D), F32), landed=((peers, NS, D), F32),
    )
    if H == 1:
        scratch["ru"] = ((um, 3, SR, DH), BF16)
    held = [jax.ShapeDtypeStruct(*v) for v in scratch.values()]
    dims["fits"] = sum(v.size * v.dtype.itemsize for v in held) <= VMEM_BYTES - (6 << 20)
    results = len(outputs)
    distant = ["out", "gtok", "g_query", "g_key", "g_value"]
    if dims["fits"]:
        scratch.pop("ags")
        scratch.pop("arc")
    else:
        for name in ("xa", "cu", "ru"):
            outputs[name] = scratch.pop(name)
            distant.append(name)
        scratch["x_rows"] = ((L, D), BF16)
        scratch["x_cols"] = ((T, 256), BF16)
        scratch["c_rows"] = ((SRH, DH), BF16)
    names = list(operands) + list(outputs) + list(scratch)
    names += ["send_sems", "recv_sems", "local_sems", "freed", "freed_again"]

    counted = [1024]

    def kernel(*refs):
        named = dict(zip(names, refs))
        for later, earlier in (("fg", "up"), ("dqt", "ot"), ("ug", "otok"), ("gtb", "ffin")):
            named[later] = named[earlier]
        named["wqt"] = named["dqkvt"].at[:, 0:D]
        if dims["fits"]:
            named["ags"] = named["xa"].at[pl.ds(0, T // 2)]
            named["arc"] = named["xa"].at[pl.ds(T // 2, T // 2)]
        counted[0] = layer_kernel(dims, named)

    whole = pl.BlockSpec(memory_space=pltpu.VMEM)
    far = ("tokens", "cotangent", "wcat", "w_out", "w_up", "w_down")
    def call(*operands):
        return pl.pallas_call(
        kernel,
        out_shape=[jax.ShapeDtypeStruct(*shape) for shape in outputs.values()],
        in_specs=[pl.BlockSpec(memory_space=pl.ANY) if k in far else whole for k in operands],
        out_specs=[pl.BlockSpec(memory_space=pl.ANY) if k in distant else whole for k in outputs],
        scratch_shapes=[pltpu.VMEM(*shape) for shape in scratch.values()]
        + [pltpu.SemaphoreType.DMA((counted[0],))] * 2
        + [pltpu.SemaphoreType.DMA((8,))]
        + [pltpu.SemaphoreType.REGULAR] * 2,
        compiler_params=pltpu.CompilerParams(
            collective_id=0, has_side_effects=True, vmem_limit_bytes=VMEM_BYTES
        ),
    )(*operands)

    jax.eval_shape(call, *operands.values())
    made = call(*operands.values())
    out, gtok, g_query, g_key, g_value, go, g_small = made[:results]
    g_out, g_up, g_down = (go[w].astype(F32) for w in range(3))
    scale = jnp.sum(g_small[5, :E].reshape(HG, HEAD_DIM), axis=0)
    scale = scale * query_base * jax.nn.sigmoid(query_scale) / math.sqrt(HEAD_DIM)
    by_head = g_small[8:, : 3 * E]
    return (
        out,
        gtok,
        g_query,
        g_key,
        g_value,
        g_out,
        g_up,
        g_down,
        g_small[0],
        g_small[1],
        scale,
        by_head[:, :E].reshape(D),
        by_head[:, 2 * E :].reshape(D),
        g_small[2],
        g_small[3],
        g_small[4],
    )


def solution(mesh):
    rows, line, copied = P(("rep", "shard"), None), P("shard", None), P()
    in_specs = (rows, P("rep", None), P("rep", None)) + (line,) * 6 + (copied,) * 8 + (rows,)
    out_specs = (rows, rows) + (line,) * 6 + (copied,) * 8
    body = functools.partial(shards, mesh.shape["rep"], mesh.shape["shard"])
    return jax.shard_map(
        body, mesh=mesh, in_specs=in_specs, out_specs=out_specs, check_vma=False
    )
```

```python
import functools
import math

import jax
import jax.numpy as jnp
from jax import lax
from jax.experimental import pallas as pl
from jax.experimental.pallas import tpu as pltpu
from jax.sharding import PartitionSpec as P

HEADS = 16
HEAD_DIM = 80
MESH = pl.DeviceIdType.MESH
F32 = jnp.float32
BF16 = jnp.bfloat16

norm_eps = 1e-06
query_base = 1.442695
masked_score = -1e30
LABELS = 16
VMEM_BYTES = 64 << 20


def dot(left, right):
    return jnp.dot(left, right, preferred_element_type=F32)


def dot_nt(left, right):
    return lax.dot_general(left, right, (((1,), (1,)), ((), ())), preferred_element_type=F32)


def when(condition, body):
    if condition is True:
        body()
    elif condition is not False:
        pl.when(condition)(body)


class Copy:
    def __init__(self, make, sends, receives):
        self.make, self.sends, self.receives = make, sends, receives

    def start(self):
        when(self.sends, lambda: self.make().start())

    def arrived(self):
        when(self.receives, lambda: self.make().wait_recv())

    def sent(self):
        when(self.sends, lambda: self.make().wait_send())


class Links:
    def __init__(self, send_sems, recv_sems):
        self.send_sems, self.recv_sems, self.used, self.copies = send_sems, recv_sems, 0, []

    def block(self, count):
        first = self.used
        self.used += count
        return first

    def copy(self, src, dst, device, sends=True, receives=True, index=None, keep=True):
        if index is None:
            index = self.block(1)

        def make():
            return pltpu.make_async_remote_copy(
                src_ref=src,
                dst_ref=dst,
                send_sem=self.send_sems.at[index],
                recv_sem=self.recv_sems.at[index],
                device_id=device,
                device_id_type=MESH,
            )

        made = Copy(make, sends, receives)
        if keep:
            self.copies.append(made)
        return made


def layer_kernel(dims, refs):
    R, S, L, D = dims["R"], dims["S"], dims["L"], dims["D"]
    HG, E, CW, SR, H, SRH = (dims[k] for k in ("HG", "E", "CW", "SR", "H", "SRH"))
    q, U, A, T = S // R, R // 2, R, S * L
    HD = HEAD_DIM
    HALF, DH = L // 2, D // 2
    W = 256
    NW = D // W
    ref = refs
    r, s = lax.axis_index("rep"), lax.axis_index("shard")
    u, c, a, b = r // 2, r % 2, s // q, s % q

    def rho(i):
        return (i % 2) * (R // 2) + i // 2

    def rho_back(j):
        return (j % (R // 2)) * 2 + j // (R // 2)

    def turned(i, layer):
        return (i + (R // 2) * (layer // (R // 2))) % R

    def place_of(line_block, layer):
        return turned(rho_back(line_block), layer)

    def device(r2, a2, b2):
        return (r2, a2 * q + b2)

    def peer(u2, c2, b2):
        return device(u2 * 2 + c2, a, b2)

    def block_of(u2, c2, b2):
        return rho(turned(u2 * 2 + c2, a)) * q + b2

    def rows_of(blk):
        return pl.ds(pl.multiple_of(blk * L, L), L)

    g = r * q + b
    blk = block_of(u, c, b)
    u_off = [(u + d) % U for d in range(U)]
    b_off = [(b + d) % q for d in range(q)]
    u_from = [(u + U - d) % U for d in range(U)]
    b_from = [(b + q - d) % q for d in range(q)]
    home_r, home_a = place_of(a, rho(r)), rho(r)
    home = device(home_r, home_a, b)
    origin_r, origin_a = rho_back(a), rho(turned(r, a))
    origin = device(origin_r, origin_a, b)
    stays = jnp.logical_and(home_r == r, home_a == a)
    moves = jnp.logical_not(stays)
    apart = jnp.logical_or(home_r != origin_r, home_a != origin_a)
    sibling = peer(u, 1 - c, b)
    above = device(r, jnp.minimum(a + 1, A - 1), b)
    below = device(r, jnp.maximum(a - 1, 0), b)
    own_half = pl.ds(pl.multiple_of(c * DH, 128), DH)
    other_half = pl.ds(pl.multiple_of((1 - c) * DH, 128), DH)

    links = Links(ref["send_sems"], ref["recv_sems"])

    local_sems = ref["local_sems"]

    def local(src, dst, n):
        return pltpu.make_async_copy(src, dst, local_sems.at[n])

    def near(src, name, n):
        if dims["fits"] or name == "q_rows":
            return src
        copy = local(src, ref[name], n)
        copy.start()
        copy.wait()
        return ref[name]

    def shard_rows(a2, b2):
        return pl.ds(pl.multiple_of((a2 * q + b2) * SR, 16), SR)

    w3 = ref["w3"]
    names = ("w_query", "w_key", "w_value")
    parts = [ref[name].at[pl.ds(0, SR)] for name in ("hid", "ffin", "outb")]
    near_parts = [local(ref[names[n]], parts[n], n) for n in range(3)]
    names = ("w_out", "w_up", "w_down")
    own_shards = [local(ref[names[w]], w3.at[w, shard_rows(a, b)], 4 + w) for w in range(3)]
    near_rows = [local(ref["tokens"], ref["otok"], 3), local(ref["cotangent"], ref["og"], 7)]
    for copy in near_rows[:1] + near_parts + own_shards + near_rows[1:]:
        copy.start()

    barrier = pltpu.get_barrier_semaphore()

    def greet(where):
        pl.semaphore_signal(barrier, inc=1, device_id=where, device_id_type=MESH)

    for k in range(1, S):
        g2 = (g + k) % S
        greet(device(g2 // q, a, g2 % q))
    for k in range(1, A):
        greet(device(r, (a + k) % A, b))
    spread_out = [(u2, k) for u2 in u_off[1:] for k in range(1, A)] if U * A <= 16 else []
    for u2, k in spread_out:
        greet(device(u2 * 2 + c, (a + k) % A, b))
    pl.when(moves)(lambda: greet(home))
    pl.when(apart)(lambda: greet(origin))

    gains, biascat, qgain, tab = ref["gains"], ref["biascat"], ref["qgain"], ref["tab"]
    rows = ("gain_attn", "gain_ff", "bias_out", "bias_up", "bias_down", "bias_query", "bias_value")
    for n, name in enumerate(rows):
        gains[n : n + 1, :] = ref[name][...].reshape(1, D)
    segments = dims["segments"]
    tab[...] = jnp.zeros((8, 128), F32)
    tab[0:1, 0:segments] = ref["lengths"][...].astype(F32)
    tab[1:2, 0:segments] = ref["parents"][...].astype(F32)
    biascat[...] = jnp.zeros((8, CW), F32)

    def bias_slice(k):
        biascat[0:1, 0:E] = gains[5:6, k * E : (k + 1) * E]
        biascat[0:1, 2 * E : 3 * E] = gains[6:7, k * E : (k + 1) * E]

    for k in range(S):
        pl.when(g == k)(functools.partial(bias_slice, k))
    scale = ref["query_scale"][...].reshape(1, HD)
    soft = jnp.maximum(scale, 0.0) + jnp.log(1.0 + jnp.exp(-jnp.abs(scale)))
    qgain[...] = jnp.ones((8, CW), F32)
    for hd in range(HG):
        qgain[0:1, hd * HD : (hd + 1) * HD] = soft * (query_base / math.sqrt(HD))

    wq, wqt, wcat = ref["wq"], ref["wqt"], ref["gall"]
    for copy in near_parts:
        copy.wait()

    def cut_columns(r2):
        for b2 in range(q):
            first = (r2 * q + b2) * E
            for n in range(3):
                wcat[b2, :, n * E : (n + 1) * E] = parts[n][:, first : first + E]
            if CW > 3 * E:
                wcat[b2, :, 3 * E : CW] = jnp.zeros((SR, CW - 3 * E), BF16)

    for r2 in range(R):
        pl.when(r == r2)(functools.partial(cut_columns, r2))
    wq[shard_rows(a, b), :] = wcat[b]
    others = S - 1 + A - 1 + len(spread_out) + jnp.where(moves, 1, 0) + jnp.where(apart, 1, 0)
    pl.semaphore_wait(barrier, others)

    swaps = []
    for copy in near_rows:
        copy.wait()
    for name, there in (("otok", "tok"), ("tab", "tabs"), ("og", "cot")):
        swaps.append(links.copy(ref[name], ref[there], home, moves, moves))

    def keep_rows():
        for name, there in (("otok", "tok"), ("tab", "tabs"), ("og", "cot")):
            ref[there][...] = ref[name][...]

    swaps[1].start()
    swaps[0].start()

    wq_rows = shard_rows
    wcat_b = {}
    for db in range(1, q):
        wcat_b[db] = links.copy(
            wcat.at[b_off[db]], wq.at[wq_rows(a, b)], device(r, a, b_off[db])
        )
        wcat_b[db].start()
    up_q, down_q = {}, {}
    for k in range(A - 1):
        for db in range(q):
            low, high = jnp.maximum(a - k, 0), jnp.minimum(a + k, A - 1)
            slot = wq_rows(low, b_from[db])
            up_q[k, db] = links.copy(
                wq.at[slot], wq.at[slot], above,
                jnp.logical_and(a - k >= 0, a < A - 1), a - 1 - k >= 0,
            )
            slot = wq_rows(high, b_from[db])
            down_q[k, db] = links.copy(
                wq.at[slot], wq.at[slot], below,
                jnp.logical_and(a + k <= A - 1, a > 0), a + 1 + k <= A - 1,
            )
    up_q[0, 0].start()
    down_q[0, 0].start()

    def wq_pass(k):
        for db in range(q):
            up_q[k, db].arrived()
            down_q[k, db].arrived()
            if k + 1 < A - 1:
                up_q[k + 1, db].start()
                down_q[k + 1, db].start()

    def piece_rows(a2, b2, u2):
        if H == 1:
            return shard_rows(a2, b2)
        return pl.ds(pl.multiple_of((a2 * q + b2) * SR + u2 * SRH, 16), SRH)

    for copy in own_shards:
        copy.wait()
    pl.when(stays)(keep_rows)

    def b_then_u(u2, w):
        return u2 % 2 != a % 2 if w < 2 else False

    up_w, down_w, side_w, own_w, core_w, core_own = {}, {}, {}, {}, {}, {}
    slots = [sign * k for k in range(1, A) for sign in (1, -1)]
    for w in range(3):
        for k in range(A - 1):
            low, high = jnp.maximum(a - k, 0), jnp.minimum(a + k, A - 1)
            at = w3.at[w, piece_rows(low, b, u), own_half]
            up_w[w, k] = links.copy(
                at, at, above, jnp.logical_and(a - k >= 0, a < A - 1), a - 1 - k >= 0
            )
            at = w3.at[w, piece_rows(high, b, u), own_half]
            down_w[w, k] = links.copy(
                at, at, below, jnp.logical_and(a + k <= A - 1, a > 0), a + 1 + k <= A - 1
            )
        for slot in slots:
            valid = a + slot <= A - 1 if slot > 0 else a + slot >= 0
            a0 = jnp.clip(a + slot, 0, A - 1)
            at = w3.at[w, piece_rows(a0, b, u), own_half]
            for db in range(1, q):
                side_w[w, slot, 0, db] = links.copy(at, at, peer(u, c, b_off[db]), valid, valid)
            if H > 1:
                for du in range(1, U):
                    side_w[w, slot, du, 0] = links.copy(at, at, peer(u_off[du], c, b), valid, valid)
                    for db in range(1, q):
                        sent, came = b_then_u(u, w), b_then_u(u_from[du], w)
                        at = w3.at[w, piece_rows(a0, b_from[db], u), own_half]
                        side_w[w, slot, du, db] = links.copy(
                            at, at, peer(u_off[du], c, b),
                            jnp.logical_and(valid, sent), jnp.logical_and(valid, came),
                        )
                        at = w3.at[w, piece_rows(a0, b, u_from[du]), own_half]
                        other = jnp.logical_and(valid, jnp.logical_not(came))
                        side_w[w, slot, du, -db] = links.copy(
                            at, at, peer(u, c, b_off[db]), other, other
                        )
            at = w3.at[w, pl.ds(pl.multiple_of(a0 * q * SR, 16), q * SR), own_half]
            core_w[w, slot] = links.copy(at, at, sibling, valid, valid)
        for db in range(1, q):
            at = w3.at[w, shard_rows(a, b), own_half]
            own_w[w, db] = links.copy(at, at, peer(u, c, b_off[db]))
            at = w3.at[w, shard_rows(a, b_from[db]), own_half]
            core_own[w, db] = links.copy(at, at, sibling)

    for moved in own_w.values():
        moved.start()

    def w3_line(w, k):
        if k < 0:
            up_w[w, 0].start()
            down_w[w, 0].start()
            return
        up_w[w, k].arrived()
        down_w[w, k].arrived()
        if k + 1 < A - 1:
            up_w[w, k + 1].start()
            down_w[w, k + 1].start()
        for slot in (-(k + 1), k + 1):
            for (w2, slot2, du, db), moved in side_w.items():
                if (w2, slot2) == (w, slot) and (du == 0 or db == 0):
                    moved.start()

    def w3_side(w, k):
        if k < 0:
            for db in range(1, q):
                own_w[w, db].arrived()
                core_own[w, db].start()
            return
        for slot in (-(k + 1), k + 1):
            for db in range(1, q):
                side_w[w, slot, 0, db].arrived()
            if H > 1:
                for du in range(1, U):
                    side_w[w, slot, du, 0].arrived()
                    for db in range(1, q):
                        side_w[w, slot, du, db].start()
                        side_w[w, slot, du, -db].start()

    def w3_core(w, k):
        for slot in (-(k + 1), k + 1):
            if H > 1:
                for du in range(1, U):
                    for db in range(1, q):
                        side_w[w, slot, du, db].arrived()
                        side_w[w, slot, du, -db].arrived()
            core_w[w, slot].start()

    def w3_whole(w):
        for db in range(1, q):
            core_own[w, db].arrived()
        for slot in slots:
            core_w[w, slot].arrived()

    tok, cot, xa = ref["tok"], ref["cot"], ref["xa"]
    gain_attn, gain_ff = gains[0:1, :], gains[1:2, :]
    STEP = 32

    def unit(x):
        return lax.rsqrt(jnp.mean(x * x, axis=-1, keepdims=True) + norm_eps)

    def half_rows(block, h):
        return pl.ds(pl.multiple_of(block * L + h * HALF, HALF), HALF)

    own_x, pass_x, sib_x = {}, {}, {}
    for h in range(2):
        at = xa.at[half_rows(blk, h)]
        for db in range(1, q):
            own_x[h, 0, db] = links.copy(at, at, peer(u, c, b_off[db]))
        for du in range(1, U):
            own_x[h, du, 0] = links.copy(at, at, peer(u_off[du], c, b))
        for du in range(1, U):
            for db in range(1, q):
                if h == 0:
                    at = xa.at[half_rows(block_of(u, c, b_from[db]), h)]
                    pass_x[h, du, db] = links.copy(at, at, peer(u_off[du], c, b))
                else:
                    at = xa.at[half_rows(block_of(u_from[du], c, b), h)]
                    pass_x[h, du, db] = links.copy(at, at, peer(u, c, b_off[db]))
        for du in range(U):
            for db in range(q):
                at = xa.at[half_rows(block_of(u_from[du], c, b_from[db]), h)]
                sib_x[h, du, db] = links.copy(at, at, sibling)

    for db in range(1, q):
        wcat_b[db].arrived()
        up_q[0, db].start()
        down_q[0, db].start()
    for w in range(3):
        w3_line(w, -1)
    swaps[0].arrived()
    for h in range(2):

        def norm_step(i, carried, h=h):
            here = pl.ds(pl.multiple_of(h * HALF + i * STEP, STEP), STEP)
            x = tok[here, :].astype(F32)
            there = pl.ds(pl.multiple_of(blk * L + h * HALF + i * STEP, STEP), STEP)
            row = (x * unit(x) * gain_attn).astype(BF16)
            if dims["fits"]:
                xa[there, :] = row
            else:
                ref["x_rows"][here, :] = row
            return carried

        lax.fori_loop(0, HALF // STEP, norm_step, 0)
        if not dims["fits"]:
            here = pl.ds(h * HALF, HALF)
            out_of = local(ref["x_rows"].at[here], xa.at[half_rows(blk, h)], 7)
            out_of.start()
            out_of.wait()
        for moved in [m for (h2, *_), m in own_x.items() if h2 == h]:
            moved.start()
        sib_x[h, 0, 0].start()
    wq_pass(0)

    swaps[1].arrived()
    lane = lax.broadcasted_iota(jnp.int32, (LABELS, 128), 1)
    row = lax.broadcasted_iota(jnp.int32, (LABELS, 128), 0)
    lengths = jnp.broadcast_to(ref["tabs"][0:1, :], (LABELS, 128))
    seg_start = jnp.sum(jnp.where(lane < row, lengths, 0.0), axis=1, keepdims=True)
    seg_end = jnp.sum(jnp.where(lane <= row, lengths, 0.0), axis=1, keepdims=True)
    lane = lax.broadcasted_iota(jnp.int32, (128, 128), 1)
    row = lax.broadcasted_iota(jnp.int32, (128, 128), 0)
    parents = jnp.broadcast_to(ref["tabs"][1:2, :], (128, 128))
    is_parent = (parents == row.astype(F32)) & (lane > 0) & (lane < segments)
    reach = jnp.where((lane == row) | is_parent, 1.0, 0.0)
    for _ in range(max(1, (segments - 1).bit_length())):
        reach = jnp.minimum(dot(reach.astype(BF16), reach.astype(BF16)), 1.0)
    blocked = ((1.0 - reach[:LABELS, :LABELS]) * masked_score).astype(BF16)

    for db in range(1, q):
        own_x[0, 0, db].arrived()
        for du in range(1, U):
            pass_x[0, du, db].start()
        sib_x[0, 0, db].start()
    for du in range(1, U):
        own_x[1, du, 0].arrived()
        for db in range(1, q):
            pass_x[1, du, db].start()
        sib_x[1, du, 0].start()
    for k in range(1, A - 2):
        wq_pass(k)
    for w in range(3):
        w3_line(w, 0)
    for db in range(1, q):
        own_x[1, 0, db].arrived()
        sib_x[1, 0, db].start()
    for du in range(1, U):
        own_x[0, du, 0].arrived()
        sib_x[0, du, 0].start()
    for w in range(3):
        w3_side(w, -1)
    if A > 2:
        for w in range(3):
            w3_line(w, 1)
    for h in range(2):
        for du in range(1, U):
            for db in range(1, q):
                pass_x[h, du, db].arrived()
                sib_x[h, du, db].start()
    wq_pass(A - 2)

    def turn_wq(i, carried):
        here = pl.ds(pl.multiple_of(i * W, W), W)
        wqt[:, here] = wq[here, :].T
        return carried

    lax.fori_loop(0, NW, turn_wq, 0)
    bias_col = jnp.transpose(biascat[...])[:, 0:1]
    qgain_col = jnp.transpose(qgain[...])[:, 0:1]
    qkvf, qpre, qt, keys, kt, vals, vt = (
        ref[k] for k in ("qkvf", "qpre", "qt", "keys", "kt", "vals", "vt")
    )

    def project(k, carried):
        for j in range(S):

            def wait_rows(j=j):
                du, db, other = (j // 2) // q, (j // 2) % q, j % 2
                if other:
                    for h in range(2):
                        sib_x[h, du, db].arrived()

            pl.when(k == j)(wait_rows)
        du, db, other = (k // 2) // q, (k // 2) % q, k % 2
        block = block_of((u + U - du) % U, (c + other) % 2, (b + q - db) % q)
        cols = rows_of(block)
        x = near(xa.at[cols], "x_rows", 7)[...]
        qkvf[...] = dot_nt(wqt[...], x) + bias_col
        place = block * L + lax.broadcasted_iota(jnp.int32, (LABELS, L), 1)
        place = place.astype(F32)
        onehot = jnp.where((place >= seg_start) & (place < seg_end), 1.0, 0.0)
        far = dot(blocked, onehot.astype(BF16)).astype(BF16)
        for hd in range(HG):
            head = pl.ds(hd * HD, HD)
            pre = qkvf[head, :]
            qpre[head, cols] = pre
            qt[hd, 0:HD, cols] = (pre * qgain_col[hd * HD : (hd + 1) * HD]).astype(BF16)
            qt[hd, HD : HD + LABELS, cols] = far
            qt[hd, HD + LABELS : 128, cols] = jnp.zeros((128 - HD - LABELS, L), BF16)
            key = qkvf[pl.ds(E + hd * HD, HD), :]
            kt[hd, :, cols] = key.astype(BF16)
            wide = jnp.concatenate([key, onehot, jnp.zeros((128 - HD - LABELS, L), F32)], axis=0)
            keys[hd, cols, :] = wide.T.astype(BF16)
            value = qkvf[pl.ds(2 * E + hd * HD, HD), :]
            vt[hd, :, cols] = value.astype(BF16)
            wide = jnp.concatenate([value, jnp.zeros((128 - HD, L), F32)], axis=0)
            vals[hd, cols, :] = wide.T.astype(BF16)
        return carried

    lax.fori_loop(0, S, project, 0)

    ot, otb, lse, oa = ref["ot"], ref["otb"], ref["lse"], ref["oa"]
    first_o = links.block(S)
    o_slot = pl.ds(pl.multiple_of(g * E, 16), E)

    def o_copy(block):
        r2, b2 = place_of(block // q, a), block % q
        index = first_o + (r2 * q + b2 + S - g) % S
        return links.copy(
            otb.at[:, rows_of(block)], oa.at[o_slot], device(r2, a, b2), index=index, keep=False
        )

    PAIR = 2
    SQ = PAIR * L
    diagonal = lax.broadcasted_iota(jnp.int32, (SQ, SQ), 0) <= lax.broadcasted_iota(
        jnp.int32, (SQ, SQ), 1
    )
    for w in range(3):
        w3_side(w, 0)

    def after_block(i):
        if A <= 2:
            return
        if i == 0:
            for w in range(3):
                w3_line(w, 2)
        elif i == 1:
            w3_core(0, 0)
            w3_side(0, 1)
            w3_core(1, 0)
        elif i == 2:
            w3_side(1, 1)
            w3_core(2, 0)
            w3_core(0, 1)
            w3_side(2, 1)
        elif i == 3:
            w3_side(0, 2)
            w3_core(1, 1)
            w3_side(1, 2)

    def wide_rows(i):
        return pl.ds(pl.multiple_of(i * SQ, SQ), SQ)

    def attend(i, carried):
        cols = wide_rows(i)
        query = [qt[hd, :, cols] for hd in range(HG)]

        def key_block(j, state, on_diagonal):
            here = wide_rows(j)
            result = []
            for hd in range(HG):
                top, total, acc = state[hd]
                score = dot(keys[hd, here, :], query[hd])
                if on_diagonal:
                    score = jnp.where(diagonal, score, masked_score)
                new_top = jnp.maximum(top, jnp.max(score, axis=0, keepdims=True))
                p = jnp.exp(score - new_top)
                fade = jnp.exp(top - new_top)
                total = total * fade + jnp.sum(p, axis=0, keepdims=True)
                acc = acc * fade + dot(vt[hd, :, here], p.astype(BF16))
                result.append((new_top, total, acc))
            return tuple(result)

        start = tuple(
            (
                jnp.full((1, SQ), masked_score, F32),
                jnp.zeros((1, SQ), F32),
                jnp.zeros((HD, SQ), F32),
            )
            for _ in range(HG)
        )
        state = lax.fori_loop(0, i, functools.partial(key_block, on_diagonal=False), start)
        state = key_block(i, state, True)
        for hd in range(HG):
            top, total, acc = state[hd]
            mixed = acc / total
            head = pl.ds(hd * HD, HD)
            ot[head, cols] = mixed
            otb[head, cols] = mixed.astype(BF16)
            lse[hd, :, cols] = jnp.broadcast_to(top + jnp.log(total), (8, SQ))
        for k in range(PAIR):
            block = i * PAIR + k

            def keep_block(block=block):
                oa[o_slot, :] = otb[:, rows_of(block)]

            pl.when(block == blk)(keep_block)
            pl.when(block != blk)(lambda block=block: o_copy(block).start())
        for j in range(4):
            pl.when(i == j)(functools.partial(after_block, j))
        return carried

    lax.fori_loop(0, S // PAIR, attend, 0)
    swaps[2].start()
    def o_arrived(k, carried):
        links.copy(
            otb.at[:, rows_of(0)], oa.at[o_slot], sibling, index=first_o + k, keep=False
        ).make().wait_recv()
        return carried

    lax.fori_loop(1, S, o_arrived, 0)
    def w3_rest(w):
        if A > 2:
            if w == 2:
                w3_core(w, 1)
                w3_side(w, 2)
            w3_core(w, 2)
        else:
            w3_core(w, 0)
        for k in range(3, A - 1):
            w3_line(w, k)
            w3_side(w, k)
            w3_core(w, k)
        w3_whole(w)

    def o_sent(i, carried):
        pl.when(i != blk)(lambda: o_copy(i).sent())
        return carried

    otok, mid, ffin, up, hid, outb = (ref[k] for k in ("otok", "mid", "ffin", "up", "hid", "outb"))
    ug, fg, mg, og, mgt = (ref[k] for k in ("ug", "fg", "mg", "og", "mgt"))
    small = ref["small"]

    def tile(n):
        return pl.ds(pl.multiple_of(n * W, W), W)

    def turn_o(n, carried):
        otok[:, tile(n)] = oa[tile(n), :].T
        return carried

    swaps[0].sent()
    links.copies.remove(swaps[0])
    lax.fori_loop(0, NW, turn_o, 0)
    w3_rest(0)

    def out_step(n, carried):
        added = dot(otok[...], w3[0, :, tile(n)]) + gains[2:3, tile(n)]
        mid[:, tile(n)] = tok[:, tile(n)].astype(F32) + added
        return carried

    lax.fori_loop(0, NW, out_step, 0)

    def strip(i):
        return pl.ds(pl.multiple_of(i * STEP, STEP), STEP)

    def ff_norm(i, carried):
        x = mid[strip(i), :]
        ffin[strip(i), :] = (x * unit(x) * gain_ff).astype(BF16)
        return carried

    lax.fori_loop(0, L // STEP, ff_norm, 0)
    w3_rest(1)

    def up_step(n, carried):
        pre = dot(ffin[...], w3[1, :, tile(n)]) + gains[3:4, tile(n)]
        up[:, tile(n)] = pre
        hid[:, tile(n)] = (pre * jax.nn.sigmoid(pre)).astype(BF16)
        return carried

    lax.fori_loop(0, NW, up_step, 0)
    w3_rest(2)

    def down_step(n, carried):
        added = dot(hid[...], w3[2, :, tile(n)]) + gains[4:5, tile(n)]
        outb[:, tile(n)] = (mid[:, tile(n)] + added).astype(BF16)
        return carried

    lax.fori_loop(0, NW, down_step, 0)
    back_out = links.copy(outb, ref["out"], origin, moves, moves)
    back_out.start()

    def keep_out():
        kept = local(outb, ref["out"], 0)
        kept.start()
        kept.wait()

    pl.when(stays)(keep_out)
    swaps[2].arrived()
    swaps[2].sent()
    links.copies.remove(swaps[2])
    small[...] = jnp.zeros_like(small)

    def up_back(n, carried):
        pre = up[:, tile(n)]
        gate = jax.nn.sigmoid(pre)
        grad = dot_nt(cot[...], w3[2, tile(n), :]) * gate * (1.0 + pre * (1.0 - gate))
        grad = grad.astype(BF16)
        ug[:, tile(n)] = grad
        small[3:4, tile(n)] = jnp.sum(grad.astype(F32), axis=0, keepdims=True)
        return carried

    lax.fori_loop(0, NW, up_back, 0)

    def ff_back(n, carried):
        fg[:, tile(n)] = dot_nt(ug[...], w3[1, tile(n), :])
        return carried

    lax.fori_loop(0, NW, ff_back, 0)

    def mid_back(i, carried):
        x, grad, above_grad = mid[strip(i), :], fg[strip(i), :], cot[strip(i), :].astype(F32)
        inverse = unit(x)
        normed = x * inverse
        small[1:2, :] += jnp.sum(grad * normed, axis=0, keepdims=True)
        scaled = grad * gain_ff
        mean = jnp.mean(scaled * normed, axis=-1, keepdims=True)
        total = above_grad + inverse * (scaled - normed * mean)
        mg[strip(i), :] = total
        rounded = total.astype(BF16)
        og[strip(i), :] = rounded
        small[2:3, :] += jnp.sum(rounded.astype(F32), axis=0, keepdims=True)
        small[4:5, :] += jnp.sum(above_grad, axis=0, keepdims=True)
        return carried

    lax.fori_loop(0, L // STEP, mid_back, 0)

    dot_t = ref["dot_t"]
    first_m = links.block(S)

    def m_copy(k):
        g2 = (g + k) % S
        at = pl.ds(pl.multiple_of(g2 * E, 16), E)
        return links.copy(
            mgt.at[at], dot_t.at[:, rows_of(blk)], device(g2 // q, a, g2 % q),
            index=first_m + k, keep=False,
        )

    def mixed_step(k, carried):
        at = pl.ds(pl.multiple_of(((g + k) % S) * E, 16), E)
        mgt[at, :] = dot_nt(w3[0, at, :], og[...]).astype(BF16)
        pl.when(k < S)(lambda: m_copy(k).start())
        return carried

    lax.fori_loop(1, S + 1, mixed_step, 0)
    dot_t[:, rows_of(blk)] = mgt[pl.ds(pl.multiple_of(g * E, 16), E), :]

    freed, freed_again = ref["freed"], ref["freed_again"]
    writers = [sibling] + [peer(u, c, v) for v in b_off[1:]] + [peer(v, c, b) for v in u_off[1:]]

    def release(sem):
        for where in writers:
            pl.semaphore_signal(sem, inc=1, device_id=where, device_id_type=MESH)

    for group in (wcat_b, up_w, down_w, side_w, own_w, core_w, core_own):
        for moved in group.values():
            moved.sent()
            links.copies.remove(moved)
    release(freed)

    gp, rc = ref["gp"], ref["rc"]
    rcin = [w3.at[0, :, 0:DH], w3.at[0, :, DH:D], w3.at[1, :, 0:DH]]
    core_g = [links.copy(gp.at[w], rcin[w], sibling) for w in range(3)]

    def weight_grad(w, left, right):
        if left is not None:

            def turn(n, carried):
                oa[tile(n), :] = left[:, tile(n)].T
                return carried

            lax.fori_loop(0, NW, turn, 0)

        def step(n, carried):
            here = pl.ds(pl.multiple_of(n * SR, 16), SR)
            side = oa[here, :]
            gp[w, here, :] = dot(side, right[:, other_half]).astype(BF16)
            rc[w, n // q, n % q] = dot(side, right[:, own_half]).astype(BF16)
            return carried

        lax.fori_loop(0, S, step, 0)

    def m_arrived(k, carried):
        m_copy(k).arrived()
        return carried

    A2 = A // 2
    u_rows = [pl.ds(pl.multiple_of(v * SRH, 16), SRH) for v in u_off]
    my_rows = u_rows[0]
    qm, um = q - 1, U - 1

    def t1b(w, db, a2):
        at = D - 3 * qm * A2 * SR + ((w * qm + db - 1) * A2 + a2) * SR
        assert at >= 0
        return w3.at[1, at : at + SR, DH:D]

    def t1u(w, du, a2, b2):
        at = (((w * um + du - 1) * A2 + a2) * q + b2) * SRH
        assert at + SRH <= D
        return w3.at[2, at : at + SRH, 0:DH]

    def t2b(w, db, a2):
        at = ((w * qm + db - 1) * A2 + a2) * SRH
        return w3.at[2, at : at + SRH, DH:D]

    def t2u(w, du, a2):
        at = (3 * qm * A2 + (w * um + du - 1) * A2 + a2) * SRH
        assert at + SRH <= D
        return w3.at[2, at : at + SRH, DH:D]

    first_b, first_u, second_b, second_u = {}, {}, {}, {}
    for w in range(3):
        for a2 in range(A2):
            for db in range(1, q):
                to = peer(u, c, b_off[db])
                first_b[w, db, a2] = links.copy(rc.at[w, a2, b_off[db]], t1b(w, db, a2), to)
                second_b[w, db, a2] = links.copy(
                    rc.at[w, A2 + a2, b_off[db], my_rows], t2b(w, db, a2), to
                )
            if H > 1:
                for du in range(1, U):
                    to = peer(u_off[du], c, b)
                    for b2 in range(q):
                        first_u[w, du, a2, b2] = links.copy(
                            rc.at[w, A2 + a2, b2, u_rows[du]], t1u(w, du, a2, b2), to
                        )
                    second_u[w, du, a2] = links.copy(
                        rc.at[w, a2, b, u_rows[du]], t2u(w, du, a2), to
                    )

    def add_into(target, *more):
        total = target[...].astype(F32)
        for other in more:
            total = total + other[...].astype(F32)
        target[...] = total.astype(BF16)

    def core_sum(w):
        core_g[w].arrived()

        def step(n, carried):
            a2, b2 = n // q, n % q
            here = pl.ds(pl.multiple_of(n * SR, 16), SR)
            add_into(rc.at[w, a2, b2], rcin[w].at[here])
            return carried

        lax.fori_loop(0, S, step, 0)
        for key, moved in list(first_b.items()) + list(first_u.items()):
            if key[0] == w:
                moved.start()

    def side_sum_1(w):
        for db in range(1, q):
            for a2 in range(A2):
                first_b[w, db, a2].arrived()
                add_into(rc.at[w, a2, b], t1b(w, db, a2))
        if H > 1:
            for du in range(1, U):
                for a2 in range(A2):
                    for b2 in range(q):
                        first_u[w, du, a2, b2].arrived()
                        add_into(rc.at[w, A2 + a2, b2, my_rows], t1u(w, du, a2, b2))
        for key, moved in list(second_b.items()) + list(second_u.items()):
            if key[0] == w:
                moved.start()

    def side_sum_2(w):
        for db in range(1, q):
            for a2 in range(A2):
                second_b[w, db, a2].arrived()
                add_into(rc.at[w, A2 + a2, b, my_rows], t2b(w, db, a2))
        if H > 1:
            for du in range(1, U):
                for a2 in range(A2):
                    second_u[w, du, a2].arrived()
                    add_into(rc.at[w, a2, b, my_rows], t2u(w, du, a2))

    weight_grad(0, None, og)
    pl.semaphore_wait(freed, len(writers))
    core_g[0].start()
    weight_grad(2, hid, cot)
    core_g[2].start()
    core_sum(0)
    weight_grad(1, ffin, ug)
    core_g[1].start()
    core_sum(2)
    lax.fori_loop(1, S, m_arrived, 0)

    assert A & (A - 1) == 0
    strides = [1 << n for n in range(A.bit_length() - 1)]

    def across(k):
        return a + k - 2 * k * (a // k % 2)

    class Line:
        def __init__(self, part, landed, near_name):
            self.part, self.landed, self.near_name, self.steps = part, landed, near_name, []
            slot = 0
            for k in strides:
                step = []
                for m in range(A // (2 * k)):
                    mine = a % (2 * k) + 2 * k * m
                    theirs = across(k) % (2 * k) + 2 * k * m
                    copy = links.copy(part(theirs), landed(slot), device(r, across(k), b))
                    step.append((copy, mine, slot))
                    slot += 1
                self.steps.append(step)

        def begin(self, n=0):
            for copy, _, _ in self.steps[n]:
                copy.start()

        def step(self, n):
            for copy, mine, slot in self.steps[n]:
                copy.arrived()
                add_into(self.part(mine), near(self.landed(slot), self.near_name, 7))
            if n + 1 < len(self.steps):
                self.begin(n + 1)

    cu = ref["cu"]
    lines = []
    for w in range(3):
        lines.append(
            Line(
                lambda d, w=w: rc.at[w, d, b, my_rows],
                lambda slot, w=w: cu.at[slot, w],
                "c_rows",
            )
        )

    delta, dqt, dqkvt = ref["delta"], ref["dqt"], ref["dqkvt"]
    for hd in range(HG):
        head = slice(hd * HD, (hd + 1) * HD)
        total = jnp.sum(dot_t[head, :].astype(F32) * ot[head, :], axis=0, keepdims=True)
        delta[hd, :, :] = jnp.broadcast_to(total, (8, T))
    dqt[...] = jnp.zeros_like(dqt)
    NB = S // PAIR
    starts = [sum(NB - k for k in range(j)) for j in range(NB)]
    pairs = NB * (NB + 1) // 2
    jobs = {
        2: [lambda: core_sum(1), lambda: release(freed_again)],
        min(3, pairs - 2): [lambda: side_sum_1(0)],
        min(7, pairs - 2): [lambda: side_sum_1(2)],
    }
    dkt, dvt = ref["dkt"], ref["dvt"]

    def attend_back(n, carried):
        j = sum(jnp.where(n >= start, 1, 0) for start in starts[1:])
        start = sum(jnp.where(n >= starts[k], starts[k] - starts[k - 1], 0) for k in range(1, NB))
        i = n - start + j
        here, cols = wide_rows(j), wide_rows(i)

        def block(on_diagonal):
            for hd in range(HG):
                head = pl.ds(hd * HD, HD)
                score = dot(keys[hd, here, :], qt[hd, :, cols])
                if on_diagonal:
                    score = jnp.where(diagonal, score, masked_score)
                p = jnp.exp(score - lse[hd, 0:1, cols])
                d_out = dot_t[head, cols]
                dp = dot(vals[hd, here, 0:HD], d_out)
                ds = (p * (dp - delta[hd, 0:1, cols])).astype(BF16)
                dv = dot_nt(d_out, p.astype(BF16))
                dk = dot_nt(qt[hd, 0:HD, cols], ds)
                if on_diagonal:
                    dvt[head, :], dkt[head, :] = dv, dk
                else:
                    dvt[head, :] += dv
                    dkt[head, :] += dk
                dqt[head, cols] += dot(kt[hd, :, here], ds)

        pl.when(i == j)(lambda: block(True))
        pl.when(i != j)(lambda: block(False))

        def keep():
            dqkvt[E : 2 * E, here] = dkt[...].astype(BF16)
            dqkvt[2 * E : 3 * E, here] = dvt[...].astype(BF16)

        pl.when(i == NB - 1)(keep)
        for m, todo in jobs.items():

            def run(todo=todo):
                for job in todo:
                    job()

            pl.when(n == m)(run)
        return carried

    lax.fori_loop(0, pairs, attend_back, 0)
    if CW > 3 * E:
        dqkvt[3 * E :, :] = jnp.zeros((CW - 3 * E, T), BF16)

    def query_part(i, carried):
        cols = rows_of(i)
        dqkvt[0:E, cols] = (dqt[:, cols] * qgain_col[0:E]).astype(BF16)
        return carried + jnp.sum(dqt[:, cols] * qpre[:, cols], axis=1, keepdims=True)

    scale_terms = lax.fori_loop(0, S, query_part, jnp.zeros((E, 1), F32))

    gq, cqu, gall = ref["gq"], ref["cqu"], ref["gall"]

    def qkv_grad(n, carried):
        gq[tile(n), :] = dot(dqkvt[...], near(xa.at[:, tile(n)], "x_cols", 7)[...]).T.astype(BF16)
        return carried

    lax.fori_loop(0, NW, qkv_grad, 0)
    QR = q * SR
    line_q = Line(
        lambda d: gq.at[pl.ds(pl.multiple_of(d * QR, 16), QR)],
        lambda slot: cqu.at[slot],
        "q_rows",
    )
    line_q.begin()

    for group in (own_x, pass_x, sib_x):
        for moved in group.values():
            moved.sent()
            links.copies.remove(moved)

    ones = jnp.ones((8, T), BF16)
    head_sums = dot_nt(ones, dqkvt[...])
    small[pl.ds(8 + g, 1), 0:CW] = head_sums[0:1]
    small[5:6, 0:E] = jnp.transpose(jnp.broadcast_to(scale_terms, (E, 128)))[0:1, :]
    sums, landed, late, late_landed = (ref[k] for k in ("sums", "landed", "late", "late_landed"))

    class Total:
        def __init__(self, held, arrivals, stages):
            self.held, self.arrivals, self.stages, count = held, arrivals, [], 0
            for n, stage in enumerate(stages):
                moves_n = []
                for to in stage:
                    copy = links.copy(held.at[n], arrivals.at[count], to)
                    moves_n.append((copy, count))
                    count += 1
                self.stages.append(moves_n)

        def begin(self, n):
            for moved, _ in self.stages[n]:
                moved.start()

        def end(self, n):
            total = self.held[n]
            for moved, at in self.stages[n]:
                moved.arrived()
                total = total + self.arrivals[at]
            self.held[n + 1] = total

    on_b = [peer(u, c, b_off[db]) for db in range(1, q)]
    on_u = [peer(u_off[du], c, b) for du in range(1, U)]
    on_a = [[device(r, across(k), b)] for k in strides]
    total = Total(sums, landed, on_a + [on_b, on_u, [sibling]])
    line_all = [device(r, (a + k) % A, b) for k in range(1, A)]
    wide_u = [device(u2 * 2 + c, (a + k) % A, b) for u2 in u_off for k in range(A)][1:]
    late_stages = [wide_u] if U * A <= 16 else [line_all, on_u]
    late_total = Total(late, late_landed, late_stages + [on_b, [sibling]])

    def late_step(n):
        late_total.end(n)
        if n + 1 < len(late_total.stages):
            late_total.begin(n + 1)

    sums[0] = small[...]
    total.begin(0)

    def total_step(n):
        total.end(n)
        if n + 1 < len(total.stages):
            total.begin(n + 1)

    ags, arc = ref["ags"], ref["arc"]

    def slot_of(n, rows):
        page, row = divmod(n * HALF, D)
        return w3.at[page, row : row + rows]

    order = [(u2, b2) for u2 in range(U) for b2 in range(q)]
    taken = {0: 0, 1: 0, 2: 0}
    if H > 1:
        taken[2] = 3 * um * A2 * q * SRH
    usable = [
        n
        for n in range(2 * U * q, 3 * D // HALF)
        if n * HALF % D >= taken[n * HALF // D]
        and (n * HALF // D != 1 or n * HALF % D + HALF <= D - 3 * qm * A2 * SR)
    ]
    core_a = {}
    for n, (u2, b2) in enumerate(order):
        core_a[u2, b2] = links.copy(ags.at[pl.ds(n * L, L)], slot_of(2 * n, L), sibling)
    dtok = ref["dtok"]
    side_sum_2(0)
    lines[0].begin()
    pl.semaphore_wait(freed_again, len(writers))

    def partial_rows(m, carried, others):
        block = block_of(m // q, 1 - c if others else c, m % q)
        dtok[...] = dqkvt[:, rows_of(block)].T
        for k in range(NW):
            at = slice(k * W, (k + 1) * W)
            part = dot_nt(dtok[...], wq[at, :]).astype(BF16)
            target = ags if others else arc
            target[rows_of(m), at] = part
        if others:
            for j, key in enumerate(order):
                pl.when(m == j)(core_a[key].start)
        return carried

    lax.fori_loop(0, U * q, functools.partial(partial_rows, others=True), 0)
    lax.fori_loop(0, U * q, functools.partial(partial_rows, others=False), 0)


    def part(u2, b2, h):
        return arc.at[half_rows(u2 * q + b2, h)]

    afb, afu, asb, asu, landing = {}, {}, {}, {}, {}

    def land(key):
        landing[key] = slot_of(usable.pop(0), HALF)
        return landing[key]

    for db in range(1, q):
        to = peer(u, c, b_off[db])
        for u2 in range(U):
            afb[db, u2] = links.copy(part(u2, b_off[db], 0), land(("fb", db, u2)), to)
        asb[db] = links.copy(part(u, b_off[db], 1), land(("sb", db)), to)
    for du in range(1, U):
        to = peer(u_off[du], c, b)
        for b2 in range(q):
            afu[du, b2] = links.copy(part(u_off[du], b2, 1), land(("fu", du, b2)), to)
        asu[du] = links.copy(part(u_off[du], b, 0), land(("su", du)), to)

    def add_rows(target, other, count):
        def step(i, carried):
            add_into(target.at[strip(i)], other.at[strip(i)])
            return carried

        lax.fori_loop(0, count // STEP, step, 0)

    side_sum_2(2)
    lines[2].begin()
    side_sum_1(1)
    for u2, b2 in order:
        core_a[u2, b2].arrived()

        add_rows(arc.at[rows_of(u2 * q + b2)], slot_of(2 * order.index((u2, b2)), L), L)
    for moved in list(afb.values()) + list(afu.values()):
        moved.start()
    lines[0].step(0)
    line_q.step(0)
    lines[2].step(0)

    for db in range(1, q):
        for u2 in range(U):
            afb[db, u2].arrived()
            add_rows(part(u2, b, 0), landing["fb", db, u2], HALF)
    for du in range(1, U):
        for b2 in range(q):
            afu[du, b2].arrived()
            add_rows(part(u, b2, 1), landing["fu", du, b2], HALF)
    for moved in list(asb.values()) + list(asu.values()):
        moved.start()

    wide, q_across, q_core = {}, [], []
    for db in range(1, q):
        at = gq.at[pl.ds(pl.multiple_of(a * QR + b_off[db] * SR, 16), SR)]
        wide[db] = links.copy(at, gall.at[g], device(r, a, b_off[db]))
    here = pl.ds(r * q, q)
    for du in range(1, U):
        q_across.append(links.copy(gall.at[here], gall.at[here], peer(u_off[du], c, b)))
    for du in range(U):
        here = pl.ds((u_from[du] * 2 + c) * q, q)
        q_core.append(links.copy(gall.at[here], gall.at[here], sibling))

    def own_q():
        for db in range(1, q):
            wide[db].start()
        gall[g] = gq[pl.ds(pl.multiple_of(a * QR + b * SR, 16), SR), :]

    def across_q():
        for db in range(1, q):
            wide[db].arrived()
        for moved in q_across:
            moved.start()
        q_core[0].start()

    def core_q():
        for du in range(1, U):
            q_across[du - 1].arrived()
            q_core[du].start()

    go = ref["go"]
    spread, core_go, partials = {}, {}, {}
    for w in range(3):
        piece = rc.at[w, a, b, my_rows]
        for du in range(1, U):
            to = peer(u_off[du], c, b)
            if H > 1:
                spread[w, du] = links.copy(piece, go.at[w, my_rows, own_half], to)
            else:
                partials[w, du] = links.copy(piece, ref["ru"].at[du - 1, w], to)
        at = go.at[w, :, own_half]
        core_go[w] = links.copy(at, at, sibling)

    def own_go(w):
        for (w2, du), moved in partials.items():
            if w2 == w:
                moved.start()
        for (w2, du), moved in partials.items():
            if w2 == w:
                moved.arrived()
                moved.sent()
                links.copies.remove(moved)
        for (w2, du), moved in partials.items():
            if w2 == w:
                add_into(rc.at[w, a, b, my_rows], near(ref["ru"].at[du - 1, w], "c_rows", 7))
        for (w2, du), moved in spread.items():
            if w2 == w:
                moved.start()
        go[w, my_rows, own_half] = rc[w, a, b, my_rows]

    def last_lines(w):
        for n in range(1, len(strides)):
            lines[w].step(n)
        own_go(w)

    def core_go_on(w):
        for (w2, du), moved in spread.items():
            if w2 == w:
                moved.arrived()
        core_go[w].start()

    total_step(0)
    side_sum_2(1)
    lines[1].begin()
    last_lines(0)

    for db in range(1, q):
        asb[db].arrived()
        add_rows(part(u, b, 1), landing["sb", db], HALF)
    for du in range(1, U):
        asu[du].arrived()
        add_rows(part(u, b, 0), landing["su", du], HALF)
    small[0:1, :] = jnp.zeros((1, D), F32)

    def tok_back(i, carried):
        x = tok[strip(i), :].astype(F32)
        grad = arc[pl.ds(pl.multiple_of((u * q + b) * L + i * STEP, STEP), STEP), :].astype(F32)
        inverse = unit(x)
        normed = x * inverse
        small[0:1, :] += jnp.sum(grad * normed, axis=0, keepdims=True)
        scaled = grad * gain_attn
        mean = jnp.mean(scaled * normed, axis=-1, keepdims=True)
        ref["gtb"][strip(i), :] = (mg[strip(i), :] + inverse * (scaled - normed * mean)).astype(BF16)
        return carried

    lax.fori_loop(0, L // STEP, tok_back, 0)
    late[0] = small[0:1, :]
    late_total.begin(0)
    back_tok = links.copy(ref["gtb"], ref["gtok"], origin, moves, moves)
    back_tok.start()

    def keep_tok():
        kept = local(ref["gtb"], ref["gtok"], 0)
        kept.start()
        kept.wait()

    pl.when(stays)(keep_tok)
    for n in range(1, len(strides)):
        line_q.step(n)
    own_q()
    lines[1].step(0)
    last_lines(2)
    across_q()
    core_go_on(0)
    last_lines(1)
    core_go_on(2)
    late_step(0)
    total_step(1)
    late_step(1)
    core_q()
    core_go_on(1)
    for n in range(2, len(late_total.stages)):
        late_step(n)
    for n in range(2, len(total.stages)):
        total_step(n)
    ref["g_small"][...] = sums[len(total.stages)]
    ref["g_small"][0:1, :] = late[len(late_total.stages)]
    for w in range(3):
        core_go[w].arrived()
    for moved in q_core:
        moved.arrived()
    back_out.arrived()
    back_tok.arrived()

    lax.fori_loop(0, S, o_sent, 0)

    def m_sent(k, carried):
        m_copy(k).sent()
        return carried

    lax.fori_loop(1, S, m_sent, 0)
    for moved in links.copies:
        moved.sent()
    return links.used


def shards(
    R,
    S,
    tokens,
    lengths,
    parents,
    w_query,
    w_key,
    w_value,
    w_out,
    w_up,
    w_down,
    gain_attn,
    gain_ff,
    query_scale,
    bias_query,
    bias_value,
    bias_out,
    bias_up,
    bias_down,
    cotangent,
):
    L, D = tokens.shape
    SR = w_query.shape[0]
    HG = HEADS // S
    E = HG * HEAD_DIM
    CW = -(-3 * E // 128) * 128
    q, U, A, T = S // R, R // 2, R, S * L
    H = U if SR % (16 * U) == 0 else 1
    SRH = SR // H
    DH = D // 2
    NS = 8 + S
    segments = lengths.shape[1]
    dims = dict(R=R, S=S, L=L, D=D, HG=HG, E=E, CW=CW, SR=SR, H=H, SRH=SRH, segments=segments)

    operands = dict(
        tokens=tokens, cotangent=cotangent, w_query=w_query, w_key=w_key, w_value=w_value,
        w_out=w_out, w_up=w_up, w_down=w_down, lengths=lengths, parents=parents,
        gain_attn=gain_attn, gain_ff=gain_ff, query_scale=query_scale, bias_query=bias_query,
        bias_value=bias_value, bias_out=bias_out, bias_up=bias_up, bias_down=bias_down,
    )
    outputs = dict(
        out=((L, D), BF16), gtok=((L, D), BF16), go=((3, SR, D), BF16),
        gall=((S, SR, CW), BF16), g_small=((NS, D), F32),
    )
    um = max(U - 1, 1)
    peers = q + U + A + (U * A if U * A <= 16 else 0)
    line_steps = A.bit_length() - 1
    scratch = dict(
        tok=((L, D), BF16), cot=((L, D), BF16), tabs=((8, 128), F32),
        wq=((D, CW), BF16), w3=((3, D, D), BF16), xa=((T, D), BF16),
        qkvf=((CW, L), F32), qpre=((E, T), F32), qt=((HG, 128, T), BF16),
        keys=((HG, T, 128), BF16), kt=((HG, HEAD_DIM, T), BF16),
        vals=((HG, T, 128), BF16), vt=((HG, HEAD_DIM, T), BF16),
        ot=((E, T), F32), otb=((E, T), BF16), lse=((HG, 8, T), F32), oa=((D, L), BF16),
        otok=((L, D), BF16), mid=((L, D), F32), ffin=((L, D), BF16), up=((L, D), F32),
        hid=((L, D), BF16), outb=((L, D), BF16),
        mg=((L, D), F32), og=((L, D), BF16), mgt=((D, L), BF16), dot_t=((E, T), BF16),
        small=((NS, D), F32), gp=((3, D, DH), BF16),
        rc=((3, A, q, SR, DH), BF16),
        cu=((A - 1, 3, SRH, DH), BF16), delta=((HG, 8, T), F32), dqkvt=((CW, T), BF16),
        dkt=((E, 2 * L), F32), dvt=((E, 2 * L), F32),
        gains=((8, D), F32), biascat=((8, CW), F32), qgain=((8, CW), F32), tab=((8, 128), F32),
        ags=((T // 2, D), BF16), arc=((T // 2, D), BF16),
        dtok=((L, CW), BF16),
        gq=((D, CW), BF16), cqu=((A - 1, q * SR, CW), BF16),
        sums=((line_steps + 4, NS, D), F32), landed=((line_steps + q + U, NS, D), F32),
        late=((5, 1, D), F32), late_landed=((peers, 1, D), F32),
    )
    if H == 1:
        scratch["ru"] = ((um, 3, SR, DH), BF16)
    held = [jax.ShapeDtypeStruct(*v) for k, v in scratch.items() if k not in ("ags", "arc")]
    dims["fits"] = sum(v.size * v.dtype.itemsize for v in held) <= VMEM_BYTES - (6 << 20)
    results = len(outputs)
    distant = ["out", "gtok"]
    if dims["fits"]:
        scratch.pop("ags")
        scratch.pop("arc")
    else:
        for name in [k for k in ("xa", "cu", "ru") if k in scratch]:
            outputs[name] = scratch.pop(name)
            distant.append(name)
        scratch["x_rows"] = ((L, D), BF16)
        scratch["x_cols"] = ((T, 256), BF16)
        scratch["c_rows"] = ((SRH, DH), BF16)
    names = list(operands) + list(outputs) + list(scratch)
    names += ["send_sems", "recv_sems", "local_sems", "freed", "freed_again"]

    counted = [1024]

    def kernel(*refs):
        named = dict(zip(names, refs))
        for later, earlier in (("fg", "up"), ("dqt", "ot"), ("ug", "otok"), ("gtb", "ffin")):
            named[later] = named[earlier]
        named["wqt"] = named["dqkvt"].at[:, 0:D]
        if dims["fits"]:
            named["ags"] = named["xa"].at[pl.ds(0, T // 2)]
            named["arc"] = named["xa"].at[pl.ds(T // 2, T // 2)]
        counted[0] = layer_kernel(dims, named)

    whole = pl.BlockSpec(memory_space=pltpu.VMEM)
    far = ("tokens", "cotangent", "w_query", "w_key", "w_value", "w_out", "w_up", "w_down")
    def call(*operands):
        return pl.pallas_call(
        kernel,
        out_shape=[jax.ShapeDtypeStruct(*shape) for shape in outputs.values()],
        in_specs=[pl.BlockSpec(memory_space=pl.ANY) if k in far else whole for k in operands],
        out_specs=[pl.BlockSpec(memory_space=pl.ANY) if k in distant else whole for k in outputs],
        scratch_shapes=[pltpu.VMEM(*shape) for shape in scratch.values()]
        + [pltpu.SemaphoreType.DMA((counted[0],))] * 2
        + [pltpu.SemaphoreType.DMA((8,))]
        + [pltpu.SemaphoreType.REGULAR] * 2,
        compiler_params=pltpu.CompilerParams(
            collective_id=0, has_side_effects=True, vmem_limit_bytes=VMEM_BYTES
        ),
    )(*operands)

    jax.eval_shape(call, *operands.values())
    made = call(*operands.values())
    out, gtok, go, gall, g_small = made[:results]

    def finish(out, gtok, go, gall, sums, scale, *refs):
        made_out, made_gtok, grads, vectors = refs[0], refs[1], refs[2:8], refs[8:16]
        made_out[...] = out[...]
        made_gtok[...] = gtok[...]
        for g2 in range(S):
            mine = gall[g2]
            for n in range(3):
                grads[n][:, g2 * E : (g2 + 1) * E] = mine[:, n * E : (n + 1) * E].astype(F32)
        for w in range(3):
            grads[3 + w][...] = go[w].astype(F32)
        for n, at in ((0, 0), (1, 1), (5, 2), (6, 3), (7, 4)):
            vectors[n][...] = sums[at : at + 1, :].reshape(D)
        for n, at in ((3, 0), (4, 2 * E)):
            whole = jnp.concatenate([sums[8 + k : 9 + k, at : at + E] for k in range(S)], axis=1)
            vectors[n][...] = whole.reshape(D)
        terms = sum(sums[5:6, hd * HEAD_DIM : (hd + 1) * HEAD_DIM] for hd in range(HG))
        gate = jax.nn.sigmoid(scale[...].reshape(1, HEAD_DIM)) * (query_base / math.sqrt(HEAD_DIM))
        vectors[2][...] = (terms * gate).reshape(HEAD_DIM)

    final = [((L, D), BF16)] * 2 + [((SR, D), F32)] * 6 + [((D,), F32)] * 8
    final[10] = ((HEAD_DIM,), F32)
    return pl.pallas_call(
        finish,
        out_shape=[jax.ShapeDtypeStruct(*shape) for shape in final],
        in_specs=[whole] * 6,
        out_specs=[whole] * 16,
        compiler_params=pltpu.CompilerParams(vmem_limit_bytes=VMEM_BYTES),
    )(out, gtok, go, gall, g_small, query_scale)


def solution(mesh):
    rows, line, copied = P(("rep", "shard"), None), P("shard", None), P()
    in_specs = (rows, P("rep", None), P("rep", None)) + (line,) * 6 + (copied,) * 8 + (rows,)
    out_specs = (rows, rows) + (line,) * 6 + (copied,) * 8
    body = functools.partial(shards, mesh.shape["rep"], mesh.shape["shard"])
    return jax.shard_map(
        body, mesh=mesh, in_specs=in_specs, out_specs=out_specs, check_vma=False
    )
```

```python
import functools
import math

import jax
import jax.numpy as jnp
from jax import lax
from jax.experimental import pallas as pl
from jax.experimental.pallas import tpu as pltpu
from jax.sharding import PartitionSpec as P

HEADS = 16
HEAD_DIM = 80
MESH = pl.DeviceIdType.MESH
F32 = jnp.float32
BF16 = jnp.bfloat16

norm_eps = 1e-06
query_base = 1.442695
masked_score = -1e30
LABELS = 16
VMEM_BYTES = 64 << 20
SECOND = (
    "wg0", "wg2", "cs0", "wg1", "mwait", "delta", "B2", "cs2", "B6", "cs1", "B9", "release", "f2",
    "f0", "BX", "t", "qg", "ago", "t0", "g2", "agm", "ac", "g0", "Q0", "ab", "f1", "h00", "h01",
    "Q1", "h20", "au", "g1", "Q2", "h10", "h21", "t1", "k0", "end", "h11", "t2", "L0", "k1", "Q3",
    "L1", "t3", "k2", "t4", "L2",
)
FIRST = (
    "wcat", "tok", "carry", "n0", "wcat2", "own", "n1", "l2", "xb0", "tables", "xu0", "l1", "q0",
    "l0", "xu1", "q1", "l20", "q2", "l10", "coth", "xb1", "xp0", "l00", "l21", "l11", "turnq",
    "l01", "xp1", "s0", "s20", "project", "l02", "s00", "s10", "s02", "c00", "s01", "s2", "A0",
    "l12", "cot", "c10", "A1", "A2", "l22", "s21", "s11", "s12", "c01", "c20", "A3", "s1", "AX",
    "c02", "c12", "c11", "c21", "s22", "owait", "F0", "F1", "F2", "c22",
)


def dot(left, right):
    return jnp.dot(left, right, preferred_element_type=F32)


def dot_nt(left, right):
    return lax.dot_general(left, right, (((1,), (1,)), ((), ())), preferred_element_type=F32)


def when(condition, body):
    if condition is True:
        body()
    elif condition is not False:
        pl.when(condition)(body)


class Copy:
    def __init__(self, make, sends, receives):
        self.make, self.sends, self.receives = make, sends, receives

    def start(self):
        when(self.sends, lambda: self.make().start())

    def arrived(self):
        when(self.receives, lambda: self.make().wait_recv())

    def sent(self):
        when(self.sends, lambda: self.make().wait_send())


class Links:
    def __init__(self, send_sems, recv_sems):
        self.send_sems, self.recv_sems, self.used, self.copies = send_sems, recv_sems, 0, []

    def block(self, count):
        first = self.used
        self.used += count
        return first

    def copy(self, src, dst, device, sends=True, receives=True, index=None, keep=True):
        if index is None:
            index = self.block(1)

        def make():
            return pltpu.make_async_remote_copy(
                src_ref=src,
                dst_ref=dst,
                send_sem=self.send_sems.at[index],
                recv_sem=self.recv_sems.at[index],
                device_id=device,
                device_id_type=MESH,
            )

        made = Copy(make, sends, receives)
        if keep:
            self.copies.append(made)
        return made


def layer_kernel(dims, refs):
    R, S, L, D = dims["R"], dims["S"], dims["L"], dims["D"]
    HG, E, CW, SR, H, SRH = (dims[k] for k in ("HG", "E", "CW", "SR", "H", "SRH"))
    q, U, A, T = S // R, R // 2, R, S * L
    HD = HEAD_DIM
    HALF, DH = L // 2, D // 2
    W = 256
    NW = D // W
    ref = refs
    r, s = lax.axis_index("rep"), lax.axis_index("shard")
    u, c, a, b = r // 2, r % 2, s // q, s % q

    def rho(i):
        return (i % 2) * (R // 2) + i // 2

    def rho_back(j):
        return (j % (R // 2)) * 2 + j // (R // 2)

    def turned(i, layer):
        return (i + (R // 2) * (layer // (R // 2))) % R

    def place_of(line_block, layer):
        return turned(rho_back(line_block), layer)

    def device(r2, a2, b2):
        return (r2, a2 * q + b2)

    def peer(u2, c2, b2):
        return device(u2 * 2 + c2, a, b2)

    def block_of(u2, c2, b2):
        return rho(turned(u2 * 2 + c2, a)) * q + b2

    def rows_of(blk):
        return pl.ds(pl.multiple_of(blk * L, L), L)

    g = r * q + b
    blk = block_of(u, c, b)
    u_off = [(u + d) % U for d in range(U)]
    b_off = [(b + d) % q for d in range(q)]
    u_from = [(u + U - d) % U for d in range(U)]
    b_from = [(b + q - d) % q for d in range(q)]
    home_r, home_a = place_of(a, rho(r)), rho(r)
    home = device(home_r, home_a, b)
    origin_r, origin_a = rho_back(a), rho(turned(r, a))
    origin = device(origin_r, origin_a, b)
    stays = jnp.logical_and(home_r == r, home_a == a)
    moves = jnp.logical_not(stays)
    apart = jnp.logical_or(home_r != origin_r, home_a != origin_a)
    by_u = U == 2

    def crosses(r2, a2):
        layer = rho(r2)
        return jnp.logical_and(place_of(a2, layer) // 2 != r2 // 2, layer != a2) if by_u else False

    next_r = (1 - u) * 2 + c
    next_home = device(place_of(a, rho(next_r)), rho(next_r), b)
    carrier = device((1 - origin_r // 2) * 2 + origin_r % 2, origin_a, b)
    i_cross, i_carry, carried_in = crosses(r, a), crosses(next_r, a), crosses(origin_r, origin_a)
    direct = jnp.logical_and(moves, jnp.logical_not(i_cross))
    direct_in = jnp.logical_and(moves, jnp.logical_not(carried_in))
    sibling = peer(u, 1 - c, b)
    above = device(r, jnp.minimum(a + 1, A - 1), b)
    below = device(r, jnp.maximum(a - 1, 0), b)
    own_half = pl.ds(pl.multiple_of(c * DH, 128), DH)
    other_half = pl.ds(pl.multiple_of((1 - c) * DH, 128), DH)

    links = Links(ref["send_sems"], ref["recv_sems"])
    events = {}

    def event(name, job):
        events[name] = job

    def play(names):
        for name in names:
            events.pop(name)()

    def segments_of(order, first, last):
        parts, at = {None: []}, None
        for name in order:
            if name[:1] == first and (name[1:].isdigit() or name == last):
                at = name
                parts[at] = []
            else:
                parts[at].append(name)
        return parts

    def start_all(*copies):
        for moved in copies:
            moved.start()


    local_sems = ref["local_sems"]

    def local(src, dst, n):
        return pltpu.make_async_copy(src, dst, local_sems.at[n])

    def near(src, name, n):
        if dims["fits"] or name == "q_rows":
            return src
        copy = local(src, ref[name], n)
        copy.start()
        copy.wait()
        return ref[name]

    def shard_rows(a2, b2):
        return pl.ds(pl.multiple_of((a2 * q + b2) * SR, 16), SR)

    w3 = ref["w3"]
    names = ("w_query", "w_key", "w_value")
    parts = [ref[name].at[pl.ds(0, SR)] for name in ("hid", "ffin", "outb")]
    near_parts = [local(ref[names[n]], parts[n], n) for n in range(3)]
    names = ("w_out", "w_up", "w_down")
    own_shards = [local(ref[names[w]], w3.at[w, shard_rows(a, b)], 4 + w) for w in range(3)]
    near_rows = [local(ref["tokens"], ref["otok"], 3), local(ref["cotangent"], ref["og"], 7)]
    for copy in near_rows[:1] + near_parts + own_shards + near_rows[1:]:
        copy.start()

    barrier = pltpu.get_barrier_semaphore()

    def greet(where):
        pl.semaphore_signal(barrier, inc=1, device_id=where, device_id_type=MESH)

    for k in range(1, S):
        g2 = (g + k) % S
        greet(device(g2 // q, a, g2 % q))
    for k in range(1, A):
        greet(device(r, (a + k) % A, b))
    spread_out = [(u2, k) for u2 in u_off[1:] for k in range(1, A)] if U * A <= 16 else []
    for u2, k in spread_out:
        greet(device(u2 * 2 + c, (a + k) % A, b))
    pl.when(moves)(lambda: greet(home))
    pl.when(apart)(lambda: greet(origin))
    if by_u:
        pl.when(i_carry)(lambda: greet(next_home))
        pl.when(carried_in)(lambda: greet(carrier))

    gains, biascat, qgain, tab = ref["gains"], ref["biascat"], ref["qgain"], ref["tab"]
    rows = ("gain_attn", "gain_ff", "bias_out", "bias_up", "bias_down", "bias_query", "bias_value")
    for n, name in enumerate(rows):
        gains[n : n + 1, :] = ref[name][...].reshape(1, D)
    segments = dims["segments"]
    tab[...] = jnp.zeros((8, 128), F32)
    tab[0:1, 0:segments] = ref["lengths"][...].astype(F32)
    tab[1:2, 0:segments] = ref["parents"][...].astype(F32)
    biascat[...] = jnp.zeros((8, CW), F32)

    def bias_slice(k):
        biascat[0:1, 0:E] = gains[5:6, k * E : (k + 1) * E]
        biascat[0:1, 2 * E : 3 * E] = gains[6:7, k * E : (k + 1) * E]

    for k in range(S):
        pl.when(g == k)(functools.partial(bias_slice, k))
    scale = ref["query_scale"][...].reshape(1, HD)
    soft = jnp.maximum(scale, 0.0) + jnp.log(1.0 + jnp.exp(-jnp.abs(scale)))
    qgain[...] = jnp.ones((8, CW), F32)
    for hd in range(HG):
        qgain[0:1, hd * HD : (hd + 1) * HD] = soft * (query_base / math.sqrt(HD))

    wq, wqt, wcat = ref["wq"], ref["wqt"], ref["gall"]
    for copy in near_parts:
        copy.wait()

    def cut_columns(r2):
        for b2 in range(q):
            first = (r2 * q + b2) * E
            for n in range(3):
                wcat[b2, :, n * E : (n + 1) * E] = parts[n][:, first : first + E]
            if CW > 3 * E:
                wcat[b2, :, 3 * E : CW] = jnp.zeros((SR, CW - 3 * E), BF16)

    for r2 in range(R):
        pl.when(r == r2)(functools.partial(cut_columns, r2))
    wq[shard_rows(a, b), :] = wcat[b]
    others = S - 1 + A - 1 + len(spread_out) + jnp.where(moves, 1, 0) + jnp.where(apart, 1, 0)
    if by_u:
        others = others + jnp.where(i_carry, 1, 0) + jnp.where(carried_in, 1, 0)
    pl.semaphore_wait(barrier, others)

    for copy in near_rows:
        copy.wait()
    swap_tab = links.copy(ref["tab"], ref["tabs"], home, moves, moves)
    swap_rows, swap_cot = [], []
    for name, there, pieces in (("otok", "tok", swap_rows), ("og", "cot", swap_cot)):
        for h in range(2):
            here = pl.ds(h * HALF, HALF)
            src, dst = ref[name].at[here], ref[there].at[here]
            piece = [links.copy(src, dst, home, direct, direct_in)]
            if by_u:
                lent = ref["lent_" + there].at[here]
                piece.append(links.copy(src, lent, peer(1 - u, c, b), i_cross, i_carry))
                piece.append(links.copy(lent, dst, next_home, i_carry, carried_in))
            pieces.append(piece)

    def swap_begin(pieces):
        for piece in pieces:
            for moved in piece[:2]:
                moved.start()

    def swap_carry(pieces):
        for piece in pieces:
            if by_u:
                piece[1].arrived()
                piece[2].start()

    def swap_end(piece):
        for moved in piece[0::2]:
            moved.arrived()

    def swap_sent(pieces):
        for moved in [m for piece in pieces for m in piece[:2]]:
            moved.sent()
            links.copies.remove(moved)

    def keep_rows():
        for name, there in (("otok", "tok"), ("tab", "tabs"), ("og", "cot")):
            ref[there][...] = ref[name][...]


    def tok_begin():
        swap_tab.start()
        swap_begin(swap_rows)

    event("tok", tok_begin)
    event("coth", lambda: start_all(*[piece[1] for piece in swap_cot if by_u]))
    event("carry", lambda: swap_carry(swap_rows))

    def cot_on():
        start_all(*[piece[0] for piece in swap_cot])
        swap_carry(swap_cot)

    event("cot", cot_on)

    wq_rows = shard_rows
    wcat_b = {}
    for db in range(1, q):
        wcat_b[db] = links.copy(
            wcat.at[b_off[db]], wq.at[wq_rows(a, b)], device(r, a, b_off[db])
        )
    up_q, down_q = {}, {}
    for k in range(A - 1):
        for db in range(q):
            low, high = jnp.maximum(a - k, 0), jnp.minimum(a + k, A - 1)
            slot = wq_rows(low, b_from[db])
            up_q[k, db] = links.copy(
                wq.at[slot], wq.at[slot], above,
                jnp.logical_and(a - k >= 0, a < A - 1), a - 1 - k >= 0,
            )
            slot = wq_rows(high, b_from[db])
            down_q[k, db] = links.copy(
                wq.at[slot], wq.at[slot], below,
                jnp.logical_and(a + k <= A - 1, a > 0), a + 1 + k <= A - 1,
            )

    def wq_begin():
        start_all(*wcat_b.values(), up_q[0, 0], down_q[0, 0])

    def wq_side():
        for db in range(1, q):
            wcat_b[db].arrived()
            start_all(up_q[0, db], down_q[0, db])

    event("wcat", wq_begin)
    event("wcat2", wq_side)
    def wq_pass(k):
        for db in range(q):
            up_q[k, db].arrived()
            down_q[k, db].arrived()
            if k + 1 < A - 1:
                up_q[k + 1, db].start()
                down_q[k + 1, db].start()

    for k in range(A - 1):
        event(f"q{k}", functools.partial(wq_pass, k))

    def piece_rows(a2, b2, u2):
        if H == 1:
            return shard_rows(a2, b2)
        return pl.ds(pl.multiple_of((a2 * q + b2) * SR + u2 * SRH, 16), SRH)

    for copy in own_shards:
        copy.wait()
    pl.when(stays)(keep_rows)

    def b_then_u(u2, w):
        return u2 % 2 != a % 2 if w < 2 else False

    up_w, down_w, side_w, own_w, core_w, core_own = {}, {}, {}, {}, {}, {}
    slots = [sign * k for k in range(1, A) for sign in (1, -1)]
    for w in range(3):
        for k in range(A - 1):
            low, high = jnp.maximum(a - k, 0), jnp.minimum(a + k, A - 1)
            at = w3.at[w, piece_rows(low, b, u), own_half]
            up_w[w, k] = links.copy(
                at, at, above, jnp.logical_and(a - k >= 0, a < A - 1), a - 1 - k >= 0
            )
            at = w3.at[w, piece_rows(high, b, u), own_half]
            down_w[w, k] = links.copy(
                at, at, below, jnp.logical_and(a + k <= A - 1, a > 0), a + 1 + k <= A - 1
            )
        for slot in slots:
            valid = a + slot <= A - 1 if slot > 0 else a + slot >= 0
            a0 = jnp.clip(a + slot, 0, A - 1)
            at = w3.at[w, piece_rows(a0, b, u), own_half]
            for db in range(1, q):
                side_w[w, slot, 0, db] = links.copy(at, at, peer(u, c, b_off[db]), valid, valid)
            if H > 1:
                for du in range(1, U):
                    side_w[w, slot, du, 0] = links.copy(at, at, peer(u_off[du], c, b), valid, valid)
                    for db in range(1, q):
                        sent, came = b_then_u(u, w), b_then_u(u_from[du], w)
                        at = w3.at[w, piece_rows(a0, b_from[db], u), own_half]
                        side_w[w, slot, du, db] = links.copy(
                            at, at, peer(u_off[du], c, b),
                            jnp.logical_and(valid, sent), jnp.logical_and(valid, came),
                        )
                        at = w3.at[w, piece_rows(a0, b, u_from[du]), own_half]
                        other = jnp.logical_and(valid, jnp.logical_not(came))
                        side_w[w, slot, du, -db] = links.copy(
                            at, at, peer(u, c, b_off[db]), other, other
                        )
            at = w3.at[w, pl.ds(pl.multiple_of(a0 * q * SR, 16), q * SR), own_half]
            core_w[w, slot] = links.copy(at, at, sibling, valid, valid)
        for db in range(1, q):
            at = w3.at[w, shard_rows(a, b), own_half]
            own_w[w, db] = links.copy(at, at, peer(u, c, b_off[db]))
            at = w3.at[w, shard_rows(a, b_from[db]), own_half]
            core_own[w, db] = links.copy(at, at, sibling)

    def w3_line(w, k):
        if k < 0:
            up_w[w, 0].start()
            down_w[w, 0].start()
            return
        up_w[w, k].arrived()
        down_w[w, k].arrived()
        if k + 1 < A - 1:
            up_w[w, k + 1].start()
            down_w[w, k + 1].start()
        for slot in (-(k + 1), k + 1):
            for (w2, slot2, du, db), moved in side_w.items():
                if (w2, slot2) == (w, slot) and (du == 0 or db == 0):
                    moved.start()

    def w3_side(w, k):
        if k < 0:
            for db in range(1, q):
                own_w[w, db].arrived()
                core_own[w, db].start()
            return
        for slot in (-(k + 1), k + 1):
            for db in range(1, q):
                side_w[w, slot, 0, db].arrived()
            if H > 1:
                for du in range(1, U):
                    side_w[w, slot, du, 0].arrived()
                    for db in range(1, q):
                        side_w[w, slot, du, db].start()
                        side_w[w, slot, du, -db].start()

    def w3_core(w, k):
        for slot in (-(k + 1), k + 1):
            if H > 1:
                for du in range(1, U):
                    for db in range(1, q):
                        side_w[w, slot, du, db].arrived()
                        side_w[w, slot, du, -db].arrived()
            core_w[w, slot].start()

    event("own", lambda: start_all(*own_w.values()))
    for w in range(3):
        event(f"l{w}", functools.partial(w3_line, w, -1))
        event(f"s{w}", functools.partial(w3_side, w, -1))
        for k in range(A - 1):
            event(f"l{w}{k}", functools.partial(w3_line, w, k))
            event(f"s{w}{k}", functools.partial(w3_side, w, k))
            event(f"c{w}{k}", functools.partial(w3_core, w, k))

    def w3_whole(w):
        for db in range(1, q):
            core_own[w, db].arrived()
        for slot in slots:
            core_w[w, slot].arrived()

    tok, cot, xa = ref["tok"], ref["cot"], ref["xa"]
    gain_attn, gain_ff = gains[0:1, :], gains[1:2, :]
    STEP = 32

    def unit(x):
        return lax.rsqrt(jnp.mean(x * x, axis=-1, keepdims=True) + norm_eps)

    def half_rows(block, h):
        return pl.ds(pl.multiple_of(block * L + h * HALF, HALF), HALF)

    own_x, pass_x, sib_x = {}, {}, {}
    for h in range(2):
        at = xa.at[half_rows(blk, h)]
        for db in range(1, q):
            own_x[h, 0, db] = links.copy(at, at, peer(u, c, b_off[db]))
        for du in range(1, U):
            own_x[h, du, 0] = links.copy(at, at, peer(u_off[du], c, b))
        for du in range(1, U):
            for db in range(1, q):
                if h == 0:
                    at = xa.at[half_rows(block_of(u, c, b_from[db]), h)]
                    pass_x[h, du, db] = links.copy(at, at, peer(u_off[du], c, b))
                else:
                    at = xa.at[half_rows(block_of(u_from[du], c, b), h)]
                    pass_x[h, du, db] = links.copy(at, at, peer(u, c, b_off[db]))
        for du in range(U):
            for db in range(q):
                at = xa.at[half_rows(block_of(u_from[du], c, b_from[db]), h)]
                sib_x[h, du, db] = links.copy(at, at, sibling)

    def norm_half(h):
        swap_end(swap_rows[h])

        def norm_step(i, carried):
            here = pl.ds(pl.multiple_of(h * HALF + i * STEP, STEP), STEP)
            x = tok[here, :].astype(F32)
            there = pl.ds(pl.multiple_of(blk * L + h * HALF + i * STEP, STEP), STEP)
            row = (x * unit(x) * gain_attn).astype(BF16)
            if dims["fits"]:
                xa[there, :] = row
            else:
                ref["x_rows"][here, :] = row
            return carried

        lax.fori_loop(0, HALF // STEP, norm_step, 0)
        if not dims["fits"]:
            here = pl.ds(h * HALF, HALF)
            out_of = local(ref["x_rows"].at[here], xa.at[half_rows(blk, h)], 7)
            out_of.start()
            out_of.wait()
        start_all(*[m for (h2, *_), m in own_x.items() if h2 == h], sib_x[h, 0, 0])

    def rows_on_b(h):
        for db in range(1, q):
            own_x[h, 0, db].arrived()
            if h == 0:
                start_all(*[pass_x[0, du, db] for du in range(1, U)])
            sib_x[h, 0, db].start()

    def rows_on_u(h):
        for du in range(1, U):
            own_x[h, du, 0].arrived()
            if h == 1:
                start_all(*[pass_x[1, du, db] for db in range(1, q)])
            sib_x[h, du, 0].start()

    def rows_passed(h):
        for du in range(1, U):
            for db in range(1, q):
                pass_x[h, du, db].arrived()
                sib_x[h, du, db].start()

    for h in range(2):
        event(f"n{h}", functools.partial(norm_half, h))
        event(f"xb{h}", functools.partial(rows_on_b, h))
        event(f"xu{h}", functools.partial(rows_on_u, h))
        event(f"xp{h}", functools.partial(rows_passed, h))

    tables = {}

    def make_tables():
        swap_tab.arrived()
        lane = lax.broadcasted_iota(jnp.int32, (LABELS, 128), 1)
        row = lax.broadcasted_iota(jnp.int32, (LABELS, 128), 0)
        lengths = jnp.broadcast_to(ref["tabs"][0:1, :], (LABELS, 128))
        seg_start = jnp.sum(jnp.where(lane < row, lengths, 0.0), axis=1, keepdims=True)
        seg_end = jnp.sum(jnp.where(lane <= row, lengths, 0.0), axis=1, keepdims=True)
        lane = lax.broadcasted_iota(jnp.int32, (128, 128), 1)
        row = lax.broadcasted_iota(jnp.int32, (128, 128), 0)
        parents = jnp.broadcast_to(ref["tabs"][1:2, :], (128, 128))
        is_parent = (parents == row.astype(F32)) & (lane > 0) & (lane < segments)
        reach = jnp.where((lane == row) | is_parent, 1.0, 0.0)
        for _ in range(max(1, (segments - 1).bit_length())):
            reach = jnp.minimum(dot(reach.astype(BF16), reach.astype(BF16)), 1.0)
        blocked = ((1.0 - reach[:LABELS, :LABELS]) * masked_score).astype(BF16)
        tables["start"], tables["end"], tables["blocked"] = seg_start, seg_end, blocked

    event("tables", make_tables)

    def turn_wq(i, carried):
        here = pl.ds(pl.multiple_of(i * W, W), W)
        wqt[:, here] = wq[here, :].T
        return carried

    event("turnq", lambda: lax.fori_loop(0, NW, turn_wq, 0))
    bias_col = jnp.transpose(biascat[...])[:, 0:1]
    qgain_col = jnp.transpose(qgain[...])[:, 0:1]
    qkvf, qpre, qt, keys, kt, vals, vt = (
        ref[k] for k in ("qkvf", "qpre", "qt", "keys", "kt", "vals", "vt")
    )

    def project(k, carried):
        for j in range(S):

            def wait_rows(j=j):
                du, db, other = (j // 2) // q, (j // 2) % q, j % 2
                if other:
                    for h in range(2):
                        sib_x[h, du, db].arrived()

            pl.when(k == j)(wait_rows)
        du, db, other = (k // 2) // q, (k // 2) % q, k % 2
        block = block_of((u + U - du) % U, (c + other) % 2, (b + q - db) % q)
        cols = rows_of(block)
        x = near(xa.at[cols], "x_rows", 7)[...]
        qkvf[...] = dot_nt(wqt[...], x) + bias_col
        place = block * L + lax.broadcasted_iota(jnp.int32, (LABELS, L), 1)
        place = place.astype(F32)
        onehot = jnp.where((place >= tables["start"]) & (place < tables["end"]), 1.0, 0.0)
        far = dot(tables["blocked"], onehot.astype(BF16)).astype(BF16)
        for hd in range(HG):
            head = pl.ds(hd * HD, HD)
            pre = qkvf[head, :]
            qpre[head, cols] = pre
            qt[hd, 0:HD, cols] = (pre * qgain_col[hd * HD : (hd + 1) * HD]).astype(BF16)
            qt[hd, HD : HD + LABELS, cols] = far
            qt[hd, HD + LABELS : 128, cols] = jnp.zeros((128 - HD - LABELS, L), BF16)
            key = qkvf[pl.ds(E + hd * HD, HD), :]
            kt[hd, :, cols] = key.astype(BF16)
            wide = jnp.concatenate([key, onehot, jnp.zeros((128 - HD - LABELS, L), F32)], axis=0)
            keys[hd, cols, :] = wide.T.astype(BF16)
            value = qkvf[pl.ds(2 * E + hd * HD, HD), :]
            vt[hd, :, cols] = value.astype(BF16)
            wide = jnp.concatenate([value, jnp.zeros((128 - HD, L), F32)], axis=0)
            vals[hd, cols, :] = wide.T.astype(BF16)
        return carried

    event("project", lambda: lax.fori_loop(0, S, project, 0))

    ot, otb, lse, oa = ref["ot"], ref["otb"], ref["lse"], ref["oa"]
    first_o = links.block(S)
    o_slot = pl.ds(pl.multiple_of(g * E, 16), E)

    def o_copy(block):
        r2, b2 = place_of(block // q, a), block % q
        index = first_o + (r2 * q + b2 + S - g) % S
        return links.copy(
            otb.at[:, rows_of(block)], oa.at[o_slot], device(r2, a, b2), index=index, keep=False
        )

    PAIR = 2
    SQ = PAIR * L
    diagonal = lax.broadcasted_iota(jnp.int32, (SQ, SQ), 0) <= lax.broadcasted_iota(
        jnp.int32, (SQ, SQ), 1
    )
    def wide_rows(i):
        return pl.ds(pl.multiple_of(i * SQ, SQ), SQ)

    def attend(i, carried):
        cols = wide_rows(i)
        query = [qt[hd, :, cols] for hd in range(HG)]

        def key_block(j, state, on_diagonal):
            here = wide_rows(j)
            result = []
            for hd in range(HG):
                top, total, acc = state[hd]
                score = dot(keys[hd, here, :], query[hd])
                if on_diagonal:
                    score = jnp.where(diagonal, score, masked_score)
                new_top = jnp.maximum(top, jnp.max(score, axis=0, keepdims=True))
                p = jnp.exp(score - new_top)
                fade = jnp.exp(top - new_top)
                total = total * fade + jnp.sum(p, axis=0, keepdims=True)
                acc = acc * fade + dot(vt[hd, :, here], p.astype(BF16))
                result.append((new_top, total, acc))
            return tuple(result)

        start = tuple(
            (
                jnp.full((1, SQ), masked_score, F32),
                jnp.zeros((1, SQ), F32),
                jnp.zeros((HD, SQ), F32),
            )
            for _ in range(HG)
        )
        state = lax.fori_loop(0, i, functools.partial(key_block, on_diagonal=False), start)
        state = key_block(i, state, True)
        for hd in range(HG):
            top, total, acc = state[hd]
            mixed = acc / total
            head = pl.ds(hd * HD, HD)
            ot[head, cols] = mixed
            otb[head, cols] = mixed.astype(BF16)
            lse[hd, :, cols] = jnp.broadcast_to(top + jnp.log(total), (8, SQ))
        for k in range(PAIR):
            block = i * PAIR + k

            def keep_block(block=block):
                oa[o_slot, :] = otb[:, rows_of(block)]

            pl.when(block == blk)(keep_block)
            pl.when(block != blk)(lambda block=block: o_copy(block).start())
        for j in range(S // PAIR):
            if order.get(f"A{j}"):
                pl.when(i == j)(functools.partial(play, order[f"A{j}"]))
        return carried

    def o_arrived(k, carried):
        links.copy(
            otb.at[:, rows_of(0)], oa.at[o_slot], sibling, index=first_o + k, keep=False
        ).make().wait_recv()
        return carried

    event("owait", lambda: lax.fori_loop(1, S, o_arrived, 0))

    names = [name for name in FIRST if name in events or name[0] in "AF"]
    for k in range(A - 1):
        for at, name in [("turnq", f"q{k}")] + [
            (f"F{w}", f"{kind}{w}{k}") for w in range(3) for kind in "lsc"
        ]:
            if name not in names:
                names.insert(names.index(at), name)
    ff_order = segments_of(names, "F", "FX")
    order = segments_of(ff_order.pop(None), "A", "AX")
    play(order[None])
    lax.fori_loop(0, S // PAIR, attend, 0)
    play(order["AX"])
    def o_sent(i, carried):
        pl.when(i != blk)(lambda: o_copy(i).sent())
        return carried

    otok, mid, ffin, up, hid, outb = (ref[k] for k in ("otok", "mid", "ffin", "up", "hid", "outb"))
    ug, fg, mg, og, mgt = (ref[k] for k in ("ug", "fg", "mg", "og", "mgt"))
    small = ref["small"]

    def tile(n):
        return pl.ds(pl.multiple_of(n * W, W), W)

    def turn_o(n, carried):
        otok[:, tile(n)] = oa[tile(n), :].T
        return carried

    swap_sent(swap_rows)
    lax.fori_loop(0, NW, turn_o, 0)
    play(ff_order["F0"])
    w3_whole(0)

    def out_step(n, carried):
        added = dot(otok[...], w3[0, :, tile(n)]) + gains[2:3, tile(n)]
        mid[:, tile(n)] = tok[:, tile(n)].astype(F32) + added
        return carried

    lax.fori_loop(0, NW, out_step, 0)

    def strip(i):
        return pl.ds(pl.multiple_of(i * STEP, STEP), STEP)

    def ff_norm(i, carried):
        x = mid[strip(i), :]
        ffin[strip(i), :] = (x * unit(x) * gain_ff).astype(BF16)
        return carried

    lax.fori_loop(0, L // STEP, ff_norm, 0)
    play(ff_order["F1"])
    w3_whole(1)

    def up_step(n, carried):
        pre = dot(ffin[...], w3[1, :, tile(n)]) + gains[3:4, tile(n)]
        up[:, tile(n)] = pre
        hid[:, tile(n)] = (pre * jax.nn.sigmoid(pre)).astype(BF16)
        return carried

    lax.fori_loop(0, NW, up_step, 0)
    play(ff_order["F2"])
    w3_whole(2)

    def down_step(n, carried):
        added = dot(hid[...], w3[2, :, tile(n)]) + gains[4:5, tile(n)]
        outb[:, tile(n)] = (mid[:, tile(n)] + added).astype(BF16)
        return carried

    lax.fori_loop(0, NW, down_step, 0)
    back_out = links.copy(outb, ref["out"], origin, moves, moves)
    back_out.start()

    def keep_out():
        kept = local(outb, ref["out"], 0)
        kept.start()
        kept.wait()

    pl.when(stays)(keep_out)
    for piece in swap_cot:
        swap_end(piece)
    swap_sent(swap_cot)
    small[...] = jnp.zeros_like(small)

    def up_back(n, carried):
        pre = up[:, tile(n)]
        gate = jax.nn.sigmoid(pre)
        grad = dot_nt(cot[...], w3[2, tile(n), :]) * gate * (1.0 + pre * (1.0 - gate))
        grad = grad.astype(BF16)
        ug[:, tile(n)] = grad
        small[3:4, tile(n)] = jnp.sum(grad.astype(F32), axis=0, keepdims=True)
        return carried

    lax.fori_loop(0, NW, up_back, 0)

    def ff_back(n, carried):
        fg[:, tile(n)] = dot_nt(ug[...], w3[1, tile(n), :])
        return carried

    lax.fori_loop(0, NW, ff_back, 0)

    def mid_back(i, carried):
        x, grad, above_grad = mid[strip(i), :], fg[strip(i), :], cot[strip(i), :].astype(F32)
        inverse = unit(x)
        normed = x * inverse
        small[1:2, :] += jnp.sum(grad * normed, axis=0, keepdims=True)
        scaled = grad * gain_ff
        mean = jnp.mean(scaled * normed, axis=-1, keepdims=True)
        total = above_grad + inverse * (scaled - normed * mean)
        mg[strip(i), :] = total
        rounded = total.astype(BF16)
        og[strip(i), :] = rounded
        small[2:3, :] += jnp.sum(rounded.astype(F32), axis=0, keepdims=True)
        small[4:5, :] += jnp.sum(above_grad, axis=0, keepdims=True)
        return carried

    lax.fori_loop(0, L // STEP, mid_back, 0)

    dot_t = ref["dot_t"]
    first_m = links.block(S)

    def m_copy(k):
        g2 = (g + k) % S
        at = pl.ds(pl.multiple_of(g2 * E, 16), E)
        return links.copy(
            mgt.at[at], dot_t.at[:, rows_of(blk)], device(g2 // q, a, g2 % q),
            index=first_m + k, keep=False,
        )

    def mixed_step(k, carried):
        at = pl.ds(pl.multiple_of(((g + k) % S) * E, 16), E)
        mgt[at, :] = dot_nt(w3[0, at, :], og[...]).astype(BF16)
        pl.when(k < S)(lambda: m_copy(k).start())
        return carried

    lax.fori_loop(1, S + 1, mixed_step, 0)
    dot_t[:, rows_of(blk)] = mgt[pl.ds(pl.multiple_of(g * E, 16), E), :]

    freed, freed_again = ref["freed"], ref["freed_again"]
    writers = [sibling] + [peer(u, c, v) for v in b_off[1:]] + [peer(v, c, b) for v in u_off[1:]]

    def release(sem):
        for where in writers:
            pl.semaphore_signal(sem, inc=1, device_id=where, device_id_type=MESH)

    for group in (wcat_b, up_w, down_w, side_w, own_w, core_w, core_own):
        for moved in group.values():
            moved.sent()
            links.copies.remove(moved)
    release(freed)

    gp, rc = ref["gp"], ref["rc"]
    rcin = [w3.at[0, :, 0:DH], w3.at[0, :, DH:D], w3.at[1, :, 0:DH]]
    core_g = [links.copy(gp.at[w], rcin[w], sibling) for w in range(3)]

    def weight_grad(w, left, right):
        if left is not None:

            def turn(n, carried):
                oa[tile(n), :] = left[:, tile(n)].T
                return carried

            lax.fori_loop(0, NW, turn, 0)

        def step(n, carried):
            here = pl.ds(pl.multiple_of(n * SR, 16), SR)
            side = oa[here, :]
            gp[w, here, :] = dot(side, right[:, other_half]).astype(BF16)
            rc[w, n // q, n % q] = dot(side, right[:, own_half]).astype(BF16)
            return carried

        lax.fori_loop(0, S, step, 0)

    def m_arrived(k, carried):
        m_copy(k).arrived()
        return carried

    A2 = A // 2
    u_rows = [pl.ds(pl.multiple_of(v * SRH, 16), SRH) for v in u_off]
    my_rows = u_rows[0]
    qm, um = q - 1, U - 1

    def t1b(w, db, a2):
        at = D - 3 * qm * A2 * SR + ((w * qm + db - 1) * A2 + a2) * SR
        assert at >= 0
        return w3.at[1, at : at + SR, DH:D]

    def t1u(w, du, a2, b2):
        at = (((w * um + du - 1) * A2 + a2) * q + b2) * SRH
        assert at + SRH <= D
        return w3.at[2, at : at + SRH, 0:DH]

    def t2b(w, db, a2):
        at = ((w * qm + db - 1) * A2 + a2) * SRH
        return w3.at[2, at : at + SRH, DH:D]

    def t2u(w, du, a2):
        at = (3 * qm * A2 + (w * um + du - 1) * A2 + a2) * SRH
        assert at + SRH <= D
        return w3.at[2, at : at + SRH, DH:D]

    first_b, first_u, second_b, second_u = {}, {}, {}, {}
    for w in range(3):
        for a2 in range(A2):
            for db in range(1, q):
                to = peer(u, c, b_off[db])
                first_b[w, db, a2] = links.copy(rc.at[w, a2, b_off[db]], t1b(w, db, a2), to)
                second_b[w, db, a2] = links.copy(
                    rc.at[w, A2 + a2, b_off[db], my_rows], t2b(w, db, a2), to
                )
            if H > 1:
                for du in range(1, U):
                    to = peer(u_off[du], c, b)
                    for b2 in range(q):
                        first_u[w, du, a2, b2] = links.copy(
                            rc.at[w, A2 + a2, b2, u_rows[du]], t1u(w, du, a2, b2), to
                        )
                    second_u[w, du, a2] = links.copy(
                        rc.at[w, a2, b, u_rows[du]], t2u(w, du, a2), to
                    )

    def add_into(target, *more):
        total = target[...].astype(F32)
        for other in more:
            total = total + other[...].astype(F32)
        target[...] = total.astype(BF16)

    def core_sum(w):
        core_g[w].arrived()

        def step(n, carried):
            a2, b2 = n // q, n % q
            here = pl.ds(pl.multiple_of(n * SR, 16), SR)
            add_into(rc.at[w, a2, b2], rcin[w].at[here])
            return carried

        lax.fori_loop(0, S, step, 0)
        for key, moved in list(first_b.items()) + list(first_u.items()):
            if key[0] == w:
                moved.start()

    def side_sum_1(w):
        for db in range(1, q):
            for a2 in range(A2):
                first_b[w, db, a2].arrived()
                add_into(rc.at[w, a2, b], t1b(w, db, a2))
        if H > 1:
            for du in range(1, U):
                for a2 in range(A2):
                    for b2 in range(q):
                        first_u[w, du, a2, b2].arrived()
                        add_into(rc.at[w, A2 + a2, b2, my_rows], t1u(w, du, a2, b2))
        for key, moved in list(second_b.items()) + list(second_u.items()):
            if key[0] == w:
                moved.start()

    def side_sum_2(w):
        for db in range(1, q):
            for a2 in range(A2):
                second_b[w, db, a2].arrived()
                add_into(rc.at[w, A2 + a2, b, my_rows], t2b(w, db, a2))
        if H > 1:
            for du in range(1, U):
                for a2 in range(A2):
                    second_u[w, du, a2].arrived()
                    add_into(rc.at[w, a2, b, my_rows], t2u(w, du, a2))

    def first_grad():
        weight_grad(0, None, og)
        pl.semaphore_wait(freed, len(writers))
        core_g[0].start()

    def next_grad(w, left, right):
        weight_grad(w, left, right)
        core_g[w].start()

    event("wg0", first_grad)
    event("wg1", lambda: next_grad(1, ffin, ug))
    event("wg2", lambda: next_grad(2, hid, cot))
    event("release", lambda: release(freed_again))
    event("mwait", lambda: lax.fori_loop(1, S, m_arrived, 0))
    for w in range(3):
        event(f"cs{w}", functools.partial(core_sum, w))
        event(f"f{w}", functools.partial(side_sum_1, w))

    assert A & (A - 1) == 0
    strides = [1 << n for n in range(A.bit_length() - 1)]

    def across(k):
        return a + k - 2 * k * (a // k % 2)

    class Line:
        def __init__(self, part, landed, near_name):
            self.part, self.landed, self.near_name, self.steps = part, landed, near_name, []
            slot = 0
            for k in strides:
                step = []
                for m in range(A // (2 * k)):
                    mine = a % (2 * k) + 2 * k * m
                    theirs = across(k) % (2 * k) + 2 * k * m
                    copy = links.copy(part(theirs), landed(slot), device(r, across(k), b))
                    step.append((copy, mine, slot))
                    slot += 1
                self.steps.append(step)

        def begin(self, n=0):
            for copy, _, _ in self.steps[n]:
                copy.start()

        def step(self, n):
            for copy, mine, slot in self.steps[n]:
                copy.arrived()
                add_into(self.part(mine), near(self.landed(slot), self.near_name, 7))
            if n + 1 < len(self.steps):
                self.begin(n + 1)

    cu = ref["cu"]
    lines = []
    for w in range(3):
        lines.append(
            Line(
                lambda d, w=w: rc.at[w, d, b, my_rows],
                lambda slot, w=w: cu.at[slot, w],
                "c_rows",
            )
        )

    def line_begin(w):
        side_sum_2(w)
        lines[w].begin()

    for w in range(3):
        event(f"g{w}", functools.partial(line_begin, w))
        event(f"h{w}0", functools.partial(lines[w].step, 0))

    delta, dqt, dqkvt = ref["delta"], ref["dqt"], ref["dqkvt"]
    def make_delta():
        for hd in range(HG):
            head = slice(hd * HD, (hd + 1) * HD)
            total = jnp.sum(dot_t[head, :].astype(F32) * ot[head, :], axis=0, keepdims=True)
            delta[hd, :, :] = jnp.broadcast_to(total, (8, T))
        dqt[...] = jnp.zeros_like(dqt)

    event("delta", make_delta)
    NB = S // PAIR
    starts = [sum(NB - k for k in range(j)) for j in range(NB)]
    pairs = NB * (NB + 1) // 2
    dkt, dvt = ref["dkt"], ref["dvt"]

    def attend_back(n, carried):
        j = sum(jnp.where(n >= start, 1, 0) for start in starts[1:])
        start = sum(jnp.where(n >= starts[k], starts[k] - starts[k - 1], 0) for k in range(1, NB))
        i = n - start + j
        here, cols = wide_rows(j), wide_rows(i)

        def block(on_diagonal):
            for hd in range(HG):
                head = pl.ds(hd * HD, HD)
                score = dot(keys[hd, here, :], qt[hd, :, cols])
                if on_diagonal:
                    score = jnp.where(diagonal, score, masked_score)
                p = jnp.exp(score - lse[hd, 0:1, cols])
                d_out = dot_t[head, cols]
                dp = dot(vals[hd, here, 0:HD], d_out)
                ds = (p * (dp - delta[hd, 0:1, cols])).astype(BF16)
                dv = dot_nt(d_out, p.astype(BF16))
                dk = dot_nt(qt[hd, 0:HD, cols], ds)
                if on_diagonal:
                    dvt[head, :], dkt[head, :] = dv, dk
                else:
                    dvt[head, :] += dv
                    dkt[head, :] += dk
                dqt[head, cols] += dot(kt[hd, :, here], ds)

        pl.when(i == j)(lambda: block(True))
        pl.when(i != j)(lambda: block(False))

        def keep():
            dqkvt[E : 2 * E, here] = dkt[...].astype(BF16)
            dqkvt[2 * E : 3 * E, here] = dvt[...].astype(BF16)

        pl.when(i == NB - 1)(keep)
        for m in range(pairs):
            if back_order.get(f"B{m}"):
                pl.when(n == m)(functools.partial(play, back_order[f"B{m}"]))
        return carried

    names = [name for name in SECOND if name in events or name[0] == "B"]
    first_part = names[: names.index("BX")]
    back_order = segments_of(first_part, "B", "BX")
    play(back_order[None])
    lax.fori_loop(0, pairs, attend_back, 0)
    if CW > 3 * E:
        dqkvt[3 * E :, :] = jnp.zeros((CW - 3 * E, T), BF16)

    def query_part(i, carried):
        cols = rows_of(i)
        dqkvt[0:E, cols] = (dqt[:, cols] * qgain_col[0:E]).astype(BF16)
        return carried + jnp.sum(dqt[:, cols] * qpre[:, cols], axis=1, keepdims=True)

    scale_terms = lax.fori_loop(0, S, query_part, jnp.zeros((E, 1), F32))

    gq, cqu, gall = ref["gq"], ref["cqu"], ref["gall"]

    def qkv_grad(n, carried):
        gq[tile(n), :] = dot(dqkvt[...], near(xa.at[:, tile(n)], "x_cols", 7)[...]).T.astype(BF16)
        return carried

    QR = q * SR
    line_q = Line(
        lambda d: gq.at[pl.ds(pl.multiple_of(d * QR, 16), QR)],
        lambda slot: cqu.at[slot],
        "q_rows",
    )

    def q_grads():
        lax.fori_loop(0, NW, qkv_grad, 0)
        line_q.begin()

    def q_last():
        for n in range(1, len(strides)):
            line_q.step(n)
        own_q()

    event("qg", q_grads)
    event("Q0", lambda: line_q.step(0))
    event("Q1", q_last)
    sums, landed, late, late_landed = (ref[k] for k in ("sums", "landed", "late", "late_landed"))

    class Total:
        def __init__(self, held, arrivals, stages):
            self.held, self.arrivals, self.stages, count = held, arrivals, [], 0
            for n, stage in enumerate(stages):
                moves_n = []
                for to in stage:
                    copy = links.copy(held.at[n], arrivals.at[count], to)
                    moves_n.append((copy, count))
                    count += 1
                self.stages.append(moves_n)

        def begin(self, n):
            for moved, _ in self.stages[n]:
                moved.start()

        def end(self, n):
            total = self.held[n]
            for moved, at in self.stages[n]:
                moved.arrived()
                total = total + self.arrivals[at]
            self.held[n + 1] = total

    on_b = [peer(u, c, b_off[db]) for db in range(1, q)]
    on_u = [peer(u_off[du], c, b) for du in range(1, U)]
    on_a = [[device(r, across(k), b)] for k in strides]
    total = Total(sums, landed, on_a + [on_b, on_u, [sibling]])
    line_all = [device(r, (a + k) % A, b) for k in range(1, A)]
    wide_u = [device(u2 * 2 + c, (a + k) % A, b) for u2 in u_off for k in range(A)][1:]
    late_stages = [wide_u] if U * A <= 16 else [line_all, on_u]
    late_total = Total(late, late_landed, late_stages + [on_b, [sibling]])

    def late_step(n):
        late_total.end(n)
        if n + 1 < len(late_total.stages):
            late_total.begin(n + 1)


    def total_begin():
        ones = jnp.ones((8, T), BF16)
        head_sums = dot_nt(ones, dqkvt[...])
        small[pl.ds(8 + g, 1), 0:CW] = head_sums[0:1]
        small[5:6, 0:E] = jnp.transpose(jnp.broadcast_to(scale_terms, (E, 128)))[0:1, :]
        sums[0] = small[...]
        total.begin(0)

    def total_step(n):
        total.end(n)
        if n + 1 < len(total.stages):
            total.begin(n + 1)

    event("t", total_begin)
    for n in range(len(total.stages)):
        event(f"t{n}", functools.partial(total_step, n))
    for n in range(len(late_total.stages)):
        event(f"L{n}", functools.partial(late_step, n))

    ags, arc = ref["ags"], ref["arc"]

    def slot_of(n, rows):
        page, row = divmod(n * HALF, D)
        return w3.at[page, row : row + rows]

    order = [(u2, b2) for u2 in range(U) for b2 in range(q)]
    taken = {0: 0, 1: 0, 2: 0}
    if H > 1:
        taken[2] = 3 * um * A2 * q * SRH
    usable = [
        n
        for n in range(2 * U * q, 3 * D // HALF)
        if n * HALF % D >= taken[n * HALF // D]
        and (n * HALF // D != 1 or n * HALF % D + HALF <= D - 3 * qm * A2 * SR)
    ]
    core_a = {}
    for n, (u2, b2) in enumerate(order):
        core_a[u2, b2] = links.copy(ags.at[pl.ds(n * L, L)], slot_of(2 * n, L), sibling)
    dtok = ref["dtok"]

    def partial_rows(m, carried, others):
        block = block_of(m // q, 1 - c if others else c, m % q)
        dtok[...] = dqkvt[:, rows_of(block)].T
        for k in range(NW):
            at = slice(k * W, (k + 1) * W)
            part = dot_nt(dtok[...], wq[at, :]).astype(BF16)
            target = ags if others else arc
            target[rows_of(m), at] = part
        if others:
            for j, key in enumerate(order):
                pl.when(m == j)(core_a[key].start)
        return carried

    def partial_others():
        for group in (own_x, pass_x, sib_x):
            for moved in group.values():
                moved.sent()
                links.copies.remove(moved)
        pl.semaphore_wait(freed_again, len(writers))
        lax.fori_loop(0, U * q, functools.partial(partial_rows, others=True), 0)

    event("ago", partial_others)
    event("agm", lambda: lax.fori_loop(0, U * q, functools.partial(partial_rows, others=False), 0))


    def part(u2, b2, h):
        return arc.at[half_rows(u2 * q + b2, h)]

    afb, afu, asb, asu, landing = {}, {}, {}, {}, {}

    def land(key):
        landing[key] = slot_of(usable.pop(0), HALF)
        return landing[key]

    for db in range(1, q):
        to = peer(u, c, b_off[db])
        for u2 in range(U):
            afb[db, u2] = links.copy(part(u2, b_off[db], 0), land(("fb", db, u2)), to)
        asb[db] = links.copy(part(u, b_off[db], 1), land(("sb", db)), to)
    for du in range(1, U):
        to = peer(u_off[du], c, b)
        for b2 in range(q):
            afu[du, b2] = links.copy(part(u_off[du], b2, 1), land(("fu", du, b2)), to)
        asu[du] = links.copy(part(u_off[du], b, 0), land(("su", du)), to)

    def add_rows(target, other, count):
        def step(i, carried):
            add_into(target.at[strip(i)], other.at[strip(i)])
            return carried

        lax.fori_loop(0, count // STEP, step, 0)

    def rows_core():
        for u2, b2 in order:
            core_a[u2, b2].arrived()
            add_rows(arc.at[rows_of(u2 * q + b2)], slot_of(2 * order.index((u2, b2)), L), L)
        start_all(*afb.values(), *afu.values())

    def rows_on_b_1():
        for db in range(1, q):
            for u2 in range(U):
                afb[db, u2].arrived()
                add_rows(part(u2, b, 0), landing["fb", db, u2], HALF)
        start_all(*asu.values())

    def rows_on_u_1():
        for du in range(1, U):
            for b2 in range(q):
                afu[du, b2].arrived()
                add_rows(part(u, b2, 1), landing["fu", du, b2], HALF)
        start_all(*asb.values())

    event("ac", rows_core)
    event("ab", rows_on_b_1)
    event("au", rows_on_u_1)

    wide, q_across, q_core = {}, [], []
    for db in range(1, q):
        at = gq.at[pl.ds(pl.multiple_of(a * QR + b_off[db] * SR, 16), SR)]
        wide[db] = links.copy(at, gall.at[g], device(r, a, b_off[db]))
    here = pl.ds(r * q, q)
    for du in range(1, U):
        q_across.append(links.copy(gall.at[here], gall.at[here], peer(u_off[du], c, b)))
    for du in range(U):
        here = pl.ds((u_from[du] * 2 + c) * q, q)
        q_core.append(links.copy(gall.at[here], gall.at[here], sibling))

    def own_q():
        for db in range(1, q):
            wide[db].start()
        gall[g] = gq[pl.ds(pl.multiple_of(a * QR + b * SR, 16), SR), :]

    def across_q():
        for db in range(1, q):
            wide[db].arrived()
        for moved in q_across:
            moved.start()
        q_core[0].start()

    def core_q():
        for du in range(1, U):
            q_across[du - 1].arrived()
            q_core[du].start()

    event("Q2", across_q)
    event("Q3", core_q)

    go = ref["go"]
    spread, core_go, partials = {}, {}, {}
    for w in range(3):
        piece = rc.at[w, a, b, my_rows]
        for du in range(1, U):
            to = peer(u_off[du], c, b)
            if H > 1:
                spread[w, du] = links.copy(piece, go.at[w, my_rows, own_half], to)
            else:
                partials[w, du] = links.copy(piece, ref["ru"].at[du - 1, w], to)
        at = go.at[w, :, own_half]
        core_go[w] = links.copy(at, at, sibling)

    def own_go(w):
        for (w2, du), moved in partials.items():
            if w2 == w:
                moved.start()
        for (w2, du), moved in partials.items():
            if w2 == w:
                moved.arrived()
                moved.sent()
                links.copies.remove(moved)
        for (w2, du), moved in partials.items():
            if w2 == w:
                add_into(rc.at[w, a, b, my_rows], near(ref["ru"].at[du - 1, w], "c_rows", 7))
        for (w2, du), moved in spread.items():
            if w2 == w:
                moved.start()
        go[w, my_rows, own_half] = rc[w, a, b, my_rows]

    def last_lines(w):
        for n in range(1, len(strides)):
            lines[w].step(n)
        own_go(w)

    def core_go_on(w):
        for (w2, du), moved in spread.items():
            if w2 == w:
                moved.arrived()
        core_go[w].start()

    for w in range(3):
        event(f"h{w}1", functools.partial(last_lines, w))
        event(f"k{w}", functools.partial(core_go_on, w))

    def rows_end():
        for db in range(1, q):
            asb[db].arrived()
            add_rows(part(u, b, 1), landing["sb", db], HALF)
        for du in range(1, U):
            asu[du].arrived()
            add_rows(part(u, b, 0), landing["su", du], HALF)
        small[0:1, :] = jnp.zeros((1, D), F32)
        lax.fori_loop(0, L // STEP, tok_back, 0)
        late[0] = small[0:1, :]
        late_total.begin(0)
        back_tok.start()
        pl.when(stays)(keep_tok)

    def tok_back(i, carried):
        x = tok[strip(i), :].astype(F32)
        grad = arc[pl.ds(pl.multiple_of((u * q + b) * L + i * STEP, STEP), STEP), :].astype(F32)
        inverse = unit(x)
        normed = x * inverse
        small[0:1, :] += jnp.sum(grad * normed, axis=0, keepdims=True)
        scaled = grad * gain_attn
        mean = jnp.mean(scaled * normed, axis=-1, keepdims=True)
        ref["gtb"][strip(i), :] = (mg[strip(i), :] + inverse * (scaled - normed * mean)).astype(BF16)
        return carried

    back_tok = links.copy(ref["gtb"], ref["gtok"], origin, moves, moves)

    def keep_tok():
        kept = local(ref["gtb"], ref["gtok"], 0)
        kept.start()
        kept.wait()

    event("end", rows_end)
    names = [name for name in SECOND[SECOND.index("BX") + 1 :] if name in events]
    play(names + [name for name in events if name not in names])
    ref["g_small"][...] = sums[len(total.stages)]
    ref["g_small"][0:1, :] = late[len(late_total.stages)]
    for w in range(3):
        core_go[w].arrived()
    for moved in q_core:
        moved.arrived()
    back_out.arrived()
    back_tok.arrived()

    lax.fori_loop(0, S, o_sent, 0)

    def m_sent(k, carried):
        m_copy(k).sent()
        return carried

    lax.fori_loop(1, S, m_sent, 0)
    for moved in links.copies:
        moved.sent()
    return links.used


def shards(
    R,
    S,
    tokens,
    lengths,
    parents,
    w_query,
    w_key,
    w_value,
    w_out,
    w_up,
    w_down,
    gain_attn,
    gain_ff,
    query_scale,
    bias_query,
    bias_value,
    bias_out,
    bias_up,
    bias_down,
    cotangent,
):
    L, D = tokens.shape
    SR = w_query.shape[0]
    HG = HEADS // S
    E = HG * HEAD_DIM
    CW = -(-3 * E // 128) * 128
    q, U, A, T = S // R, R // 2, R, S * L
    H = U if SR % (16 * U) == 0 else 1
    SRH = SR // H
    DH = D // 2
    NS = 8 + S
    segments = lengths.shape[1]
    dims = dict(R=R, S=S, L=L, D=D, HG=HG, E=E, CW=CW, SR=SR, H=H, SRH=SRH, segments=segments)

    operands = dict(
        tokens=tokens, cotangent=cotangent, w_query=w_query, w_key=w_key, w_value=w_value,
        w_out=w_out, w_up=w_up, w_down=w_down, lengths=lengths, parents=parents,
        gain_attn=gain_attn, gain_ff=gain_ff, query_scale=query_scale, bias_query=bias_query,
        bias_value=bias_value, bias_out=bias_out, bias_up=bias_up, bias_down=bias_down,
    )
    outputs = dict(
        out=((L, D), BF16), gtok=((L, D), BF16), go=((3, SR, D), BF16),
        gall=((S, SR, CW), BF16), g_small=((NS, D), F32),
    )
    um = max(U - 1, 1)
    peers = q + U + A + (U * A if U * A <= 16 else 0)
    line_steps = A.bit_length() - 1
    scratch = dict(
        tok=((L, D), BF16), cot=((L, D), BF16), tabs=((8, 128), F32),
        wq=((D, CW), BF16), w3=((3, D, D), BF16), xa=((T, D), BF16),
        qkvf=((CW, L), F32), qpre=((E, T), F32), qt=((HG, 128, T), BF16),
        keys=((HG, T, 128), BF16), kt=((HG, HEAD_DIM, T), BF16),
        vals=((HG, T, 128), BF16), vt=((HG, HEAD_DIM, T), BF16),
        ot=((E, T), F32), otb=((E, T), BF16), lse=((HG, 8, T), F32), oa=((D, L), BF16),
        otok=((L, D), BF16), mid=((L, D), F32), ffin=((L, D), BF16), up=((L, D), F32),
        hid=((L, D), BF16), outb=((L, D), BF16),
        mg=((L, D), F32), og=((L, D), BF16), mgt=((D, L), BF16), dot_t=((E, T), BF16),
        small=((NS, D), F32), gp=((3, D, DH), BF16),
        rc=((3, A, q, SR, DH), BF16),
        cu=((A - 1, 3, SRH, DH), BF16), delta=((HG, 8, T), F32), dqkvt=((CW, T), BF16),
        dkt=((E, 2 * L), F32), dvt=((E, 2 * L), F32),
        gains=((8, D), F32), biascat=((8, CW), F32), qgain=((8, CW), F32), tab=((8, 128), F32),
        ags=((T // 2, D), BF16), arc=((T // 2, D), BF16),
        dtok=((L, CW), BF16),
        gq=((D, CW), BF16), cqu=((A - 1, q * SR, CW), BF16),
        sums=((line_steps + 4, NS, D), F32), landed=((line_steps + q + U, NS, D), F32),
        late=((5, 1, D), F32), late_landed=((peers, 1, D), F32),
    )
    if H == 1:
        scratch["ru"] = ((um, 3, SR, DH), BF16)
    held = [jax.ShapeDtypeStruct(*v) for k, v in scratch.items() if k not in ("ags", "arc")]
    dims["fits"] = sum(v.size * v.dtype.itemsize for v in held) <= VMEM_BYTES - (6 << 20)
    results = len(outputs)
    distant = ["out", "gtok"]
    if dims["fits"]:
        scratch.pop("ags")
        scratch.pop("arc")
    else:
        for name in [k for k in ("xa", "cu", "ru") if k in scratch]:
            outputs[name] = scratch.pop(name)
            distant.append(name)
        scratch["x_rows"] = ((L, D), BF16)
        scratch["x_cols"] = ((T, 256), BF16)
        scratch["c_rows"] = ((SRH, DH), BF16)
    if U == 2:
        scratch["lent_tok"] = scratch["lent_cot"] = ((L, D), BF16)
    names = list(operands) + list(outputs) + list(scratch)
    names += ["send_sems", "recv_sems", "local_sems", "freed", "freed_again"]

    counted = [1024]

    def kernel(*refs):
        named = dict(zip(names, refs))
        for later, earlier in (("fg", "up"), ("dqt", "ot"), ("ug", "otok"), ("gtb", "ffin")):
            named[later] = named[earlier]
        named["wqt"] = named["dqkvt"].at[:, 0:D]
        if dims["fits"]:
            named["ags"] = named["xa"].at[pl.ds(0, T // 2)]
            named["arc"] = named["xa"].at[pl.ds(T // 2, T // 2)]
        counted[0] = layer_kernel(dims, named)

    whole = pl.BlockSpec(memory_space=pltpu.VMEM)
    far = ("tokens", "cotangent", "w_query", "w_key", "w_value", "w_out", "w_up", "w_down")
    def call(*operands):
        return pl.pallas_call(
        kernel,
        out_shape=[jax.ShapeDtypeStruct(*shape) for shape in outputs.values()],
        in_specs=[pl.BlockSpec(memory_space=pl.ANY) if k in far else whole for k in operands],
        out_specs=[pl.BlockSpec(memory_space=pl.ANY) if k in distant else whole for k in outputs],
        scratch_shapes=[pltpu.VMEM(*shape) for shape in scratch.values()]
        + [pltpu.SemaphoreType.DMA((counted[0],))] * 2
        + [pltpu.SemaphoreType.DMA((8,))]
        + [pltpu.SemaphoreType.REGULAR] * 2,
        compiler_params=pltpu.CompilerParams(
            collective_id=0, has_side_effects=True, vmem_limit_bytes=VMEM_BYTES
        ),
    )(*operands)

    jax.eval_shape(call, *operands.values())
    made = call(*operands.values())
    out, gtok, go, gall, g_small = made[:results]

    def finish(out, gtok, go, gall, sums, scale, *refs):
        made_out, made_gtok, grads, vectors = refs[0], refs[1], refs[2:8], refs[8:16]
        made_out[...] = out[...]
        made_gtok[...] = gtok[...]
        for g2 in range(S):
            mine = gall[g2]
            for n in range(3):
                grads[n][:, g2 * E : (g2 + 1) * E] = mine[:, n * E : (n + 1) * E].astype(F32)
        for w in range(3):
            grads[3 + w][...] = go[w].astype(F32)
        for n, at in ((0, 0), (1, 1), (5, 2), (6, 3), (7, 4)):
            vectors[n][...] = sums[at : at + 1, :].reshape(D)
        for n, at in ((3, 0), (4, 2 * E)):
            whole = jnp.concatenate([sums[8 + k : 9 + k, at : at + E] for k in range(S)], axis=1)
            vectors[n][...] = whole.reshape(D)
        terms = sum(sums[5:6, hd * HEAD_DIM : (hd + 1) * HEAD_DIM] for hd in range(HG))
        gate = jax.nn.sigmoid(scale[...].reshape(1, HEAD_DIM)) * (query_base / math.sqrt(HEAD_DIM))
        vectors[2][...] = (terms * gate).reshape(HEAD_DIM)

    final = [((L, D), BF16)] * 2 + [((SR, D), F32)] * 6 + [((D,), F32)] * 8
    final[10] = ((HEAD_DIM,), F32)
    return pl.pallas_call(
        finish,
        out_shape=[jax.ShapeDtypeStruct(*shape) for shape in final],
        in_specs=[whole] * 6,
        out_specs=[whole] * 16,
        compiler_params=pltpu.CompilerParams(vmem_limit_bytes=VMEM_BYTES),
    )(out, gtok, go, gall, g_small, query_scale)


def solution(mesh):
    rows, line, copied = P(("rep", "shard"), None), P("shard", None), P()
    in_specs = (rows, P("rep", None), P("rep", None)) + (line,) * 6 + (copied,) * 8 + (rows,)
    out_specs = (rows, rows) + (line,) * 6 + (copied,) * 8
    body = functools.partial(shards, mesh.shape["rep"], mesh.shape["shard"])
    return jax.shard_map(
        body, mesh=mesh, in_specs=in_specs, out_specs=out_specs, check_vma=False
    )
```

```python
import functools
import math

import jax
import jax.numpy as jnp
from jax import lax
from jax.experimental import pallas as pl
from jax.experimental.pallas import tpu as pltpu
from jax.sharding import PartitionSpec as P

HEADS = 16
HEAD_DIM = 80
MESH = pl.DeviceIdType.MESH
F32 = jnp.float32
BF16 = jnp.bfloat16

norm_eps = 1e-06
query_base = 1.442695
masked_score = -1e30
LABELS = 16
VMEM_BYTES = 64 << 20
SECOND = (
    "wg0", "wg2", "out", "cs0", "mwait", "wg1", "delta", "B1", "cs2", "B2", "cs1", "release", "BX",
    "qg0", "t", "qg1", "f2", "ago", "f0", "agm", "t0", "g2", "ac", "Q00", "f1", "g0", "Q01", "ab",
    "Q10", "Q11", "h00", "g1", "Q20", "au", "Q21", "h20", "Q30", "h01", "t1", "h10", "end", "h21",
    "h11", "t2", "L0", "L1", "k0", "t3", "k1", "Q31", "L2", "t4", "k2",
)
FIRST = (
    "tok", "wcat", "own", "carry", "l2", "l1", "coth", "n0", "wcat2", "l0", "n1", "xu0", "s0", "q0",
    "xb0", "xu1", "l10", "l11", "l00", "l12", "tables", "q1", "l20", "l01", "xp1", "xp0", "q2",
    "turnq", "xb1", "s00", "s20", "s10", "l21", "l02", "s12", "project", "l22", "s02", "cot", "A0",
    "A1", "c02", "s21", "s01", "c10", "A2", "c00", "A3", "c01", "s11", "s22", "AX", "c21", "c20",
    "c12", "owait", "F0", "s1", "F1", "s2", "c11", "c22", "F2",
)


def dot(left, right):
    return jnp.dot(left, right, preferred_element_type=F32)


def dot_nt(left, right):
    return lax.dot_general(left, right, (((1,), (1,)), ((), ())), preferred_element_type=F32)


def when(condition, body):
    if condition is True:
        body()
    elif condition is not False:
        pl.when(condition)(body)


class Copy:
    def __init__(self, make, sends, receives):
        self.make, self.sends, self.receives = make, sends, receives

    def start(self):
        when(self.sends, lambda: self.make().start())

    def arrived(self):
        when(self.receives, lambda: self.make().wait_recv())

    def sent(self):
        when(self.sends, lambda: self.make().wait_send())


class Links:
    def __init__(self, send_sems, recv_sems):
        self.send_sems, self.recv_sems, self.used, self.copies = send_sems, recv_sems, 0, []

    def block(self, count):
        first = self.used
        self.used += count
        return first

    def copy(self, src, dst, device, sends=True, receives=True, index=None, keep=True):
        if index is None:
            index = self.block(1)

        def make():
            return pltpu.make_async_remote_copy(
                src_ref=src,
                dst_ref=dst,
                send_sem=self.send_sems.at[index],
                recv_sem=self.recv_sems.at[index],
                device_id=device,
                device_id_type=MESH,
            )

        made = Copy(make, sends, receives)
        if keep:
            self.copies.append(made)
        return made


def layer_kernel(dims, refs):
    R, S, L, D = dims["R"], dims["S"], dims["L"], dims["D"]
    HG, E, CW, SR, H, SRH = (dims[k] for k in ("HG", "E", "CW", "SR", "H", "SRH"))
    q, U, A, T = S // R, R // 2, R, S * L
    HD = HEAD_DIM
    HALF, DH = L // 2, D // 2
    W = 256
    NW = D // W
    ref = refs
    r, s = lax.axis_index("rep"), lax.axis_index("shard")
    u, c, a, b = r // 2, r % 2, s // q, s % q

    def rho(i):
        return (i % 2) * (R // 2) + i // 2

    def rho_back(j):
        return (j % (R // 2)) * 2 + j // (R // 2)

    def turned(i, layer):
        return (i + (R // 2) * (layer // (R // 2))) % R

    def place_of(line_block, layer):
        return turned(rho_back(line_block), layer)

    def device(r2, a2, b2):
        return (r2, a2 * q + b2)

    def peer(u2, c2, b2):
        return device(u2 * 2 + c2, a, b2)

    def block_of(u2, c2, b2):
        return rho(turned(u2 * 2 + c2, a)) * q + b2

    def rows_of(blk):
        return pl.ds(pl.multiple_of(blk * L, L), L)

    g = r * q + b
    blk = block_of(u, c, b)
    u_off = [(u + d) % U for d in range(U)]
    b_off = [(b + d) % q for d in range(q)]
    u_from = [(u + U - d) % U for d in range(U)]
    b_from = [(b + q - d) % q for d in range(q)]
    home_r, home_a = place_of(a, rho(r)), rho(r)
    home = device(home_r, home_a, b)
    origin_r, origin_a = rho_back(a), rho(turned(r, a))
    origin = device(origin_r, origin_a, b)
    stays = jnp.logical_and(home_r == r, home_a == a)
    moves = jnp.logical_not(stays)
    apart = jnp.logical_or(home_r != origin_r, home_a != origin_a)
    by_u = U == 2

    def crosses(r2, a2):
        layer = rho(r2)
        return jnp.logical_and(place_of(a2, layer) // 2 != r2 // 2, layer != a2) if by_u else False

    next_r = (1 - u) * 2 + c
    next_home = device(place_of(a, rho(next_r)), rho(next_r), b)
    carrier = device((1 - origin_r // 2) * 2 + origin_r % 2, origin_a, b)
    i_cross, i_carry, carried_in = crosses(r, a), crosses(next_r, a), crosses(origin_r, origin_a)
    direct = jnp.logical_and(moves, jnp.logical_not(i_cross))
    direct_in = jnp.logical_and(moves, jnp.logical_not(carried_in))
    sibling = peer(u, 1 - c, b)
    above = device(r, jnp.minimum(a + 1, A - 1), b)
    below = device(r, jnp.maximum(a - 1, 0), b)
    own_half = pl.ds(pl.multiple_of(c * DH, 128), DH)
    other_half = pl.ds(pl.multiple_of((1 - c) * DH, 128), DH)

    links = Links(ref["send_sems"], ref["recv_sems"])
    events = {}

    def event(name, job):
        events[name] = job

    def play(names):
        for name in names:
            events.pop(name)()

    def segments_of(order, first, last):
        parts, at = {None: []}, None
        for name in order:
            if name[:1] == first and (name[1:].isdigit() or name == last):
                at = name
                parts[at] = []
            else:
                parts[at].append(name)
        return parts

    def start_all(*copies):
        for moved in copies:
            moved.start()


    local_sems = ref["local_sems"]

    def local(src, dst, n):
        return pltpu.make_async_copy(src, dst, local_sems.at[n])

    def near(src, name, n):
        if dims["fits"] or name == "q_rows":
            return src
        copy = local(src, ref[name], n)
        copy.start()
        copy.wait()
        return ref[name]

    def shard_rows(a2, b2):
        return pl.ds(pl.multiple_of((a2 * q + b2) * SR, 16), SR)

    w3 = ref["w3"]
    names = ("w_query", "w_key", "w_value")
    parts = [ref[name].at[pl.ds(0, SR)] for name in ("hid", "ffin", "outb")]
    near_parts = [local(ref[names[n]], parts[n], n) for n in range(3)]
    names = ("w_out", "w_up", "w_down")
    own_shards = [local(ref[names[w]], w3.at[w, shard_rows(a, b)], 4 + w) for w in range(3)]
    near_rows = [local(ref["tokens"], ref["otok"], 3), local(ref["cotangent"], ref["og"], 7)]
    for copy in near_rows[:1] + near_parts + own_shards + near_rows[1:]:
        copy.start()

    barrier = pltpu.get_barrier_semaphore()

    def greet(where):
        pl.semaphore_signal(barrier, inc=1, device_id=where, device_id_type=MESH)

    for k in range(1, S):
        g2 = (g + k) % S
        greet(device(g2 // q, a, g2 % q))
    for k in range(1, A):
        greet(device(r, (a + k) % A, b))
    spread_out = [(u2, k) for u2 in u_off[1:] for k in range(1, A)] if U * A <= 16 else []
    for u2, k in spread_out:
        greet(device(u2 * 2 + c, (a + k) % A, b))
    pl.when(moves)(lambda: greet(home))
    pl.when(apart)(lambda: greet(origin))
    if by_u:
        pl.when(i_carry)(lambda: greet(next_home))
        pl.when(carried_in)(lambda: greet(carrier))

    gains, biascat, qgain, tab = ref["gains"], ref["biascat"], ref["qgain"], ref["tab"]
    rows = ("gain_attn", "gain_ff", "bias_out", "bias_up", "bias_down", "bias_query", "bias_value")
    for n, name in enumerate(rows):
        gains[n : n + 1, :] = ref[name][...].reshape(1, D)
    segments = dims["segments"]
    tab[...] = jnp.zeros((8, 128), F32)
    tab[0:1, 0:segments] = ref["lengths"][...].astype(F32)
    tab[1:2, 0:segments] = ref["parents"][...].astype(F32)
    biascat[...] = jnp.zeros((8, CW), F32)

    def bias_slice(k):
        biascat[0:1, 0:E] = gains[5:6, k * E : (k + 1) * E]
        biascat[0:1, 2 * E : 3 * E] = gains[6:7, k * E : (k + 1) * E]

    for k in range(S):
        pl.when(g == k)(functools.partial(bias_slice, k))
    scale = ref["query_scale"][...].reshape(1, HD)
    soft = jnp.maximum(scale, 0.0) + jnp.log(1.0 + jnp.exp(-jnp.abs(scale)))
    qgain[...] = jnp.ones((8, CW), F32)
    for hd in range(HG):
        qgain[0:1, hd * HD : (hd + 1) * HD] = soft * (query_base / math.sqrt(HD))

    wq, wqt, wcat = ref["wq"], ref["wqt"], ref["gall"]
    for copy in near_parts:
        copy.wait()

    def cut_columns(r2):
        for b2 in range(q):
            first = (r2 * q + b2) * E
            for n in range(3):
                wcat[b2, :, n * E : (n + 1) * E] = parts[n][:, first : first + E]
            if CW > 3 * E:
                wcat[b2, :, 3 * E : CW] = jnp.zeros((SR, CW - 3 * E), BF16)

    for r2 in range(R):
        pl.when(r == r2)(functools.partial(cut_columns, r2))
    wq[shard_rows(a, b), :] = wcat[b]
    others = S - 1 + A - 1 + len(spread_out) + jnp.where(moves, 1, 0) + jnp.where(apart, 1, 0)
    if by_u:
        others = others + jnp.where(i_carry, 1, 0) + jnp.where(carried_in, 1, 0)
    pl.semaphore_wait(barrier, others)

    for copy in near_rows:
        copy.wait()
    swap_tab = links.copy(ref["tab"], ref["tabs"], home, moves, moves)
    swap_rows, swap_cot = [], []
    for name, there, pieces in (("otok", "tok", swap_rows), ("og", "cot", swap_cot)):
        for h in range(2):
            here = pl.ds(h * HALF, HALF)
            src, dst = ref[name].at[here], ref[there].at[here]
            piece = [links.copy(src, dst, home, direct, direct_in)]
            if by_u:
                lent = ref["lent_" + there].at[here]
                piece.append(links.copy(src, lent, peer(1 - u, c, b), i_cross, i_carry))
                piece.append(links.copy(lent, dst, next_home, i_carry, carried_in))
            pieces.append(piece)

    def swap_begin(pieces):
        for piece in pieces:
            for moved in piece[:2]:
                moved.start()

    def swap_carry(pieces):
        for piece in pieces:
            if by_u:
                piece[1].arrived()
                piece[2].start()

    def swap_end(piece):
        for moved in piece[0::2]:
            moved.arrived()

    def swap_sent(pieces):
        for moved in [m for piece in pieces for m in piece[:2]]:
            moved.sent()
            links.copies.remove(moved)

    def keep_rows():
        for name, there in (("otok", "tok"), ("tab", "tabs"), ("og", "cot")):
            ref[there][...] = ref[name][...]


    def tok_begin():
        swap_tab.start()
        swap_begin(swap_rows)

    event("tok", tok_begin)
    event("coth", lambda: start_all(*[piece[1] for piece in swap_cot if by_u]))
    event("carry", lambda: swap_carry(swap_rows))

    def cot_on():
        start_all(*[piece[0] for piece in swap_cot])
        swap_carry(swap_cot)

    event("cot", cot_on)

    wq_rows = shard_rows
    wcat_b = {}
    for db in range(1, q):
        wcat_b[db] = links.copy(
            wcat.at[b_off[db]], wq.at[wq_rows(a, b)], device(r, a, b_off[db])
        )
    up_q, down_q = {}, {}
    for k in range(A - 1):
        for db in range(q):
            low, high = jnp.maximum(a - k, 0), jnp.minimum(a + k, A - 1)
            slot = wq_rows(low, b_from[db])
            up_q[k, db] = links.copy(
                wq.at[slot], wq.at[slot], above,
                jnp.logical_and(a - k >= 0, a < A - 1), a - 1 - k >= 0,
            )
            slot = wq_rows(high, b_from[db])
            down_q[k, db] = links.copy(
                wq.at[slot], wq.at[slot], below,
                jnp.logical_and(a + k <= A - 1, a > 0), a + 1 + k <= A - 1,
            )

    def wq_begin():
        start_all(*wcat_b.values(), up_q[0, 0], down_q[0, 0])

    def wq_side():
        for db in range(1, q):
            wcat_b[db].arrived()
            start_all(up_q[0, db], down_q[0, db])

    event("wcat", wq_begin)
    event("wcat2", wq_side)
    def wq_pass(k):
        for db in range(q):
            up_q[k, db].arrived()
            down_q[k, db].arrived()
            if k + 1 < A - 1:
                up_q[k + 1, db].start()
                down_q[k + 1, db].start()

    for k in range(A - 1):
        event(f"q{k}", functools.partial(wq_pass, k))

    def piece_rows(a2, b2, u2):
        if H == 1:
            return shard_rows(a2, b2)
        return pl.ds(pl.multiple_of((a2 * q + b2) * SR + u2 * SRH, 16), SRH)

    for copy in own_shards:
        copy.wait()
    pl.when(stays)(keep_rows)

    def b_then_u(u2, w):
        return u2 % 2 != a % 2 if w < 2 else False

    up_w, down_w, side_w, own_w, core_w, core_own = {}, {}, {}, {}, {}, {}
    slots = [sign * k for k in range(1, A) for sign in (1, -1)]
    for w in range(3):
        for k in range(A - 1):
            low, high = jnp.maximum(a - k, 0), jnp.minimum(a + k, A - 1)
            at = w3.at[w, piece_rows(low, b, u), own_half]
            up_w[w, k] = links.copy(
                at, at, above, jnp.logical_and(a - k >= 0, a < A - 1), a - 1 - k >= 0
            )
            at = w3.at[w, piece_rows(high, b, u), own_half]
            down_w[w, k] = links.copy(
                at, at, below, jnp.logical_and(a + k <= A - 1, a > 0), a + 1 + k <= A - 1
            )
        by_place = {}

        def sems(kind, place):
            if kind not in by_place:
                by_place[kind] = links.block(A)
            return by_place[kind] + place

        for slot in slots:
            valid = a + slot <= A - 1 if slot > 0 else a + slot >= 0
            a0 = jnp.clip(a + slot, 0, A - 1)
            at = w3.at[w, piece_rows(a0, b, u), own_half]
            for db in range(1, q):
                side_w[w, slot, 0, db] = links.copy(
                    at, at, peer(u, c, b_off[db]), valid, valid, index=sems(("b", db), a0)
                )
            if H > 1:
                for du in range(1, U):
                    side_w[w, slot, du, 0] = links.copy(
                        at, at, peer(u_off[du], c, b), valid, valid, index=sems(("u", du), a0)
                    )
                    for db in range(1, q):
                        sent, came = b_then_u(u, w), b_then_u(u_from[du], w)
                        at = w3.at[w, piece_rows(a0, b_from[db], u), own_half]
                        side_w[w, slot, du, db] = links.copy(
                            at, at, peer(u_off[du], c, b),
                            jnp.logical_and(valid, sent), jnp.logical_and(valid, came),
                            index=sems(("bu", du, db), a0),
                        )
                        at = w3.at[w, piece_rows(a0, b, u_from[du]), own_half]
                        other = jnp.logical_and(valid, jnp.logical_not(came))
                        side_w[w, slot, du, -db] = links.copy(
                            at, at, peer(u, c, b_off[db]), other, other,
                            index=sems(("ub", du, db), a0),
                        )
            at = w3.at[w, pl.ds(pl.multiple_of(a0 * q * SR, 16), q * SR), own_half]
            core_w[w, slot] = links.copy(at, at, sibling, valid, valid, index=sems("core", a0))
        for db in range(1, q):
            at = w3.at[w, shard_rows(a, b), own_half]
            own_w[w, db] = links.copy(at, at, peer(u, c, b_off[db]))
            at = w3.at[w, shard_rows(a, b_from[db]), own_half]
            core_own[w, db] = links.copy(at, at, sibling)

    def w3_line(w, k):
        if k < 0:
            up_w[w, 0].start()
            down_w[w, 0].start()
            return
        up_w[w, k].arrived()
        down_w[w, k].arrived()
        if k + 1 < A - 1:
            up_w[w, k + 1].start()
            down_w[w, k + 1].start()
        for slot in (-(k + 1), k + 1):
            for (w2, slot2, du, db), moved in side_w.items():
                if (w2, slot2) == (w, slot) and (du == 0 or db == 0):
                    moved.start()

    def w3_side(w, k):
        if k < 0:
            for db in range(1, q):
                own_w[w, db].arrived()
                core_own[w, db].start()
            return
        for slot in (-(k + 1), k + 1):
            for db in range(1, q):
                side_w[w, slot, 0, db].arrived()
            if H > 1:
                for du in range(1, U):
                    side_w[w, slot, du, 0].arrived()
                    for db in range(1, q):
                        side_w[w, slot, du, db].start()
                        side_w[w, slot, du, -db].start()

    def w3_core(w, k):
        for slot in (-(k + 1), k + 1):
            if H > 1:
                for du in range(1, U):
                    for db in range(1, q):
                        side_w[w, slot, du, db].arrived()
                        side_w[w, slot, du, -db].arrived()
            core_w[w, slot].start()

    event("own", lambda: start_all(*own_w.values()))
    for w in range(3):
        event(f"l{w}", functools.partial(w3_line, w, -1))
        event(f"s{w}", functools.partial(w3_side, w, -1))
        for k in range(A - 1):
            event(f"l{w}{k}", functools.partial(w3_line, w, k))
            event(f"s{w}{k}", functools.partial(w3_side, w, k))
            event(f"c{w}{k}", functools.partial(w3_core, w, k))

    def w3_whole(w):
        for db in range(1, q):
            core_own[w, db].arrived()
        for slot in slots:
            core_w[w, slot].arrived()

    tok, cot, xa = ref["tok"], ref["cot"], ref["xa"]
    gain_attn, gain_ff = gains[0:1, :], gains[1:2, :]
    STEP = 32

    def unit(x):
        return lax.rsqrt(jnp.mean(x * x, axis=-1, keepdims=True) + norm_eps)

    def half_rows(block, h):
        return pl.ds(pl.multiple_of(block * L + h * HALF, HALF), HALF)

    own_x, pass_x, sib_x = {}, {}, {}
    for h in range(2):
        at = xa.at[half_rows(blk, h)]
        for db in range(1, q):
            own_x[h, 0, db] = links.copy(at, at, peer(u, c, b_off[db]))
        for du in range(1, U):
            own_x[h, du, 0] = links.copy(at, at, peer(u_off[du], c, b))
        for du in range(1, U):
            for db in range(1, q):
                if h == 0:
                    at = xa.at[half_rows(block_of(u, c, b_from[db]), h)]
                    pass_x[h, du, db] = links.copy(at, at, peer(u_off[du], c, b))
                else:
                    at = xa.at[half_rows(block_of(u_from[du], c, b), h)]
                    pass_x[h, du, db] = links.copy(at, at, peer(u, c, b_off[db]))
        for du in range(U):
            for db in range(q):
                at = xa.at[half_rows(block_of(u_from[du], c, b_from[db]), h)]
                sib_x[h, du, db] = links.copy(at, at, sibling)

    def norm_half(h):
        swap_end(swap_rows[h])

        def norm_step(i, carried):
            here = pl.ds(pl.multiple_of(h * HALF + i * STEP, STEP), STEP)
            x = tok[here, :].astype(F32)
            there = pl.ds(pl.multiple_of(blk * L + h * HALF + i * STEP, STEP), STEP)
            row = (x * unit(x) * gain_attn).astype(BF16)
            if dims["fits"]:
                xa[there, :] = row
            else:
                ref["x_rows"][here, :] = row
            return carried

        lax.fori_loop(0, HALF // STEP, norm_step, 0)
        if not dims["fits"]:
            here = pl.ds(h * HALF, HALF)
            out_of = local(ref["x_rows"].at[here], xa.at[half_rows(blk, h)], 7)
            out_of.start()
            out_of.wait()
        start_all(*[m for (h2, *_), m in own_x.items() if h2 == h], sib_x[h, 0, 0])

    def rows_on_b(h):
        for db in range(1, q):
            own_x[h, 0, db].arrived()
            if h == 0:
                start_all(*[pass_x[0, du, db] for du in range(1, U)])
            sib_x[h, 0, db].start()

    def rows_on_u(h):
        for du in range(1, U):
            own_x[h, du, 0].arrived()
            if h == 1:
                start_all(*[pass_x[1, du, db] for db in range(1, q)])
            sib_x[h, du, 0].start()

    def rows_passed(h):
        for du in range(1, U):
            for db in range(1, q):
                pass_x[h, du, db].arrived()
                sib_x[h, du, db].start()

    for h in range(2):
        event(f"n{h}", functools.partial(norm_half, h))
        event(f"xb{h}", functools.partial(rows_on_b, h))
        event(f"xu{h}", functools.partial(rows_on_u, h))
        event(f"xp{h}", functools.partial(rows_passed, h))

    tables = {}

    def make_tables():
        swap_tab.arrived()
        lane = lax.broadcasted_iota(jnp.int32, (LABELS, 128), 1)
        row = lax.broadcasted_iota(jnp.int32, (LABELS, 128), 0)
        lengths = jnp.broadcast_to(ref["tabs"][0:1, :], (LABELS, 128))
        seg_start = jnp.sum(jnp.where(lane < row, lengths, 0.0), axis=1, keepdims=True)
        seg_end = jnp.sum(jnp.where(lane <= row, lengths, 0.0), axis=1, keepdims=True)
        lane = lax.broadcasted_iota(jnp.int32, (128, 128), 1)
        row = lax.broadcasted_iota(jnp.int32, (128, 128), 0)
        parents = jnp.broadcast_to(ref["tabs"][1:2, :], (128, 128))
        is_parent = (parents == row.astype(F32)) & (lane > 0) & (lane < segments)
        reach = jnp.where((lane == row) | is_parent, 1.0, 0.0)
        for _ in range(max(1, (segments - 1).bit_length())):
            reach = jnp.minimum(dot(reach.astype(BF16), reach.astype(BF16)), 1.0)
        blocked = ((1.0 - reach[:LABELS, :LABELS]) * masked_score).astype(BF16)
        tables["start"], tables["end"], tables["blocked"] = seg_start, seg_end, blocked

    event("tables", make_tables)

    def turn_wq(i, carried):
        here = pl.ds(pl.multiple_of(i * W, W), W)
        wqt[:, here] = wq[here, :].T
        return carried

    event("turnq", lambda: lax.fori_loop(0, NW, turn_wq, 0))
    bias_col = jnp.transpose(biascat[...])[:, 0:1]
    qgain_col = jnp.transpose(qgain[...])[:, 0:1]
    qkvf, qpre, qt, keys, kt, vals, vt = (
        ref[k] for k in ("qkvf", "qpre", "qt", "keys", "kt", "vals", "vt")
    )

    def project(k, carried):
        for j in range(S):

            def wait_rows(j=j):
                du, db, other = (j // 2) // q, (j // 2) % q, j % 2
                if other:
                    for h in range(2):
                        sib_x[h, du, db].arrived()

            pl.when(k == j)(wait_rows)
        du, db, other = (k // 2) // q, (k // 2) % q, k % 2
        block = block_of((u + U - du) % U, (c + other) % 2, (b + q - db) % q)
        cols = rows_of(block)
        x = near(xa.at[cols], "x_rows", 7)[...]
        qkvf[...] = dot_nt(wqt[...], x) + bias_col
        place = block * L + lax.broadcasted_iota(jnp.int32, (LABELS, L), 1)
        place = place.astype(F32)
        onehot = jnp.where((place >= tables["start"]) & (place < tables["end"]), 1.0, 0.0)
        far = dot(tables["blocked"], onehot.astype(BF16)).astype(BF16)
        for hd in range(HG):
            head = pl.ds(hd * HD, HD)
            pre = qkvf[head, :]
            qpre[head, cols] = pre
            qt[hd, 0:HD, cols] = (pre * qgain_col[hd * HD : (hd + 1) * HD]).astype(BF16)
            qt[hd, HD : HD + LABELS, cols] = far
            qt[hd, HD + LABELS : 128, cols] = jnp.zeros((128 - HD - LABELS, L), BF16)
            key = qkvf[pl.ds(E + hd * HD, HD), :]
            kt[hd, :, cols] = key.astype(BF16)
            wide = jnp.concatenate([key, onehot, jnp.zeros((128 - HD - LABELS, L), F32)], axis=0)
            keys[hd, cols, :] = wide.T.astype(BF16)
            value = qkvf[pl.ds(2 * E + hd * HD, HD), :]
            vt[hd, :, cols] = value.astype(BF16)
            wide = jnp.concatenate([value, jnp.zeros((128 - HD, L), F32)], axis=0)
            vals[hd, cols, :] = wide.T.astype(BF16)
        return carried

    event("project", lambda: lax.fori_loop(0, S, project, 0))

    ot, otb, lse, oa = ref["ot"], ref["otb"], ref["lse"], ref["oa"]
    first_o = links.block(S)
    o_slot = pl.ds(pl.multiple_of(g * E, 16), E)

    def o_copy(block):
        r2, b2 = place_of(block // q, a), block % q
        index = first_o + (r2 * q + b2 + S - g) % S
        return links.copy(
            otb.at[:, rows_of(block)], oa.at[o_slot], device(r2, a, b2), index=index, keep=False
        )

    PAIR = 2
    SQ = PAIR * L
    diagonal = lax.broadcasted_iota(jnp.int32, (SQ, SQ), 0) <= lax.broadcasted_iota(
        jnp.int32, (SQ, SQ), 1
    )
    def wide_rows(i):
        return pl.ds(pl.multiple_of(i * SQ, SQ), SQ)

    def attend(i, carried):
        cols = wide_rows(i)
        query = [qt[hd, :, cols] for hd in range(HG)]

        def key_block(j, state, on_diagonal):
            here = wide_rows(j)
            result = []
            for hd in range(HG):
                top, total, acc = state[hd]
                score = dot(keys[hd, here, :], query[hd])
                if on_diagonal:
                    score = jnp.where(diagonal, score, masked_score)
                new_top = jnp.maximum(top, jnp.max(score, axis=0, keepdims=True))
                p = jnp.exp(score - new_top)
                fade = jnp.exp(top - new_top)
                total = total * fade + jnp.sum(p, axis=0, keepdims=True)
                acc = acc * fade + dot(vt[hd, :, here], p.astype(BF16))
                result.append((new_top, total, acc))
            return tuple(result)

        start = tuple(
            (
                jnp.full((1, SQ), masked_score, F32),
                jnp.zeros((1, SQ), F32),
                jnp.zeros((HD, SQ), F32),
            )
            for _ in range(HG)
        )
        state = lax.fori_loop(0, i, functools.partial(key_block, on_diagonal=False), start)
        state = key_block(i, state, True)
        for hd in range(HG):
            top, total, acc = state[hd]
            mixed = acc / total
            head = pl.ds(hd * HD, HD)
            ot[head, cols] = mixed
            otb[head, cols] = mixed.astype(BF16)
            lse[hd, :, cols] = jnp.broadcast_to(top + jnp.log(total), (8, SQ))
        for k in range(PAIR):
            block = i * PAIR + k

            def keep_block(block=block):
                oa[o_slot, :] = otb[:, rows_of(block)]

            pl.when(block == blk)(keep_block)
            pl.when(block != blk)(lambda block=block: o_copy(block).start())
        for j in range(S // PAIR):
            if order.get(f"A{j}"):
                pl.when(i == j)(functools.partial(play, order[f"A{j}"]))
        return carried

    def o_arrived(k, carried):
        links.copy(
            otb.at[:, rows_of(0)], oa.at[o_slot], sibling, index=first_o + k, keep=False
        ).make().wait_recv()
        return carried

    event("owait", lambda: lax.fori_loop(1, S, o_arrived, 0))

    names = [name for name in FIRST if name in events or name[0] in "AF"]
    for k in range(A - 1):
        for at, name in [("turnq", f"q{k}")] + [
            (f"F{w}", f"{kind}{w}{k}") for w in range(3) for kind in "lsc"
        ]:
            if name not in names:
                names.insert(names.index(at), name)
    ff_order = segments_of(names, "F", "FX")
    order = segments_of(ff_order.pop(None), "A", "AX")
    play(order[None])
    lax.fori_loop(0, S // PAIR, attend, 0)
    play(order["AX"])
    def o_sent(i, carried):
        pl.when(i != blk)(lambda: o_copy(i).sent())
        return carried

    otok, mid, ffin, up, hid, outb = (ref[k] for k in ("otok", "mid", "ffin", "up", "hid", "outb"))
    ug, fg, mg, og, mgt = (ref[k] for k in ("ug", "fg", "mg", "og", "mgt"))
    small = ref["small"]

    def tile(n):
        return pl.ds(pl.multiple_of(n * W, W), W)

    def turn_o(n, carried):
        otok[:, tile(n)] = oa[tile(n), :].T
        return carried

    swap_sent(swap_rows)
    lax.fori_loop(0, NW, turn_o, 0)
    play(ff_order["F0"])
    w3_whole(0)

    def out_step(n, carried):
        added = dot(otok[...], w3[0, :, tile(n)]) + gains[2:3, tile(n)]
        mid[:, tile(n)] = tok[:, tile(n)].astype(F32) + added
        return carried

    lax.fori_loop(0, NW, out_step, 0)

    def strip(i):
        return pl.ds(pl.multiple_of(i * STEP, STEP), STEP)

    def ff_norm(i, carried):
        x = mid[strip(i), :]
        ffin[strip(i), :] = (x * unit(x) * gain_ff).astype(BF16)
        return carried

    lax.fori_loop(0, L // STEP, ff_norm, 0)
    play(ff_order["F1"])
    w3_whole(1)

    def up_step(n, carried):
        pre = dot(ffin[...], w3[1, :, tile(n)]) + gains[3:4, tile(n)]
        up[:, tile(n)] = pre
        hid[:, tile(n)] = (pre * jax.nn.sigmoid(pre)).astype(BF16)
        return carried

    lax.fori_loop(0, NW, up_step, 0)
    play(ff_order["F2"])
    w3_whole(2)

    def down_step(n, carried):
        added = dot(hid[...], w3[2, :, tile(n)]) + gains[4:5, tile(n)]
        outb[:, tile(n)] = (mid[:, tile(n)] + added).astype(BF16)
        return carried

    lax.fori_loop(0, NW, down_step, 0)
    back_out = links.copy(outb, ref["out"], origin, moves, moves)

    def keep_out():
        kept = local(outb, ref["out"], 0)
        kept.start()
        kept.wait()

    def out_back():
        back_out.start()
        pl.when(stays)(keep_out)

    event("out", out_back)
    for piece in swap_cot:
        swap_end(piece)
    swap_sent(swap_cot)
    small[...] = jnp.zeros_like(small)

    def up_back(n, carried):
        pre = up[:, tile(n)]
        gate = jax.nn.sigmoid(pre)
        grad = dot_nt(cot[...], w3[2, tile(n), :]) * gate * (1.0 + pre * (1.0 - gate))
        grad = grad.astype(BF16)
        ug[:, tile(n)] = grad
        small[3:4, tile(n)] = jnp.sum(grad.astype(F32), axis=0, keepdims=True)
        return carried

    lax.fori_loop(0, NW, up_back, 0)

    def ff_back(n, carried):
        fg[:, tile(n)] = dot_nt(ug[...], w3[1, tile(n), :])
        return carried

    lax.fori_loop(0, NW, ff_back, 0)

    def mid_back(i, carried):
        x, grad, above_grad = mid[strip(i), :], fg[strip(i), :], cot[strip(i), :].astype(F32)
        inverse = unit(x)
        normed = x * inverse
        small[1:2, :] += jnp.sum(grad * normed, axis=0, keepdims=True)
        scaled = grad * gain_ff
        mean = jnp.mean(scaled * normed, axis=-1, keepdims=True)
        total = above_grad + inverse * (scaled - normed * mean)
        mg[strip(i), :] = total
        rounded = total.astype(BF16)
        og[strip(i), :] = rounded
        small[2:3, :] += jnp.sum(rounded.astype(F32), axis=0, keepdims=True)
        small[4:5, :] += jnp.sum(above_grad, axis=0, keepdims=True)
        return carried

    lax.fori_loop(0, L // STEP, mid_back, 0)

    dot_t = ref["dot_t"]
    first_m = links.block(S)

    def m_copy(k):
        g2 = (g + k) % S
        at = pl.ds(pl.multiple_of(g2 * E, 16), E)
        return links.copy(
            mgt.at[at], dot_t.at[:, rows_of(blk)], device(g2 // q, a, g2 % q),
            index=first_m + k, keep=False,
        )

    def mixed_step(k, carried):
        at = pl.ds(pl.multiple_of(((g + k) % S) * E, 16), E)
        mgt[at, :] = dot_nt(w3[0, at, :], og[...]).astype(BF16)
        pl.when(k < S)(lambda: m_copy(k).start())
        return carried

    lax.fori_loop(1, S + 1, mixed_step, 0)
    dot_t[:, rows_of(blk)] = mgt[pl.ds(pl.multiple_of(g * E, 16), E), :]

    freed, freed_again = ref["freed"], ref["freed_again"]
    writers = [sibling] + [peer(u, c, v) for v in b_off[1:]] + [peer(v, c, b) for v in u_off[1:]]

    def release(sem):
        for where in writers:
            pl.semaphore_signal(sem, inc=1, device_id=where, device_id_type=MESH)

    for group in (wcat_b, up_w, down_w, side_w, own_w, core_w, core_own):
        for moved in group.values():
            moved.sent()
            links.copies.remove(moved)
    release(freed)

    gp, rc = ref["gp"], ref["rc"]
    rcin = [w3.at[0, :, 0:DH], w3.at[0, :, DH:D], w3.at[1, :, 0:DH]]
    core_g = [links.copy(gp.at[w], rcin[w], sibling) for w in range(3)]

    def weight_grad(w, left, right):
        if left is not None:

            def turn(n, carried):
                oa[tile(n), :] = left[:, tile(n)].T
                return carried

            lax.fori_loop(0, NW, turn, 0)

        def step(n, carried):
            here = pl.ds(pl.multiple_of(n * SR, 16), SR)
            side = oa[here, :]
            gp[w, here, :] = dot(side, right[:, other_half]).astype(BF16)
            rc[w, n // q, n % q] = dot(side, right[:, own_half]).astype(BF16)
            return carried

        lax.fori_loop(0, S, step, 0)

    def m_arrived(k, carried):
        m_copy(k).arrived()
        return carried

    A2 = A // 2
    u_rows = [pl.ds(pl.multiple_of(v * SRH, 16), SRH) for v in u_off]
    my_rows = u_rows[0]
    qm, um = q - 1, U - 1

    def t1b(w, db, a2):
        at = D - 3 * qm * A2 * SR + ((w * qm + db - 1) * A2 + a2) * SR
        assert at >= 0
        return w3.at[1, at : at + SR, DH:D]

    def t1u(w, du, a2, b2):
        at = (((w * um + du - 1) * A2 + a2) * q + b2) * SRH
        assert at + SRH <= D
        return w3.at[2, at : at + SRH, 0:DH]

    def t2b(w, db, a2):
        at = ((w * qm + db - 1) * A2 + a2) * SRH
        return w3.at[2, at : at + SRH, DH:D]

    def t2u(w, du, a2):
        at = (3 * qm * A2 + (w * um + du - 1) * A2 + a2) * SRH
        assert at + SRH <= D
        return w3.at[2, at : at + SRH, DH:D]

    first_b, first_u, second_b, second_u = {}, {}, {}, {}
    for w in range(3):
        for a2 in range(A2):
            for db in range(1, q):
                to = peer(u, c, b_off[db])
                first_b[w, db, a2] = links.copy(rc.at[w, a2, b_off[db]], t1b(w, db, a2), to)
                second_b[w, db, a2] = links.copy(
                    rc.at[w, A2 + a2, b_off[db], my_rows], t2b(w, db, a2), to
                )
            if H > 1:
                for du in range(1, U):
                    to = peer(u_off[du], c, b)
                    for b2 in range(q):
                        first_u[w, du, a2, b2] = links.copy(
                            rc.at[w, A2 + a2, b2, u_rows[du]], t1u(w, du, a2, b2), to
                        )
                    second_u[w, du, a2] = links.copy(
                        rc.at[w, a2, b, u_rows[du]], t2u(w, du, a2), to
                    )

    def add_into(target, *more):
        total = target[...].astype(F32)
        for other in more:
            total = total + other[...].astype(F32)
        target[...] = total.astype(BF16)

    def core_sum(w):
        core_g[w].arrived()

        def step(n, carried):
            a2, b2 = n // q, n % q
            here = pl.ds(pl.multiple_of(n * SR, 16), SR)
            add_into(rc.at[w, a2, b2], rcin[w].at[here])
            return carried

        lax.fori_loop(0, S, step, 0)
        for key, moved in list(first_b.items()) + list(first_u.items()):
            if key[0] == w:
                moved.start()

    def side_sum_1(w):
        for db in range(1, q):
            for a2 in range(A2):
                first_b[w, db, a2].arrived()
                add_into(rc.at[w, a2, b], t1b(w, db, a2))
        if H > 1:
            for du in range(1, U):
                for a2 in range(A2):
                    for b2 in range(q):
                        first_u[w, du, a2, b2].arrived()
                        add_into(rc.at[w, A2 + a2, b2, my_rows], t1u(w, du, a2, b2))
        for key, moved in list(second_b.items()) + list(second_u.items()):
            if key[0] == w:
                moved.start()

    def side_sum_2(w):
        for db in range(1, q):
            for a2 in range(A2):
                second_b[w, db, a2].arrived()
                add_into(rc.at[w, A2 + a2, b, my_rows], t2b(w, db, a2))
        if H > 1:
            for du in range(1, U):
                for a2 in range(A2):
                    second_u[w, du, a2].arrived()
                    add_into(rc.at[w, a2, b, my_rows], t2u(w, du, a2))

    def first_grad():
        weight_grad(0, None, og)
        pl.semaphore_wait(freed, len(writers))
        core_g[0].start()

    def next_grad(w, left, right):
        weight_grad(w, left, right)
        core_g[w].start()

    event("wg0", first_grad)
    event("wg1", lambda: next_grad(1, ffin, ug))
    event("wg2", lambda: next_grad(2, hid, cot))
    event("release", lambda: release(freed_again))
    event("mwait", lambda: lax.fori_loop(1, S, m_arrived, 0))
    for w in range(3):
        event(f"cs{w}", functools.partial(core_sum, w))
        event(f"f{w}", functools.partial(side_sum_1, w))

    assert A & (A - 1) == 0
    strides = [1 << n for n in range(A.bit_length() - 1)]

    def across(k):
        return a + k - 2 * k * (a // k % 2)

    class Line:
        def __init__(self, part, landed, near_name):
            self.part, self.landed, self.near_name, self.steps = part, landed, near_name, []
            slot = 0
            for k in strides:
                step = []
                for m in range(A // (2 * k)):
                    mine = a % (2 * k) + 2 * k * m
                    theirs = across(k) % (2 * k) + 2 * k * m
                    copy = links.copy(part(theirs), landed(slot), device(r, across(k), b))
                    step.append((copy, mine, slot))
                    slot += 1
                self.steps.append(step)

        def begin(self, n=0):
            for copy, _, _ in self.steps[n]:
                copy.start()

        def step(self, n):
            for copy, mine, slot in self.steps[n]:
                copy.arrived()
                add_into(self.part(mine), near(self.landed(slot), self.near_name, 7))
            if n + 1 < len(self.steps):
                self.begin(n + 1)

    cu = ref["cu"]
    lines = []
    for w in range(3):
        lines.append(
            Line(
                lambda d, w=w: rc.at[w, d, b, my_rows],
                lambda slot, w=w: cu.at[slot, w],
                "c_rows",
            )
        )

    def line_begin(w):
        side_sum_2(w)
        lines[w].begin()

    for w in range(3):
        event(f"g{w}", functools.partial(line_begin, w))
        event(f"h{w}0", functools.partial(lines[w].step, 0))

    delta, dqt, dqkvt = ref["delta"], ref["dqt"], ref["dqkvt"]
    def make_delta():
        for hd in range(HG):
            head = slice(hd * HD, (hd + 1) * HD)
            total = jnp.sum(dot_t[head, :].astype(F32) * ot[head, :], axis=0, keepdims=True)
            delta[hd, :, :] = jnp.broadcast_to(total, (8, T))
        dqt[...] = jnp.zeros_like(dqt)

    event("delta", make_delta)
    NB = S // PAIR
    starts = [sum(NB - k for k in range(j)) for j in range(NB)]
    pairs = NB * (NB + 1) // 2
    dkt, dvt = ref["dkt"], ref["dvt"]

    def attend_back(n, carried):
        j = sum(jnp.where(n >= start, 1, 0) for start in starts[1:])
        start = sum(jnp.where(n >= starts[k], starts[k] - starts[k - 1], 0) for k in range(1, NB))
        i = n - start + j
        here, cols = wide_rows(j), wide_rows(i)

        def block(on_diagonal):
            for hd in range(HG):
                head = pl.ds(hd * HD, HD)
                score = dot(keys[hd, here, :], qt[hd, :, cols])
                if on_diagonal:
                    score = jnp.where(diagonal, score, masked_score)
                p = jnp.exp(score - lse[hd, 0:1, cols])
                d_out = dot_t[head, cols]
                dp = dot(vals[hd, here, 0:HD], d_out)
                ds = (p * (dp - delta[hd, 0:1, cols])).astype(BF16)
                dv = dot_nt(d_out, p.astype(BF16))
                dk = dot_nt(qt[hd, 0:HD, cols], ds)
                if on_diagonal:
                    dvt[head, :], dkt[head, :] = dv, dk
                else:
                    dvt[head, :] += dv
                    dkt[head, :] += dk
                dqt[head, cols] += dot(kt[hd, :, here], ds)

        pl.when(i == j)(lambda: block(True))
        pl.when(i != j)(lambda: block(False))

        def keep():
            dqkvt[E : 2 * E, here] = dkt[...].astype(BF16)
            dqkvt[2 * E : 3 * E, here] = dvt[...].astype(BF16)

        pl.when(i == NB - 1)(keep)
        for m in range(pairs):
            if back_order.get(f"B{m}"):
                pl.when(n == m)(functools.partial(play, back_order[f"B{m}"]))
        return carried

    names = [name for name in SECOND if name in events or name[0] == "B"]
    first_part = names[: names.index("BX")]
    back_order = segments_of(first_part, "B", "BX")
    play(back_order[None])
    lax.fori_loop(0, pairs, attend_back, 0)
    if CW > 3 * E:
        dqkvt[3 * E :, :] = jnp.zeros((CW - 3 * E, T), BF16)

    def query_part(i, carried):
        cols = rows_of(i)
        dqkvt[0:E, cols] = (dqt[:, cols] * qgain_col[0:E]).astype(BF16)
        return carried + jnp.sum(dqt[:, cols] * qpre[:, cols], axis=1, keepdims=True)

    scale_terms = lax.fori_loop(0, S, query_part, jnp.zeros((E, 1), F32))

    gq, cqu, gall = ref["gq"], ref["cqu"], ref["gall"]

    CH = CW // 2
    lanes = [pl.ds(k * CH, CH) for k in range(2)]

    def qkv_grad(n, carried, k):
        x = near(xa.at[:, tile(n)], "x_cols", 7)[...]
        gq[tile(n), lanes[k]] = dot(dqkvt[lanes[k], :], x).T.astype(BF16)
        return carried

    QR = q * SR
    line_q = [
        Line(
            lambda d, k=k: gq.at[pl.ds(pl.multiple_of(d * QR, 16), QR), lanes[k]],
            lambda slot, k=k: cqu.at[slot, :, lanes[k]],
            "q_rows",
        )
        for k in range(2)
    ]

    def q_grads(k):
        lax.fori_loop(0, NW, functools.partial(qkv_grad, k=k), 0)
        line_q[k].begin()

    def q_last(k):
        for n in range(1, len(strides)):
            line_q[k].step(n)
        own_q(k)

    for k in range(2):
        event(f"qg{k}", functools.partial(q_grads, k))
        event(f"Q0{k}", functools.partial(line_q[k].step, 0))
        event(f"Q1{k}", functools.partial(q_last, k))
    sums, landed, late, late_landed = (ref[k] for k in ("sums", "landed", "late", "late_landed"))

    class Total:
        def __init__(self, held, arrivals, stages):
            self.held, self.arrivals, self.stages, count = held, arrivals, [], 0
            for n, stage in enumerate(stages):
                moves_n = []
                for to in stage:
                    copy = links.copy(held.at[n], arrivals.at[count], to)
                    moves_n.append((copy, count))
                    count += 1
                self.stages.append(moves_n)

        def begin(self, n):
            for moved, _ in self.stages[n]:
                moved.start()

        def end(self, n):
            total = self.held[n]
            for moved, at in self.stages[n]:
                moved.arrived()
                total = total + self.arrivals[at]
            self.held[n + 1] = total

    on_b = [peer(u, c, b_off[db]) for db in range(1, q)]
    on_u = [peer(u_off[du], c, b) for du in range(1, U)]
    on_a = [[device(r, across(k), b)] for k in strides]
    total = Total(sums, landed, on_a + [on_b, on_u, [sibling]])
    line_all = [device(r, (a + k) % A, b) for k in range(1, A)]
    wide_u = [device(u2 * 2 + c, (a + k) % A, b) for u2 in u_off for k in range(A)][1:]
    late_stages = [wide_u] if U * A <= 16 else [line_all, on_u]
    late_total = Total(late, late_landed, late_stages + [on_b, [sibling]])

    def late_step(n):
        late_total.end(n)
        if n + 1 < len(late_total.stages):
            late_total.begin(n + 1)


    def total_begin():
        ones = jnp.ones((8, T), BF16)
        head_sums = dot_nt(ones, dqkvt[...])
        biascat[...] = head_sums

        def place_sums(k):
            small[6:7, k * E : (k + 1) * E] = biascat[0:1, 0:E]
            small[7:8, k * E : (k + 1) * E] = biascat[0:1, 2 * E : 3 * E]

        for k in range(S):
            pl.when(g == k)(functools.partial(place_sums, k))
        small[5:6, 0:E] = jnp.transpose(jnp.broadcast_to(scale_terms, (E, 128)))[0:1, :]
        sums[0] = small[...]
        total.begin(0)

    def total_step(n):
        total.end(n)
        if n + 1 < len(total.stages):
            total.begin(n + 1)

    event("t", total_begin)
    for n in range(len(total.stages)):
        event(f"t{n}", functools.partial(total_step, n))
    for n in range(len(late_total.stages)):
        event(f"L{n}", functools.partial(late_step, n))

    ags, arc = ref["ags"], ref["arc"]

    def slot_of(n, rows):
        page, row = divmod(n * HALF, D)
        return w3.at[page, row : row + rows]

    order = [(u2, b2) for u2 in range(U) for b2 in range(q)]
    taken = {0: 0, 1: 0, 2: 0}
    if H > 1:
        taken[2] = 3 * um * A2 * q * SRH
    usable = [
        n
        for n in range(2 * U * q, 3 * D // HALF)
        if n * HALF % D >= taken[n * HALF // D]
        and (n * HALF // D != 1 or n * HALF % D + HALF <= D - 3 * qm * A2 * SR)
    ]
    core_a = {}
    for n, (u2, b2) in enumerate(order):
        core_a[u2, b2] = links.copy(ags.at[pl.ds(n * L, L)], slot_of(2 * n, L), sibling)
    dtok = ref["dtok"]

    def partial_rows(m, carried, others):
        block = block_of(m // q, 1 - c if others else c, m % q)
        dtok[...] = dqkvt[:, rows_of(block)].T
        for k in range(NW):
            at = slice(k * W, (k + 1) * W)
            part = dot_nt(dtok[...], wq[at, :]).astype(BF16)
            target = ags if others else arc
            target[rows_of(m), at] = part
        if others:
            for j, key in enumerate(order):
                pl.when(m == j)(core_a[key].start)
        return carried

    def partial_others():
        for group in (own_x, pass_x, sib_x):
            for moved in group.values():
                moved.sent()
                links.copies.remove(moved)
        pl.semaphore_wait(freed_again, len(writers))
        lax.fori_loop(0, U * q, functools.partial(partial_rows, others=True), 0)

    event("ago", partial_others)
    event("agm", lambda: lax.fori_loop(0, U * q, functools.partial(partial_rows, others=False), 0))


    def part(u2, b2, h):
        return arc.at[half_rows(u2 * q + b2, h)]

    afb, afu, asb, asu, landing = {}, {}, {}, {}, {}

    def land(key):
        landing[key] = slot_of(usable.pop(0), HALF)
        return landing[key]

    for db in range(1, q):
        to = peer(u, c, b_off[db])
        for u2 in range(U):
            afb[db, u2] = links.copy(part(u2, b_off[db], 0), land(("fb", db, u2)), to)
        asb[db] = links.copy(part(u, b_off[db], 1), land(("sb", db)), to)
    for du in range(1, U):
        to = peer(u_off[du], c, b)
        for b2 in range(q):
            afu[du, b2] = links.copy(part(u_off[du], b2, 1), land(("fu", du, b2)), to)
        asu[du] = links.copy(part(u_off[du], b, 0), land(("su", du)), to)

    def add_rows(target, other, count):
        def step(i, carried):
            add_into(target.at[strip(i)], other.at[strip(i)])
            return carried

        lax.fori_loop(0, count // STEP, step, 0)

    def rows_core():
        for u2, b2 in order:
            core_a[u2, b2].arrived()
            add_rows(arc.at[rows_of(u2 * q + b2)], slot_of(2 * order.index((u2, b2)), L), L)
        start_all(*afb.values(), *afu.values())

    def rows_on_b_1():
        for db in range(1, q):
            for u2 in range(U):
                afb[db, u2].arrived()
                add_rows(part(u2, b, 0), landing["fb", db, u2], HALF)
        start_all(*asu.values())

    def rows_on_u_1():
        for du in range(1, U):
            for b2 in range(q):
                afu[du, b2].arrived()
                add_rows(part(u, b2, 1), landing["fu", du, b2], HALF)
        start_all(*asb.values())

    event("ac", rows_core)
    event("ab", rows_on_b_1)
    event("au", rows_on_u_1)

    wide, q_across, q_core = {}, {}, {}
    for k in range(2):
        for db in range(1, q):
            rows = pl.ds(pl.multiple_of(a * QR + b_off[db] * SR, 16), SR)
            wide[k, db] = links.copy(
                gq.at[rows, lanes[k]], gall.at[g, :, lanes[k]], device(r, a, b_off[db])
            )
        at = gall.at[pl.ds(r * q, q), :, lanes[k]]
        for du in range(1, U):
            q_across[k, du] = links.copy(at, at, peer(u_off[du], c, b))
        for du in range(U):
            at = gall.at[pl.ds((u_from[du] * 2 + c) * q, q), :, lanes[k]]
            q_core[k, du] = links.copy(at, at, sibling)

    def own_q(k):
        for db in range(1, q):
            wide[k, db].start()
        rows = pl.ds(pl.multiple_of(a * QR + b * SR, 16), SR)
        gall[g, :, lanes[k]] = gq[rows, lanes[k]]

    def across_q(k):
        for db in range(1, q):
            wide[k, db].arrived()
        start_all(*[q_across[k, du] for du in range(1, U)], q_core[k, 0])

    def core_q(k):
        for du in range(1, U):
            q_across[k, du].arrived()
            q_core[k, du].start()

    for k in range(2):
        event(f"Q2{k}", functools.partial(across_q, k))
        event(f"Q3{k}", functools.partial(core_q, k))

    go = ref["go"]
    spread, core_go, partials = {}, {}, {}
    for w in range(3):
        piece = rc.at[w, a, b, my_rows]
        for du in range(1, U):
            to = peer(u_off[du], c, b)
            if H > 1:
                spread[w, du] = links.copy(piece, go.at[w, my_rows, own_half], to)
            else:
                partials[w, du] = links.copy(piece, ref["ru"].at[du - 1, w], to)
        at = go.at[w, :, own_half]
        core_go[w] = links.copy(at, at, sibling)

    def own_go(w):
        for (w2, du), moved in partials.items():
            if w2 == w:
                moved.start()
        for (w2, du), moved in partials.items():
            if w2 == w:
                moved.arrived()
                moved.sent()
                links.copies.remove(moved)
        for (w2, du), moved in partials.items():
            if w2 == w:
                add_into(rc.at[w, a, b, my_rows], near(ref["ru"].at[du - 1, w], "c_rows", 7))
        for (w2, du), moved in spread.items():
            if w2 == w:
                moved.start()
        go[w, my_rows, own_half] = rc[w, a, b, my_rows]

    def last_lines(w):
        for n in range(1, len(strides)):
            lines[w].step(n)
        own_go(w)

    def core_go_on(w):
        for (w2, du), moved in spread.items():
            if w2 == w:
                moved.arrived()
        core_go[w].start()

    for w in range(3):
        event(f"h{w}1", functools.partial(last_lines, w))
        event(f"k{w}", functools.partial(core_go_on, w))

    def rows_end():
        for db in range(1, q):
            asb[db].arrived()
            add_rows(part(u, b, 1), landing["sb", db], HALF)
        for du in range(1, U):
            asu[du].arrived()
            add_rows(part(u, b, 0), landing["su", du], HALF)
        small[0:1, :] = jnp.zeros((1, D), F32)
        lax.fori_loop(0, L // STEP, tok_back, 0)
        late[0] = small[0:1, :]
        late_total.begin(0)
        back_tok.start()
        pl.when(stays)(keep_tok)

    def tok_back(i, carried):
        x = tok[strip(i), :].astype(F32)
        grad = arc[pl.ds(pl.multiple_of((u * q + b) * L + i * STEP, STEP), STEP), :].astype(F32)
        inverse = unit(x)
        normed = x * inverse
        small[0:1, :] += jnp.sum(grad * normed, axis=0, keepdims=True)
        scaled = grad * gain_attn
        mean = jnp.mean(scaled * normed, axis=-1, keepdims=True)
        ref["gtb"][strip(i), :] = (mg[strip(i), :] + inverse * (scaled - normed * mean)).astype(BF16)
        return carried

    back_tok = links.copy(ref["gtb"], ref["gtok"], origin, moves, moves)

    def keep_tok():
        kept = local(ref["gtb"], ref["gtok"], 0)
        kept.start()
        kept.wait()

    event("end", rows_end)
    names = [name for name in SECOND[SECOND.index("BX") + 1 :] if name in events]
    play(names + [name for name in events if name not in names])
    ref["g_small"][...] = sums[len(total.stages)]
    ref["g_small"][0:1, :] = late[len(late_total.stages)]
    for w in range(3):
        core_go[w].arrived()
    for moved in q_core.values():
        moved.arrived()
    back_out.arrived()
    back_tok.arrived()

    lax.fori_loop(0, S, o_sent, 0)

    def m_sent(k, carried):
        m_copy(k).sent()
        return carried

    lax.fori_loop(1, S, m_sent, 0)
    for moved in links.copies:
        moved.sent()
    return links.used


def shards(
    R,
    S,
    tokens,
    lengths,
    parents,
    w_query,
    w_key,
    w_value,
    w_out,
    w_up,
    w_down,
    gain_attn,
    gain_ff,
    query_scale,
    bias_query,
    bias_value,
    bias_out,
    bias_up,
    bias_down,
    cotangent,
):
    L, D = tokens.shape
    SR = w_query.shape[0]
    HG = HEADS // S
    E = HG * HEAD_DIM
    CW = -(-3 * E // 128) * 128
    q, U, A, T = S // R, R // 2, R, S * L
    H = U if SR % (16 * U) == 0 else 1
    SRH = SR // H
    DH = D // 2
    NS = 8
    segments = lengths.shape[1]
    dims = dict(R=R, S=S, L=L, D=D, HG=HG, E=E, CW=CW, SR=SR, H=H, SRH=SRH, segments=segments)

    operands = dict(
        tokens=tokens, cotangent=cotangent, w_query=w_query, w_key=w_key, w_value=w_value,
        w_out=w_out, w_up=w_up, w_down=w_down, lengths=lengths, parents=parents,
        gain_attn=gain_attn, gain_ff=gain_ff, query_scale=query_scale, bias_query=bias_query,
        bias_value=bias_value, bias_out=bias_out, bias_up=bias_up, bias_down=bias_down,
    )
    outputs = dict(
        out=((L, D), BF16), gtok=((L, D), BF16), go=((3, SR, D), BF16),
        gall=((S, SR, CW), BF16), g_small=((NS, D), F32),
    )
    um = max(U - 1, 1)
    peers = q + U + A + (U * A if U * A <= 16 else 0)
    line_steps = A.bit_length() - 1
    scratch = dict(
        tok=((L, D), BF16), cot=((L, D), BF16), tabs=((8, 128), F32),
        wq=((D, CW), BF16), w3=((3, D, D), BF16), xa=((T, D), BF16),
        qkvf=((CW, L), F32), qpre=((E, T), F32), qt=((HG, 128, T), BF16),
        keys=((HG, T, 128), BF16), kt=((HG, HEAD_DIM, T), BF16),
        vals=((HG, T, 128), BF16), vt=((HG, HEAD_DIM, T), BF16),
        ot=((E, T), F32), otb=((E, T), BF16), lse=((HG, 8, T), F32), oa=((D, L), BF16),
        otok=((L, D), BF16), mid=((L, D), F32), ffin=((L, D), BF16), up=((L, D), F32),
        hid=((L, D), BF16), outb=((L, D), BF16),
        mg=((L, D), F32), og=((L, D), BF16), mgt=((D, L), BF16), dot_t=((E, T), BF16),
        small=((NS, D), F32), gp=((3, D, DH), BF16),
        rc=((3, A, q, SR, DH), BF16),
        cu=((A - 1, 3, SRH, DH), BF16), delta=((HG, 8, T), F32), dqkvt=((CW, T), BF16),
        dkt=((E, 2 * L), F32), dvt=((E, 2 * L), F32),
        gains=((8, D), F32), biascat=((8, CW), F32), qgain=((8, CW), F32), tab=((8, 128), F32),
        ags=((T // 2, D), BF16), arc=((T // 2, D), BF16),
        dtok=((L, CW), BF16),
        gq=((D, CW), BF16), cqu=((A - 1, q * SR, CW), BF16),
        sums=((line_steps + 4, NS, D), F32), landed=((line_steps + q + U, NS, D), F32),
        late=((5, 1, D), F32), late_landed=((peers, 1, D), F32),
    )
    if H == 1:
        scratch["ru"] = ((um, 3, SR, DH), BF16)
    held = [jax.ShapeDtypeStruct(*v) for k, v in scratch.items() if k not in ("ags", "arc")]
    dims["fits"] = sum(v.size * v.dtype.itemsize for v in held) <= VMEM_BYTES - (6 << 20)
    results = len(outputs)
    distant = ["out", "gtok"]
    if dims["fits"]:
        scratch.pop("ags")
        scratch.pop("arc")
    else:
        for name in [k for k in ("xa", "cu", "ru") if k in scratch]:
            outputs[name] = scratch.pop(name)
            distant.append(name)
        scratch["x_rows"] = ((L, D), BF16)
        scratch["x_cols"] = ((T, 256), BF16)
        scratch["c_rows"] = ((SRH, DH), BF16)
    if U == 2:
        scratch["lent_tok"] = scratch["lent_cot"] = ((L, D), BF16)
    names = list(operands) + list(outputs) + list(scratch)
    names += ["send_sems", "recv_sems", "local_sems", "freed", "freed_again"]

    counted = [1024]

    def kernel(*refs):
        named = dict(zip(names, refs))
        for later, earlier in (("fg", "up"), ("dqt", "ot"), ("ug", "otok"), ("gtb", "ffin")):
            named[later] = named[earlier]
        named["wqt"] = named["dqkvt"].at[:, 0:D]
        if dims["fits"]:
            named["ags"] = named["xa"].at[pl.ds(0, T // 2)]
            named["arc"] = named["xa"].at[pl.ds(T // 2, T // 2)]
        counted[0] = layer_kernel(dims, named)

    whole = pl.BlockSpec(memory_space=pltpu.VMEM)
    far = ("tokens", "cotangent", "w_query", "w_key", "w_value", "w_out", "w_up", "w_down")
    def call(*operands):
        return pl.pallas_call(
        kernel,
        out_shape=[jax.ShapeDtypeStruct(*shape) for shape in outputs.values()],
        in_specs=[pl.BlockSpec(memory_space=pl.ANY) if k in far else whole for k in operands],
        out_specs=[pl.BlockSpec(memory_space=pl.ANY) if k in distant else whole for k in outputs],
        scratch_shapes=[pltpu.VMEM(*shape) for shape in scratch.values()]
        + [pltpu.SemaphoreType.DMA((counted[0],))] * 2
        + [pltpu.SemaphoreType.DMA((8,))]
        + [pltpu.SemaphoreType.REGULAR] * 2,
        compiler_params=pltpu.CompilerParams(
            collective_id=0, has_side_effects=True, vmem_limit_bytes=VMEM_BYTES
        ),
    )(*operands)

    jax.eval_shape(call, *operands.values())
    made = call(*operands.values())
    out, gtok, go, gall, g_small = made[:results]

    def finish(out, gtok, go, gall, sums, scale, *refs):
        outs, vectors, held, sems = refs[0:8], refs[8:16], refs[16:26], refs[26]
        came = [out, gtok, gall, go]
        loads = [pltpu.make_async_copy(came[n], held[n], sems.at[n]) for n in range(4)]
        left = [held[0], held[1], *held[4:10]]
        stores = [pltpu.make_async_copy(left[n], outs[n], sems.at[4 + n]) for n in range(8)]
        for n in (2, 3, 0, 1):
            loads[n].start()
        for n, at in ((0, 0), (1, 1), (3, 6), (4, 7), (5, 2), (6, 3), (7, 4)):
            vectors[n][...] = sums[at : at + 1, :].reshape(D)
        terms = sum(sums[5:6, hd * HEAD_DIM : (hd + 1) * HEAD_DIM] for hd in range(HG))
        gate = jax.nn.sigmoid(scale[...].reshape(1, HEAD_DIM)) * (query_base / math.sqrt(HEAD_DIM))
        vectors[2][...] = (terms * gate).reshape(HEAD_DIM)
        loads[2].wait()
        for n in range(3):
            for g2 in range(S):
                mine = held[2][g2, :, n * E : (n + 1) * E]
                held[4 + n][:, g2 * E : (g2 + 1) * E] = mine.astype(F32)
            stores[2 + n].start()
        loads[3].wait()
        for w in range(3):
            held[7 + w][...] = held[3][w].astype(F32)
            stores[5 + w].start()
        for n in range(2):
            loads[n].wait()
            stores[n].start()
        for copy in stores:
            copy.wait()

    distant = pl.BlockSpec(memory_space=pl.ANY)
    final = [((L, D), BF16)] * 2 + [((SR, D), F32)] * 6 + [((D,), F32)] * 8
    final[10] = ((HEAD_DIM,), F32)
    held = [((L, D), BF16)] * 2 + [((S, SR, CW), BF16), ((3, SR, D), BF16)] + [((SR, D), F32)] * 6
    return pl.pallas_call(
        finish,
        out_shape=[jax.ShapeDtypeStruct(*shape) for shape in final],
        in_specs=[distant] * 4 + [whole] * 2,
        out_specs=[distant] * 8 + [whole] * 8,
        scratch_shapes=[pltpu.VMEM(*shape) for shape in held] + [pltpu.SemaphoreType.DMA((12,))],
        compiler_params=pltpu.CompilerParams(vmem_limit_bytes=VMEM_BYTES),
    )(out, gtok, go, gall, g_small, query_scale)


def solution(mesh):
    rows, line, copied = P(("rep", "shard"), None), P("shard", None), P()
    in_specs = (rows, P("rep", None), P("rep", None)) + (line,) * 6 + (copied,) * 8 + (rows,)
    out_specs = (rows, rows) + (line,) * 6 + (copied,) * 8
    body = functools.partial(shards, mesh.shape["rep"], mesh.shape["shard"])
    return jax.shard_map(
        body, mesh=mesh, in_specs=in_specs, out_specs=out_specs, check_vma=False
    )
```

```python
import functools
import math
import types

import jax
import jax.numpy as jnp
from jax import lax
from jax.experimental import pallas as pl
from jax.experimental.pallas import tpu as pltpu
from jax.sharding import PartitionSpec as P

HEADS = 16
HEAD_DIM = 80
MESH = pl.DeviceIdType.MESH
F32 = jnp.float32
BF16 = jnp.bfloat16

norm_eps = 1e-06
query_base = 1.442695
masked_score = -1e30
LABELS = 16
VMEM_BYTES = 64 << 20
SECOND = (
    "wg0", "wg2", "out", "cs0", "mwait", "wg1", "delta", "B1", "cs2", "B2", "cs1", "release", "BX",
    "qg0", "t", "qg1", "f2", "ago", "f0", "agm", "t0", "g2", "ac", "Q00", "f1", "g0", "Q01", "ab",
    "Q10", "Q11", "h00", "g1", "Q20", "au", "Q21", "h20", "Q30", "h01", "t1", "h10", "end", "h21",
    "h11", "t2", "L0", "L1", "k0", "t3", "k1", "Q31", "L2", "t4", "k2",
)
FIRST = (
    "tok", "wcat", "own", "carry", "l2", "l1", "coth", "n0", "wcat2", "l0", "n1", "xu0", "s0", "q0",
    "xb0", "xu1", "l10", "l11", "l00", "l12", "tables", "q1", "l20", "l01", "xp1", "xp0", "q2",
    "turnq", "xb1", "s00", "s20", "s10", "l21", "l02", "s12", "project", "l22", "s02", "cot", "A0",
    "A1", "c02", "s21", "s01", "c10", "A2", "c00", "A3", "c01", "s11", "s22", "AX", "c21", "c20",
    "c12", "owait", "F0", "s1", "F1", "s2", "c11", "c22", "F2",
)


def dot(left, right):
    return jnp.dot(left, right, preferred_element_type=F32)


def dot_nt(left, right):
    return lax.dot_general(left, right, (((1,), (1,)), ((), ())), preferred_element_type=F32)


def steps(count, body):
    for i in range(count):
        body(i, 0)


def when(condition, body):
    if condition is True:
        body()
    elif condition is not False:
        pl.when(condition)(body)


class Copy:
    def __init__(self, make, sends, receives):
        self.make, self.sends, self.receives = make, sends, receives

    def start(self):
        when(self.sends, lambda: self.make().start())

    def arrived(self):
        when(self.receives, lambda: self.make().wait_recv())

    def sent(self):
        when(self.sends, lambda: self.make().wait_send())


class Links:
    def __init__(self, send_sems, recv_sems):
        self.send_sems, self.recv_sems, self.used, self.copies = send_sems, recv_sems, 0, []

    def block(self, count):
        first = self.used
        self.used += count
        return first

    def copy(self, src, dst, device, sends=True, receives=True, index=None, keep=True):
        if index is None:
            index = self.block(1)

        def make():
            return pltpu.make_async_remote_copy(
                src_ref=src,
                dst_ref=dst,
                send_sem=self.send_sems.at[index],
                recv_sem=self.recv_sems.at[index],
                device_id=device,
                device_id_type=MESH,
            )

        made = Copy(make, sends, receives)
        if keep:
            self.copies.append(made)
        return made


def layer_kernel(dims, refs):
    R, S, L, D = dims.R, dims.S, dims.L, dims.D
    HG, E, CW, SR, H, SRH = dims.HG, dims.E, dims.CW, dims.SR, dims.H, dims.SRH
    q, U, A, T = S // R, R // 2, R, S * L
    HD = HEAD_DIM
    HALF, DH = L // 2, D // 2
    W = 256
    NW = D // W
    ref = refs
    r, s = lax.axis_index("rep"), lax.axis_index("shard")
    u, c, a, b = r // 2, r % 2, s // q, s % q

    def rho(i):
        return (i % 2) * (R // 2) + i // 2

    def rho_back(j):
        return (j % (R // 2)) * 2 + j // (R // 2)

    def turned(i, layer):
        return (i + (R // 2) * (layer // (R // 2))) % R

    def place_of(line_block, layer):
        return turned(rho_back(line_block), layer)

    def device(r2, a2, b2):
        return (r2, a2 * q + b2)

    def peer(u2, c2, b2):
        return device(u2 * 2 + c2, a, b2)

    def block_of(u2, c2, b2):
        return rho(turned(u2 * 2 + c2, a)) * q + b2

    def rows_of(blk):
        return pl.ds(pl.multiple_of(blk * L, L), L)

    g = r * q + b
    blk = block_of(u, c, b)
    u_off = [(u + d) % U for d in range(U)]
    b_off = [(b + d) % q for d in range(q)]
    u_from = [(u + U - d) % U for d in range(U)]
    b_from = [(b + q - d) % q for d in range(q)]
    home_r, home_a = place_of(a, rho(r)), rho(r)
    home = device(home_r, home_a, b)
    origin_r, origin_a = rho_back(a), rho(turned(r, a))
    origin = device(origin_r, origin_a, b)
    stays = jnp.logical_and(home_r == r, home_a == a)
    moves = jnp.logical_not(stays)
    apart = jnp.logical_or(home_r != origin_r, home_a != origin_a)
    by_u = U == 2

    def crosses(r2, a2):
        layer = rho(r2)
        return jnp.logical_and(place_of(a2, layer) // 2 != r2 // 2, layer != a2) if by_u else False

    next_r = (1 - u) * 2 + c
    next_home = device(place_of(a, rho(next_r)), rho(next_r), b)
    carrier = device((1 - origin_r // 2) * 2 + origin_r % 2, origin_a, b)
    i_cross, i_carry, carried_in = crosses(r, a), crosses(next_r, a), crosses(origin_r, origin_a)
    direct = jnp.logical_and(moves, jnp.logical_not(i_cross))
    direct_in = jnp.logical_and(moves, jnp.logical_not(carried_in))
    sibling = peer(u, 1 - c, b)
    above = device(r, jnp.minimum(a + 1, A - 1), b)
    below = device(r, jnp.maximum(a - 1, 0), b)
    own_half = pl.ds(pl.multiple_of(c * DH, 128), DH)
    other_half = pl.ds(pl.multiple_of((1 - c) * DH, 128), DH)

    links = Links(ref.send_sems, ref.recv_sems)
    events = {}

    def event(name, job):
        events[name] = job

    def play(names):
        for name in names:
            events.pop(name)()

    def segments_of(order, first, last):
        parts, at = {None: []}, None
        for name in order:
            if name[:1] == first and (name[1:].isdigit() or name == last):
                at = name
                parts[at] = []
            else:
                parts[at].append(name)
        return parts

    def start_all(*copies):
        for moved in copies:
            moved.start()


    local_sems = ref.local_sems

    def local(src, dst, n):
        return pltpu.make_async_copy(src, dst, local_sems.at[n])

    def near(src, name, n):
        if dims.fits or name == "q_rows":
            return src
        copy = local(src, getattr(ref, name), n)
        copy.start()
        copy.wait()
        return getattr(ref, name)

    def shard_rows(a2, b2):
        return pl.ds(pl.multiple_of((a2 * q + b2) * SR, 16), SR)

    w3 = ref.w3
    parts = [held.at[pl.ds(0, SR)] for held in (ref.hid, ref.ffin, ref.outb)]
    near_parts = [local(w, parts[n], n) for n, w in enumerate((ref.w_query, ref.w_key, ref.w_value))]
    own_shards = [
        local(shard, w3.at[w, shard_rows(a, b)], 4 + w)
        for w, shard in enumerate((ref.w_out, ref.w_up, ref.w_down))
    ]
    near_rows = [local(ref.tokens, ref.otok, 3), local(ref.cotangent, ref.og, 7)]
    for copy in near_rows[:1] + near_parts + own_shards + near_rows[1:]:
        copy.start()

    barrier = pltpu.get_barrier_semaphore()

    def greet(where):
        pl.semaphore_signal(barrier, inc=1, device_id=where, device_id_type=MESH)

    for k in range(1, S):
        g2 = (g + k) % S
        greet(device(g2 // q, a, g2 % q))
    for k in range(1, A):
        greet(device(r, (a + k) % A, b))
    spread_out = [(u2, k) for u2 in u_off[1:] for k in range(1, A)] if U * A <= 16 else []
    for u2, k in spread_out:
        greet(device(u2 * 2 + c, (a + k) % A, b))
    pl.when(moves)(lambda: greet(home))
    pl.when(apart)(lambda: greet(origin))
    if by_u:
        pl.when(i_carry)(lambda: greet(next_home))
        pl.when(carried_in)(lambda: greet(carrier))

    gains, biascat, qgain, tab = ref.gains, ref.biascat, ref.qgain, ref.tab
    rows = [ref.gain_attn, ref.gain_ff, ref.bias_out, ref.bias_up, ref.bias_down]
    rows += [ref.bias_query, ref.bias_value]
    for n, row in enumerate(rows):
        gains[n : n + 1, :] = row[...].reshape(1, D)
    segments = dims.segments
    tab[...] = jnp.zeros((8, 128), F32)
    tab[0:1, 0:segments] = ref.lengths[...].astype(F32)
    tab[1:2, 0:segments] = ref.parents[...].astype(F32)
    biascat[...] = jnp.zeros((8, CW), F32)

    def bias_slice(k):
        biascat[0:1, 0:E] = gains[5:6, k * E : (k + 1) * E]
        biascat[0:1, 2 * E : 3 * E] = gains[6:7, k * E : (k + 1) * E]

    for k in range(S):
        pl.when(g == k)(functools.partial(bias_slice, k))
    scale = ref.query_scale[...].reshape(1, HD)
    soft = jnp.maximum(scale, 0.0) + jnp.log(1.0 + jnp.exp(-jnp.abs(scale)))
    qgain[...] = jnp.ones((8, CW), F32)
    for hd in range(HG):
        qgain[0:1, hd * HD : (hd + 1) * HD] = soft * (query_base / math.sqrt(HD))

    wq, wqt, wcat = ref.wq, ref.wqt, ref.gall
    for copy in near_parts:
        copy.wait()

    def cut_columns(r2):
        for b2 in range(q):
            first = (r2 * q + b2) * E
            for n in range(3):
                wcat[b2, :, n * E : (n + 1) * E] = parts[n][:, first : first + E]
            if CW > 3 * E:
                wcat[b2, :, 3 * E : CW] = jnp.zeros((SR, CW - 3 * E), BF16)

    for r2 in range(R):
        pl.when(r == r2)(functools.partial(cut_columns, r2))
    wq[shard_rows(a, b), :] = wcat[b]
    others = S - 1 + A - 1 + len(spread_out) + jnp.where(moves, 1, 0) + jnp.where(apart, 1, 0)
    if by_u:
        others = others + jnp.where(i_carry, 1, 0) + jnp.where(carried_in, 1, 0)
    pl.semaphore_wait(barrier, others)

    for copy in near_rows:
        copy.wait()
    swap_tab = links.copy(ref.tab, ref.tabs, home, moves, moves)
    swap_rows, swap_cot = [], []
    lent_tok, lent_cot = (ref.lent_tok, ref.lent_cot) if by_u else (None, None)
    for left, there, lent_to, pieces in (
        (ref.otok, ref.tok, lent_tok, swap_rows),
        (ref.og, ref.cot, lent_cot, swap_cot),
    ):
        for h in range(2):
            here = pl.ds(h * HALF, HALF)
            src, dst = left.at[here], there.at[here]
            piece = [links.copy(src, dst, home, direct, direct_in)]
            if by_u:
                lent = lent_to.at[here]
                piece.append(links.copy(src, lent, peer(1 - u, c, b), i_cross, i_carry))
                piece.append(links.copy(lent, dst, next_home, i_carry, carried_in))
            pieces.append(piece)

    def swap_begin(pieces):
        for piece in pieces:
            for moved in piece[:2]:
                moved.start()

    def swap_carry(pieces):
        for piece in pieces:
            if by_u:
                piece[1].arrived()
                piece[2].start()

    def swap_end(piece):
        for moved in piece[0::2]:
            moved.arrived()

    def swap_sent(pieces):
        for moved in [m for piece in pieces for m in piece[:2]]:
            moved.sent()
            links.copies.remove(moved)

    def keep_rows():
        for left, there in ((ref.otok, ref.tok), (ref.tab, ref.tabs), (ref.og, ref.cot)):
            there[...] = left[...]


    def tok_begin():
        swap_tab.start()
        swap_begin(swap_rows)

    event("tok", tok_begin)
    event("coth", lambda: start_all(*[piece[1] for piece in swap_cot if by_u]))
    event("carry", lambda: swap_carry(swap_rows))

    def cot_on():
        start_all(*[piece[0] for piece in swap_cot])
        swap_carry(swap_cot)

    event("cot", cot_on)

    wq_rows = shard_rows
    wcat_b = {}
    for db in range(1, q):
        wcat_b[db] = links.copy(
            wcat.at[b_off[db]], wq.at[wq_rows(a, b)], device(r, a, b_off[db])
        )
    up_q, down_q = {}, {}
    for k in range(A - 1):
        for db in range(q):
            low, high = jnp.maximum(a - k, 0), jnp.minimum(a + k, A - 1)
            slot = wq_rows(low, b_from[db])
            up_q[k, db] = links.copy(
                wq.at[slot], wq.at[slot], above,
                jnp.logical_and(a - k >= 0, a < A - 1), a - 1 - k >= 0,
            )
            slot = wq_rows(high, b_from[db])
            down_q[k, db] = links.copy(
                wq.at[slot], wq.at[slot], below,
                jnp.logical_and(a + k <= A - 1, a > 0), a + 1 + k <= A - 1,
            )

    def wq_begin():
        start_all(*wcat_b.values(), up_q[0, 0], down_q[0, 0])

    def wq_side():
        for db in range(1, q):
            wcat_b[db].arrived()
            start_all(up_q[0, db], down_q[0, db])

    event("wcat", wq_begin)
    event("wcat2", wq_side)
    def wq_pass(k):
        for db in range(q):
            up_q[k, db].arrived()
            down_q[k, db].arrived()
            if k + 1 < A - 1:
                up_q[k + 1, db].start()
                down_q[k + 1, db].start()

    for k in range(A - 1):
        event(f"q{k}", functools.partial(wq_pass, k))

    def piece_rows(a2, b2, u2):
        if H == 1:
            return shard_rows(a2, b2)
        return pl.ds(pl.multiple_of((a2 * q + b2) * SR + u2 * SRH, 16), SRH)

    for copy in own_shards:
        copy.wait()
    pl.when(stays)(keep_rows)

    def b_then_u(u2, w):
        return u2 % 2 != a % 2 if w < 2 else False

    up_w, down_w, side_w, own_w, core_w, core_own = {}, {}, {}, {}, {}, {}
    slots = [sign * k for k in range(1, A) for sign in (1, -1)]
    for w in range(3):
        for k in range(A - 1):
            low, high = jnp.maximum(a - k, 0), jnp.minimum(a + k, A - 1)
            at = w3.at[w, piece_rows(low, b, u), own_half]
            up_w[w, k] = links.copy(
                at, at, above, jnp.logical_and(a - k >= 0, a < A - 1), a - 1 - k >= 0
            )
            at = w3.at[w, piece_rows(high, b, u), own_half]
            down_w[w, k] = links.copy(
                at, at, below, jnp.logical_and(a + k <= A - 1, a > 0), a + 1 + k <= A - 1
            )
        by_place = {}

        def sems(kind, place):
            if kind not in by_place:
                by_place[kind] = links.block(A)
            return by_place[kind] + place

        for slot in slots:
            valid = a + slot <= A - 1 if slot > 0 else a + slot >= 0
            a0 = jnp.clip(a + slot, 0, A - 1)
            at = w3.at[w, piece_rows(a0, b, u), own_half]
            for db in range(1, q):
                side_w[w, slot, 0, db] = links.copy(
                    at, at, peer(u, c, b_off[db]), valid, valid, index=sems(("b", db), a0)
                )
            if H > 1:
                for du in range(1, U):
                    side_w[w, slot, du, 0] = links.copy(
                        at, at, peer(u_off[du], c, b), valid, valid, index=sems(("u", du), a0)
                    )
                    for db in range(1, q):
                        sent, came = b_then_u(u, w), b_then_u(u_from[du], w)
                        at = w3.at[w, piece_rows(a0, b_from[db], u), own_half]
                        side_w[w, slot, du, db] = links.copy(
                            at, at, peer(u_off[du], c, b),
                            jnp.logical_and(valid, sent), jnp.logical_and(valid, came),
                            index=sems(("bu", du, db), a0),
                        )
                        at = w3.at[w, piece_rows(a0, b, u_from[du]), own_half]
                        other = jnp.logical_and(valid, jnp.logical_not(came))
                        side_w[w, slot, du, -db] = links.copy(
                            at, at, peer(u, c, b_off[db]), other, other,
                            index=sems(("ub", du, db), a0),
                        )
            at = w3.at[w, pl.ds(pl.multiple_of(a0 * q * SR, 16), q * SR), own_half]
            core_w[w, slot] = links.copy(at, at, sibling, valid, valid, index=sems("core", a0))
        for db in range(1, q):
            at = w3.at[w, shard_rows(a, b), own_half]
            own_w[w, db] = links.copy(at, at, peer(u, c, b_off[db]))
            at = w3.at[w, shard_rows(a, b_from[db]), own_half]
            core_own[w, db] = links.copy(at, at, sibling)

    def w3_line(w, k):
        if k < 0:
            up_w[w, 0].start()
            down_w[w, 0].start()
            return
        up_w[w, k].arrived()
        down_w[w, k].arrived()
        if k + 1 < A - 1:
            up_w[w, k + 1].start()
            down_w[w, k + 1].start()
        for slot in (-(k + 1), k + 1):
            for (w2, slot2, du, db), moved in side_w.items():
                if (w2, slot2) == (w, slot) and (du == 0 or db == 0):
                    moved.start()

    def w3_side(w, k):
        if k < 0:
            for db in range(1, q):
                own_w[w, db].arrived()
                core_own[w, db].start()
            return
        for slot in (-(k + 1), k + 1):
            for db in range(1, q):
                side_w[w, slot, 0, db].arrived()
            if H > 1:
                for du in range(1, U):
                    side_w[w, slot, du, 0].arrived()
                    for db in range(1, q):
                        side_w[w, slot, du, db].start()
                        side_w[w, slot, du, -db].start()

    def w3_core(w, k):
        for slot in (-(k + 1), k + 1):
            if H > 1:
                for du in range(1, U):
                    for db in range(1, q):
                        side_w[w, slot, du, db].arrived()
                        side_w[w, slot, du, -db].arrived()
            core_w[w, slot].start()

    event("own", lambda: start_all(*own_w.values()))
    for w in range(3):
        event(f"l{w}", functools.partial(w3_line, w, -1))
        event(f"s{w}", functools.partial(w3_side, w, -1))
        for k in range(A - 1):
            event(f"l{w}{k}", functools.partial(w3_line, w, k))
            event(f"s{w}{k}", functools.partial(w3_side, w, k))
            event(f"c{w}{k}", functools.partial(w3_core, w, k))

    def w3_whole(w):
        for db in range(1, q):
            core_own[w, db].arrived()
        for slot in slots:
            core_w[w, slot].arrived()

    tok, cot, xa = ref.tok, ref.cot, ref.xa
    gain_attn, gain_ff = gains[0:1, :], gains[1:2, :]
    STEP = 32

    def unit(x):
        return lax.rsqrt(jnp.mean(x * x, axis=-1, keepdims=True) + norm_eps)

    def half_rows(block, h):
        return pl.ds(pl.multiple_of(block * L + h * HALF, HALF), HALF)

    own_x, pass_x, sib_x = {}, {}, {}
    for h in range(2):
        at = xa.at[half_rows(blk, h)]
        for db in range(1, q):
            own_x[h, 0, db] = links.copy(at, at, peer(u, c, b_off[db]))
        for du in range(1, U):
            own_x[h, du, 0] = links.copy(at, at, peer(u_off[du], c, b))
        for du in range(1, U):
            for db in range(1, q):
                if h == 0:
                    at = xa.at[half_rows(block_of(u, c, b_from[db]), h)]
                    pass_x[h, du, db] = links.copy(at, at, peer(u_off[du], c, b))
                else:
                    at = xa.at[half_rows(block_of(u_from[du], c, b), h)]
                    pass_x[h, du, db] = links.copy(at, at, peer(u, c, b_off[db]))
        for du in range(U):
            for db in range(q):
                at = xa.at[half_rows(block_of(u_from[du], c, b_from[db]), h)]
                sib_x[h, du, db] = links.copy(at, at, sibling)

    def norm_half(h):
        swap_end(swap_rows[h])

        def norm_step(i, carried):
            here = pl.ds(pl.multiple_of(h * HALF + i * STEP, STEP), STEP)
            x = tok[here, :].astype(F32)
            there = pl.ds(pl.multiple_of(blk * L + h * HALF + i * STEP, STEP), STEP)
            row = (x * unit(x) * gain_attn).astype(BF16)
            if dims.fits:
                xa[there, :] = row
            else:
                ref.x_rows[here, :] = row
            return carried

        steps(HALF // STEP, norm_step)
        if not dims.fits:
            here = pl.ds(h * HALF, HALF)
            out_of = local(ref.x_rows.at[here], xa.at[half_rows(blk, h)], 7)
            out_of.start()
            out_of.wait()
        start_all(*[m for (h2, *_), m in own_x.items() if h2 == h], sib_x[h, 0, 0])

    def rows_on_b(h):
        for db in range(1, q):
            own_x[h, 0, db].arrived()
            if h == 0:
                start_all(*[pass_x[0, du, db] for du in range(1, U)])
            sib_x[h, 0, db].start()

    def rows_on_u(h):
        for du in range(1, U):
            own_x[h, du, 0].arrived()
            if h == 1:
                start_all(*[pass_x[1, du, db] for db in range(1, q)])
            sib_x[h, du, 0].start()

    def rows_passed(h):
        for du in range(1, U):
            for db in range(1, q):
                pass_x[h, du, db].arrived()
                sib_x[h, du, db].start()

    for h in range(2):
        event(f"n{h}", functools.partial(norm_half, h))
        event(f"xb{h}", functools.partial(rows_on_b, h))
        event(f"xu{h}", functools.partial(rows_on_u, h))
        event(f"xp{h}", functools.partial(rows_passed, h))

    tables = types.SimpleNamespace()

    def make_tables():
        swap_tab.arrived()
        lane = lax.broadcasted_iota(jnp.int32, (LABELS, 128), 1)
        row = lax.broadcasted_iota(jnp.int32, (LABELS, 128), 0)
        lengths = jnp.broadcast_to(ref.tabs[0:1, :], (LABELS, 128))
        seg_start = jnp.sum(jnp.where(lane < row, lengths, 0.0), axis=1, keepdims=True)
        seg_end = jnp.sum(jnp.where(lane <= row, lengths, 0.0), axis=1, keepdims=True)
        lane = lax.broadcasted_iota(jnp.int32, (128, 128), 1)
        row = lax.broadcasted_iota(jnp.int32, (128, 128), 0)
        parents = jnp.broadcast_to(ref.tabs[1:2, :], (128, 128))
        is_parent = (parents == row.astype(F32)) & (lane > 0) & (lane < segments)
        reach = jnp.where((lane == row) | is_parent, 1.0, 0.0)
        for _ in range(max(1, (segments - 1).bit_length())):
            reach = jnp.minimum(dot(reach.astype(BF16), reach.astype(BF16)), 1.0)
        blocked = ((1.0 - reach[:LABELS, :LABELS]) * masked_score).astype(BF16)
        tables.start, tables.end, tables.blocked = seg_start, seg_end, blocked

    event("tables", make_tables)

    def turn_wq(i, carried):
        here = pl.ds(pl.multiple_of(i * W, W), W)
        wqt[:, here] = wq[here, :].T
        return carried

    event("turnq", lambda: steps(NW, turn_wq))
    bias_col = jnp.transpose(biascat[...])[:, 0:1]
    qgain_col = jnp.transpose(qgain[...])[:, 0:1]
    qkvf, qpre, qt, keys = ref.qkvf, ref.qpre, ref.qt, ref.keys
    kt, vals, vt = ref.kt, ref.vals, ref.vt

    def project(k, carried):
        for j in range(S):

            def wait_rows(j=j):
                du, db, other = (j // 2) // q, (j // 2) % q, j % 2
                if other:
                    for h in range(2):
                        sib_x[h, du, db].arrived()

            pl.when(k == j)(wait_rows)
        du, db, other = (k // 2) // q, (k // 2) % q, k % 2
        block = block_of((u + U - du) % U, (c + other) % 2, (b + q - db) % q)
        cols = rows_of(block)
        x = near(xa.at[cols], "x_rows", 7)[...]
        qkvf[...] = dot_nt(wqt[...], x) + bias_col
        place = block * L + lax.broadcasted_iota(jnp.int32, (LABELS, L), 1)
        place = place.astype(F32)
        onehot = jnp.where((place >= tables.start) & (place < tables.end), 1.0, 0.0)
        far = dot(tables.blocked, onehot.astype(BF16)).astype(BF16)
        for hd in range(HG):
            head = pl.ds(hd * HD, HD)
            pre = qkvf[head, :]
            qpre[head, cols] = pre
            qt[hd, 0:HD, cols] = (pre * qgain_col[hd * HD : (hd + 1) * HD]).astype(BF16)
            qt[hd, HD : HD + LABELS, cols] = far
            qt[hd, HD + LABELS : 128, cols] = jnp.zeros((128 - HD - LABELS, L), BF16)
            key = qkvf[pl.ds(E + hd * HD, HD), :]
            kt[hd, :, cols] = key.astype(BF16)
            wide = jnp.concatenate([key, onehot, jnp.zeros((128 - HD - LABELS, L), F32)], axis=0)
            keys[hd, cols, :] = wide.T.astype(BF16)
            value = qkvf[pl.ds(2 * E + hd * HD, HD), :]
            vt[hd, :, cols] = value.astype(BF16)
            wide = jnp.concatenate([value, jnp.zeros((128 - HD, L), F32)], axis=0)
            vals[hd, cols, :] = wide.T.astype(BF16)
        return carried

    event("project", lambda: steps(S, project))

    ot, otb, lse, oa = ref.ot, ref.otb, ref.lse, ref.oa
    first_o = links.block(S)
    o_slot = pl.ds(pl.multiple_of(g * E, 16), E)

    def o_copy(block):
        r2, b2 = place_of(block // q, a), block % q
        index = first_o + (r2 * q + b2 + S - g) % S
        return links.copy(
            otb.at[:, rows_of(block)], oa.at[o_slot], device(r2, a, b2), index=index, keep=False
        )

    PAIR = 2
    SQ = PAIR * L
    diagonal = lax.broadcasted_iota(jnp.int32, (SQ, SQ), 0) <= lax.broadcasted_iota(
        jnp.int32, (SQ, SQ), 1
    )
    def wide_rows(i):
        return pl.ds(pl.multiple_of(i * SQ, SQ), SQ)

    def attend(i, carried):
        cols = wide_rows(i)
        query = [qt[hd, :, cols] for hd in range(HG)]

        def key_block(j, state, on_diagonal):
            here = wide_rows(j)
            result = []
            for hd in range(HG):
                top, total, acc = state[hd]
                score = dot(keys[hd, here, :], query[hd])
                if on_diagonal:
                    score = jnp.where(diagonal, score, masked_score)
                new_top = jnp.maximum(top, jnp.max(score, axis=0, keepdims=True))
                p = jnp.exp(score - new_top)
                fade = jnp.exp(top - new_top)
                total = total * fade + jnp.sum(p, axis=0, keepdims=True)
                acc = acc * fade + dot(vt[hd, :, here], p.astype(BF16))
                result.append((new_top, total, acc))
            return tuple(result)

        start = tuple(
            (
                jnp.full((1, SQ), masked_score, F32),
                jnp.zeros((1, SQ), F32),
                jnp.zeros((HD, SQ), F32),
            )
            for _ in range(HG)
        )
        state = lax.fori_loop(0, i, functools.partial(key_block, on_diagonal=False), start)
        state = key_block(i, state, True)
        for hd in range(HG):
            top, total, acc = state[hd]
            mixed = acc / total
            head = pl.ds(hd * HD, HD)
            ot[head, cols] = mixed
            otb[head, cols] = mixed.astype(BF16)
            lse[hd, :, cols] = jnp.broadcast_to(top + jnp.log(total), (8, SQ))
        for k in range(PAIR):
            block = i * PAIR + k

            def keep_block(block=block):
                oa[o_slot, :] = otb[:, rows_of(block)]

            pl.when(block == blk)(keep_block)
            pl.when(block != blk)(lambda block=block: o_copy(block).start())
        for j in range(S // PAIR):
            if order.get(f"A{j}"):
                pl.when(i == j)(functools.partial(play, order[f"A{j}"]))
        return carried

    def o_arrived(k, carried):
        links.copy(
            otb.at[:, rows_of(0)], oa.at[o_slot], sibling, index=first_o + k, keep=False
        ).make().wait_recv()
        return carried

    event("owait", lambda: lax.fori_loop(1, S, o_arrived, 0))

    names = [name for name in FIRST if name in events or name[0] in "AF"]
    for k in range(A - 1):
        for at, name in [("turnq", f"q{k}")] + [
            (f"F{w}", f"{kind}{w}{k}") for w in range(3) for kind in "lsc"
        ]:
            if name not in names:
                names.insert(names.index(at), name)
    ff_order = segments_of(names, "F", "FX")
    order = segments_of(ff_order.pop(None), "A", "AX")
    play(order[None])
    lax.fori_loop(0, S // PAIR, attend, 0)
    play(order["AX"])
    def o_sent(i, carried):
        pl.when(i != blk)(lambda: o_copy(i).sent())
        return carried

    otok, mid, ffin, up, hid, outb = ref.otok, ref.mid, ref.ffin, ref.up, ref.hid, ref.outb
    ug, fg, mg, og, mgt = ref.ug, ref.fg, ref.mg, ref.og, ref.mgt
    small = ref.small

    def tile(n):
        return pl.ds(pl.multiple_of(n * W, W), W)

    def turn_o(n, carried):
        otok[:, tile(n)] = oa[tile(n), :].T
        return carried

    swap_sent(swap_rows)
    steps(NW, turn_o)
    play(ff_order["F0"])
    w3_whole(0)

    def out_step(n, carried):
        added = dot(otok[...], w3[0, :, tile(n)]) + gains[2:3, tile(n)]
        mid[:, tile(n)] = tok[:, tile(n)].astype(F32) + added
        return carried

    steps(NW, out_step)

    def strip(i):
        return pl.ds(pl.multiple_of(i * STEP, STEP), STEP)

    def ff_norm(i, carried):
        x = mid[strip(i), :]
        ffin[strip(i), :] = (x * unit(x) * gain_ff).astype(BF16)
        return carried

    steps(L // STEP, ff_norm)
    play(ff_order["F1"])
    w3_whole(1)

    def up_step(n, carried):
        pre = dot(ffin[...], w3[1, :, tile(n)]) + gains[3:4, tile(n)]
        up[:, tile(n)] = pre
        hid[:, tile(n)] = (pre * jax.nn.sigmoid(pre)).astype(BF16)
        return carried

    steps(NW, up_step)
    play(ff_order["F2"])
    w3_whole(2)

    def down_step(n, carried):
        added = dot(hid[...], w3[2, :, tile(n)]) + gains[4:5, tile(n)]
        outb[:, tile(n)] = (mid[:, tile(n)] + added).astype(BF16)
        return carried

    steps(NW, down_step)
    back_out = links.copy(outb, ref.out, origin, moves, moves)

    def keep_out():
        kept = local(outb, ref.out, 0)
        kept.start()
        kept.wait()

    def out_back():
        back_out.start()
        pl.when(stays)(keep_out)

    event("out", out_back)
    for piece in swap_cot:
        swap_end(piece)
    swap_sent(swap_cot)
    small[...] = jnp.zeros_like(small)

    def up_back(n, carried):
        pre = up[:, tile(n)]
        gate = jax.nn.sigmoid(pre)
        grad = dot_nt(cot[...], w3[2, tile(n), :]) * gate * (1.0 + pre * (1.0 - gate))
        grad = grad.astype(BF16)
        ug[:, tile(n)] = grad
        small[3:4, tile(n)] = jnp.sum(grad.astype(F32), axis=0, keepdims=True)
        return carried

    steps(NW, up_back)

    def ff_back(n, carried):
        fg[:, tile(n)] = dot_nt(ug[...], w3[1, tile(n), :])
        return carried

    steps(NW, ff_back)

    def mid_back(i, carried):
        x, grad, above_grad = mid[strip(i), :], fg[strip(i), :], cot[strip(i), :].astype(F32)
        inverse = unit(x)
        normed = x * inverse
        small[1:2, :] += jnp.sum(grad * normed, axis=0, keepdims=True)
        scaled = grad * gain_ff
        mean = jnp.mean(scaled * normed, axis=-1, keepdims=True)
        total = above_grad + inverse * (scaled - normed * mean)
        mg[strip(i), :] = total
        rounded = total.astype(BF16)
        og[strip(i), :] = rounded
        small[2:3, :] += jnp.sum(rounded.astype(F32), axis=0, keepdims=True)
        small[4:5, :] += jnp.sum(above_grad, axis=0, keepdims=True)
        return carried

    steps(L // STEP, mid_back)

    dot_t = ref.dot_t
    first_m = links.block(S)

    def m_copy(k):
        g2 = (g + k) % S
        at = pl.ds(pl.multiple_of(g2 * E, 16), E)
        return links.copy(
            mgt.at[at], dot_t.at[:, rows_of(blk)], device(g2 // q, a, g2 % q),
            index=first_m + k, keep=False,
        )

    def mixed_step(k, carried):
        at = pl.ds(pl.multiple_of(((g + k) % S) * E, 16), E)
        mgt[at, :] = dot_nt(w3[0, at, :], og[...]).astype(BF16)
        pl.when(k < S)(lambda: m_copy(k).start())
        return carried

    for k in range(1, S + 1):
        mixed_step(k, 0)
    dot_t[:, rows_of(blk)] = mgt[pl.ds(pl.multiple_of(g * E, 16), E), :]

    freed, freed_again = ref.freed, ref.freed_again
    writers = [sibling] + [peer(u, c, v) for v in b_off[1:]] + [peer(v, c, b) for v in u_off[1:]]

    def release(sem):
        for where in writers:
            pl.semaphore_signal(sem, inc=1, device_id=where, device_id_type=MESH)

    for group in (wcat_b, up_w, down_w, side_w, own_w, core_w, core_own):
        for moved in group.values():
            moved.sent()
            links.copies.remove(moved)
    release(freed)

    gp, rc = ref.gp, ref.rc
    rcin = [w3.at[0, :, 0:DH], w3.at[0, :, DH:D], w3.at[1, :, 0:DH]]
    core_g = [links.copy(gp.at[w], rcin[w], sibling) for w in range(3)]

    def weight_grad(w, left, right):
        if left is not None:

            def turn(n, carried):
                oa[tile(n), :] = left[:, tile(n)].T
                return carried

            steps(NW, turn)

        def step(n, carried):
            here = pl.ds(pl.multiple_of(n * SR, 16), SR)
            side = oa[here, :]
            gp[w, here, :] = dot(side, right[:, other_half]).astype(BF16)
            rc[w, n // q, n % q] = dot(side, right[:, own_half]).astype(BF16)
            return carried

        steps(S, step)

    def m_arrived(k, carried):
        m_copy(k).arrived()
        return carried

    A2 = A // 2
    u_rows = [pl.ds(pl.multiple_of(v * SRH, 16), SRH) for v in u_off]
    my_rows = u_rows[0]
    qm, um = q - 1, U - 1

    def t1b(w, db, a2):
        at = D - 3 * qm * A2 * SR + ((w * qm + db - 1) * A2 + a2) * SR
        assert at >= 0
        return w3.at[1, at : at + SR, DH:D]

    def t1u(w, du, a2, b2):
        at = (((w * um + du - 1) * A2 + a2) * q + b2) * SRH
        assert at + SRH <= D
        return w3.at[2, at : at + SRH, 0:DH]

    def t2b(w, db, a2):
        at = ((w * qm + db - 1) * A2 + a2) * SRH
        return w3.at[2, at : at + SRH, DH:D]

    def t2u(w, du, a2):
        at = (3 * qm * A2 + (w * um + du - 1) * A2 + a2) * SRH
        assert at + SRH <= D
        return w3.at[2, at : at + SRH, DH:D]

    first_b, first_u, second_b, second_u = {}, {}, {}, {}
    for w in range(3):
        for a2 in range(A2):
            for db in range(1, q):
                to = peer(u, c, b_off[db])
                first_b[w, db, a2] = links.copy(rc.at[w, a2, b_off[db]], t1b(w, db, a2), to)
                second_b[w, db, a2] = links.copy(
                    rc.at[w, A2 + a2, b_off[db], my_rows], t2b(w, db, a2), to
                )
            if H > 1:
                for du in range(1, U):
                    to = peer(u_off[du], c, b)
                    for b2 in range(q):
                        first_u[w, du, a2, b2] = links.copy(
                            rc.at[w, A2 + a2, b2, u_rows[du]], t1u(w, du, a2, b2), to
                        )
                    second_u[w, du, a2] = links.copy(
                        rc.at[w, a2, b, u_rows[du]], t2u(w, du, a2), to
                    )

    def add_into(target, *more):
        total = target[...].astype(F32)
        for other in more:
            total = total + other[...].astype(F32)
        target[...] = total.astype(BF16)

    def core_sum(w):
        core_g[w].arrived()

        def step(n, carried):
            a2, b2 = n // q, n % q
            here = pl.ds(pl.multiple_of(n * SR, 16), SR)
            add_into(rc.at[w, a2, b2], rcin[w].at[here])
            return carried

        steps(S, step)
        for key, moved in list(first_b.items()) + list(first_u.items()):
            if key[0] == w:
                moved.start()

    def side_sum_1(w):
        for db in range(1, q):
            for a2 in range(A2):
                first_b[w, db, a2].arrived()
                add_into(rc.at[w, a2, b], t1b(w, db, a2))
        if H > 1:
            for du in range(1, U):
                for a2 in range(A2):
                    for b2 in range(q):
                        first_u[w, du, a2, b2].arrived()
                        add_into(rc.at[w, A2 + a2, b2, my_rows], t1u(w, du, a2, b2))
        for key, moved in list(second_b.items()) + list(second_u.items()):
            if key[0] == w:
                moved.start()

    def side_sum_2(w):
        for db in range(1, q):
            for a2 in range(A2):
                second_b[w, db, a2].arrived()
                add_into(rc.at[w, A2 + a2, b, my_rows], t2b(w, db, a2))
        if H > 1:
            for du in range(1, U):
                for a2 in range(A2):
                    second_u[w, du, a2].arrived()
                    add_into(rc.at[w, a2, b, my_rows], t2u(w, du, a2))

    def first_grad():
        weight_grad(0, None, og)
        pl.semaphore_wait(freed, len(writers))
        core_g[0].start()

    def next_grad(w, left, right):
        weight_grad(w, left, right)
        core_g[w].start()

    event("wg0", first_grad)
    event("wg1", lambda: next_grad(1, ffin, ug))
    event("wg2", lambda: next_grad(2, hid, cot))
    event("release", lambda: release(freed_again))
    event("mwait", lambda: lax.fori_loop(1, S, m_arrived, 0))
    for w in range(3):
        event(f"cs{w}", functools.partial(core_sum, w))
        event(f"f{w}", functools.partial(side_sum_1, w))

    assert A & (A - 1) == 0
    strides = [1 << n for n in range(A.bit_length() - 1)]

    def across(k):
        return a + k - 2 * k * (a // k % 2)

    class Line:
        def __init__(self, part, landed, near_name):
            self.part, self.landed, self.near_name, self.steps = part, landed, near_name, []
            slot = 0
            for k in strides:
                step = []
                for m in range(A // (2 * k)):
                    mine = a % (2 * k) + 2 * k * m
                    theirs = across(k) % (2 * k) + 2 * k * m
                    copy = links.copy(part(theirs), landed(slot), device(r, across(k), b))
                    step.append((copy, mine, slot))
                    slot += 1
                self.steps.append(step)

        def begin(self, n=0):
            for copy, _, _ in self.steps[n]:
                copy.start()

        def step(self, n):
            for copy, mine, slot in self.steps[n]:
                copy.arrived()
                add_into(self.part(mine), near(self.landed(slot), self.near_name, 7))
            if n + 1 < len(self.steps):
                self.begin(n + 1)

    cu = ref.cu
    lines = []
    for w in range(3):
        lines.append(
            Line(
                lambda d, w=w: rc.at[w, d, b, my_rows],
                lambda slot, w=w: cu.at[slot, w],
                "c_rows",
            )
        )

    def line_begin(w):
        side_sum_2(w)
        lines[w].begin()

    for w in range(3):
        event(f"g{w}", functools.partial(line_begin, w))
        event(f"h{w}0", functools.partial(lines[w].step, 0))

    delta, dqt, dqkvt = ref.delta, ref.dqt, ref.dqkvt
    def make_delta():
        for hd in range(HG):
            head = slice(hd * HD, (hd + 1) * HD)
            total = jnp.sum(dot_t[head, :].astype(F32) * ot[head, :], axis=0, keepdims=True)
            delta[hd, :, :] = jnp.broadcast_to(total, (8, T))
        dqt[...] = jnp.zeros_like(dqt)

    event("delta", make_delta)
    NB = S // PAIR
    starts = [sum(NB - k for k in range(j)) for j in range(NB)]
    pairs = NB * (NB + 1) // 2
    dkt, dvt = ref.dkt, ref.dvt

    def attend_back(n, carried):
        j = sum(jnp.where(n >= start, 1, 0) for start in starts[1:])
        start = sum(jnp.where(n >= starts[k], starts[k] - starts[k - 1], 0) for k in range(1, NB))
        i = n - start + j
        here, cols = wide_rows(j), wide_rows(i)

        def block(on_diagonal):
            for hd in range(HG):
                head = pl.ds(hd * HD, HD)
                score = dot(keys[hd, here, :], qt[hd, :, cols])
                if on_diagonal:
                    score = jnp.where(diagonal, score, masked_score)
                p = jnp.exp(score - lse[hd, 0:1, cols])
                d_out = dot_t[head, cols]
                dp = dot(vals[hd, here, 0:HD], d_out)
                ds = (p * (dp - delta[hd, 0:1, cols])).astype(BF16)
                dv = dot_nt(d_out, p.astype(BF16))
                dk = dot_nt(qt[hd, 0:HD, cols], ds)
                if on_diagonal:
                    dvt[head, :], dkt[head, :] = dv, dk
                else:
                    dvt[head, :] += dv
                    dkt[head, :] += dk
                dqt[head, cols] += dot(kt[hd, :, here], ds)

        pl.when(i == j)(lambda: block(True))
        pl.when(i != j)(lambda: block(False))

        def keep():
            dqkvt[E : 2 * E, here] = dkt[...].astype(BF16)
            dqkvt[2 * E : 3 * E, here] = dvt[...].astype(BF16)

        pl.when(i == NB - 1)(keep)
        for m in range(pairs):
            if back_order.get(f"B{m}"):
                pl.when(n == m)(functools.partial(play, back_order[f"B{m}"]))
        return carried

    names = [name for name in SECOND if name in events or name[0] == "B"]
    first_part = names[: names.index("BX")]
    back_order = segments_of(first_part, "B", "BX")
    play(back_order[None])
    lax.fori_loop(0, pairs, attend_back, 0)
    if CW > 3 * E:
        dqkvt[3 * E :, :] = jnp.zeros((CW - 3 * E, T), BF16)

    def query_part(i, carried):
        cols = rows_of(i)
        dqkvt[0:E, cols] = (dqt[:, cols] * qgain_col[0:E]).astype(BF16)
        return carried + jnp.sum(dqt[:, cols] * qpre[:, cols], axis=1, keepdims=True)

    scale_terms = jnp.zeros((E, 1), F32)
    for i in range(S):
        scale_terms = query_part(i, scale_terms)

    gq, cqu, gall = ref.gq, ref.cqu, ref.gall

    CH = CW // 2
    lanes = [pl.ds(k * CH, CH) for k in range(2)]

    def qkv_grad(n, carried, k):
        x = near(xa.at[:, tile(n)], "x_cols", 7)[...]
        gq[tile(n), lanes[k]] = dot(dqkvt[lanes[k], :], x).T.astype(BF16)
        return carried

    QR = q * SR
    line_q = [
        Line(
            lambda d, k=k: gq.at[pl.ds(pl.multiple_of(d * QR, 16), QR), lanes[k]],
            lambda slot, k=k: cqu.at[slot, :, lanes[k]],
            "q_rows",
        )
        for k in range(2)
    ]

    def q_grads(k):
        steps(NW, functools.partial(qkv_grad, k=k))
        line_q[k].begin()

    def q_last(k):
        for n in range(1, len(strides)):
            line_q[k].step(n)
        own_q(k)

    for k in range(2):
        event(f"qg{k}", functools.partial(q_grads, k))
        event(f"Q0{k}", functools.partial(line_q[k].step, 0))
        event(f"Q1{k}", functools.partial(q_last, k))
    sums, landed, late, late_landed = ref.sums, ref.landed, ref.late, ref.late_landed

    class Total:
        def __init__(self, held, arrivals, stages):
            self.held, self.arrivals, self.stages, count = held, arrivals, [], 0
            for n, stage in enumerate(stages):
                moves_n = []
                for to in stage:
                    copy = links.copy(held.at[n], arrivals.at[count], to)
                    moves_n.append((copy, count))
                    count += 1
                self.stages.append(moves_n)

        def begin(self, n):
            for moved, _ in self.stages[n]:
                moved.start()

        def end(self, n):
            total = self.held[n]
            for moved, at in self.stages[n]:
                moved.arrived()
                total = total + self.arrivals[at]
            self.held[n + 1] = total

    on_b = [peer(u, c, b_off[db]) for db in range(1, q)]
    on_u = [peer(u_off[du], c, b) for du in range(1, U)]
    on_a = [[device(r, across(k), b)] for k in strides]
    total = Total(sums, landed, on_a + [on_b, on_u, [sibling]])
    line_all = [device(r, (a + k) % A, b) for k in range(1, A)]
    wide_u = [device(u2 * 2 + c, (a + k) % A, b) for u2 in u_off for k in range(A)][1:]
    late_stages = [wide_u] if U * A <= 16 else [line_all, on_u]
    late_total = Total(late, late_landed, late_stages + [on_b, [sibling]])

    def late_step(n):
        late_total.end(n)
        if n + 1 < len(late_total.stages):
            late_total.begin(n + 1)


    def total_begin():
        ones = jnp.ones((8, T), BF16)
        head_sums = dot_nt(ones, dqkvt[...])
        biascat[...] = head_sums

        def place_sums(k):
            small[6:7, k * E : (k + 1) * E] = biascat[0:1, 0:E]
            small[7:8, k * E : (k + 1) * E] = biascat[0:1, 2 * E : 3 * E]

        for k in range(S):
            pl.when(g == k)(functools.partial(place_sums, k))
        small[5:6, 0:E] = jnp.transpose(jnp.broadcast_to(scale_terms, (E, 128)))[0:1, :]
        sums[0] = small[...]
        total.begin(0)

    def total_step(n):
        total.end(n)
        if n + 1 < len(total.stages):
            total.begin(n + 1)

    event("t", total_begin)
    for n in range(len(total.stages)):
        event(f"t{n}", functools.partial(total_step, n))
    for n in range(len(late_total.stages)):
        event(f"L{n}", functools.partial(late_step, n))

    ags, arc = ref.ags, ref.arc

    def slot_of(n, rows):
        page, row = divmod(n * HALF, D)
        return w3.at[page, row : row + rows]

    order = [(u2, b2) for u2 in range(U) for b2 in range(q)]
    taken = {0: 0, 1: 0, 2: 0}
    if H > 1:
        taken[2] = 3 * um * A2 * q * SRH
    usable = [
        n
        for n in range(2 * U * q, 3 * D // HALF)
        if n * HALF % D >= taken[n * HALF // D]
        and (n * HALF // D != 1 or n * HALF % D + HALF <= D - 3 * qm * A2 * SR)
    ]
    core_a = {}
    for n, (u2, b2) in enumerate(order):
        core_a[u2, b2] = links.copy(ags.at[pl.ds(n * L, L)], slot_of(2 * n, L), sibling)
    dtok = ref.dtok

    def partial_rows(m, carried, others):
        block = block_of(m // q, 1 - c if others else c, m % q)
        dtok[...] = dqkvt[:, rows_of(block)].T
        for k in range(NW):
            at = slice(k * W, (k + 1) * W)
            part = dot_nt(dtok[...], wq[at, :]).astype(BF16)
            target = ags if others else arc
            target[rows_of(m), at] = part
        if others:
            for j, key in enumerate(order):
                pl.when(m == j)(core_a[key].start)
        return carried

    def partial_others():
        for group in (own_x, pass_x, sib_x):
            for moved in group.values():
                moved.sent()
                links.copies.remove(moved)
        pl.semaphore_wait(freed_again, len(writers))
        steps(U * q, functools.partial(partial_rows, others=True))

    event("ago", partial_others)
    event("agm", lambda: steps(U * q, functools.partial(partial_rows, others=False)))


    def part(u2, b2, h):
        return arc.at[half_rows(u2 * q + b2, h)]

    afb, afu, asb, asu, landing = {}, {}, {}, {}, {}

    def land(key):
        landing[key] = slot_of(usable.pop(0), HALF)
        return landing[key]

    for db in range(1, q):
        to = peer(u, c, b_off[db])
        for u2 in range(U):
            afb[db, u2] = links.copy(part(u2, b_off[db], 0), land(("fb", db, u2)), to)
        asb[db] = links.copy(part(u, b_off[db], 1), land(("sb", db)), to)
    for du in range(1, U):
        to = peer(u_off[du], c, b)
        for b2 in range(q):
            afu[du, b2] = links.copy(part(u_off[du], b2, 1), land(("fu", du, b2)), to)
        asu[du] = links.copy(part(u_off[du], b, 0), land(("su", du)), to)

    def add_rows(target, other, count):
        def step(i, carried):
            add_into(target.at[strip(i)], other.at[strip(i)])
            return carried

        steps(count // STEP, step)

    def rows_core():
        for u2, b2 in order:
            core_a[u2, b2].arrived()
            add_rows(arc.at[rows_of(u2 * q + b2)], slot_of(2 * order.index((u2, b2)), L), L)
        start_all(*afb.values(), *afu.values())

    def rows_on_b_1():
        for db in range(1, q):
            for u2 in range(U):
                afb[db, u2].arrived()
                add_rows(part(u2, b, 0), landing["fb", db, u2], HALF)
        start_all(*asu.values())

    def rows_on_u_1():
        for du in range(1, U):
            for b2 in range(q):
                afu[du, b2].arrived()
                add_rows(part(u, b2, 1), landing["fu", du, b2], HALF)
        start_all(*asb.values())

    event("ac", rows_core)
    event("ab", rows_on_b_1)
    event("au", rows_on_u_1)

    wide, q_across, q_core = {}, {}, {}
    for k in range(2):
        for db in range(1, q):
            rows = pl.ds(pl.multiple_of(a * QR + b_off[db] * SR, 16), SR)
            wide[k, db] = links.copy(
                gq.at[rows, lanes[k]], gall.at[g, :, lanes[k]], device(r, a, b_off[db])
            )
        at = gall.at[pl.ds(r * q, q), :, lanes[k]]
        for du in range(1, U):
            q_across[k, du] = links.copy(at, at, peer(u_off[du], c, b))
        for du in range(U):
            at = gall.at[pl.ds((u_from[du] * 2 + c) * q, q), :, lanes[k]]
            q_core[k, du] = links.copy(at, at, sibling)

    def own_q(k):
        for db in range(1, q):
            wide[k, db].start()
        rows = pl.ds(pl.multiple_of(a * QR + b * SR, 16), SR)
        gall[g, :, lanes[k]] = gq[rows, lanes[k]]

    def across_q(k):
        for db in range(1, q):
            wide[k, db].arrived()
        start_all(*[q_across[k, du] for du in range(1, U)], q_core[k, 0])

    def core_q(k):
        for du in range(1, U):
            q_across[k, du].arrived()
            q_core[k, du].start()

    for k in range(2):
        event(f"Q2{k}", functools.partial(across_q, k))
        event(f"Q3{k}", functools.partial(core_q, k))

    go = ref.go
    spread, core_go, partials = {}, {}, {}
    for w in range(3):
        piece = rc.at[w, a, b, my_rows]
        for du in range(1, U):
            to = peer(u_off[du], c, b)
            if H > 1:
                spread[w, du] = links.copy(piece, go.at[w, my_rows, own_half], to)
            else:
                partials[w, du] = links.copy(piece, ref.ru.at[du - 1, w], to)
        at = go.at[w, :, own_half]
        core_go[w] = links.copy(at, at, sibling)

    def own_go(w):
        for (w2, du), moved in partials.items():
            if w2 == w:
                moved.start()
        for (w2, du), moved in partials.items():
            if w2 == w:
                moved.arrived()
                moved.sent()
                links.copies.remove(moved)
        for (w2, du), moved in partials.items():
            if w2 == w:
                add_into(rc.at[w, a, b, my_rows], near(ref.ru.at[du - 1, w], "c_rows", 7))
        for (w2, du), moved in spread.items():
            if w2 == w:
                moved.start()
        go[w, my_rows, own_half] = rc[w, a, b, my_rows]

    def last_lines(w):
        for n in range(1, len(strides)):
            lines[w].step(n)
        own_go(w)

    def core_go_on(w):
        for (w2, du), moved in spread.items():
            if w2 == w:
                moved.arrived()
        core_go[w].start()

    for w in range(3):
        event(f"h{w}1", functools.partial(last_lines, w))
        event(f"k{w}", functools.partial(core_go_on, w))

    def rows_end():
        for db in range(1, q):
            asb[db].arrived()
            add_rows(part(u, b, 1), landing["sb", db], HALF)
        for du in range(1, U):
            asu[du].arrived()
            add_rows(part(u, b, 0), landing["su", du], HALF)
        small[0:1, :] = jnp.zeros((1, D), F32)
        steps(L // STEP, tok_back)
        late[0] = small[0:1, :]
        late_total.begin(0)
        back_tok.start()
        pl.when(stays)(keep_tok)

    def tok_back(i, carried):
        x = tok[strip(i), :].astype(F32)
        grad = arc[pl.ds(pl.multiple_of((u * q + b) * L + i * STEP, STEP), STEP), :].astype(F32)
        inverse = unit(x)
        normed = x * inverse
        small[0:1, :] += jnp.sum(grad * normed, axis=0, keepdims=True)
        scaled = grad * gain_attn
        mean = jnp.mean(scaled * normed, axis=-1, keepdims=True)
        ref.gtb[strip(i), :] = (mg[strip(i), :] + inverse * (scaled - normed * mean)).astype(BF16)
        return carried

    back_tok = links.copy(ref.gtb, ref.gtok, origin, moves, moves)

    def keep_tok():
        kept = local(ref.gtb, ref.gtok, 0)
        kept.start()
        kept.wait()

    event("end", rows_end)
    names = [name for name in SECOND[SECOND.index("BX") + 1 :] if name in events]
    play(names + [name for name in events if name not in names])
    ref.g_small[...] = sums[len(total.stages)]
    ref.g_small[0:1, :] = late[len(late_total.stages)]
    for w in range(3):
        core_go[w].arrived()
    for moved in q_core.values():
        moved.arrived()
    back_out.arrived()
    back_tok.arrived()

    lax.fori_loop(0, S, o_sent, 0)

    def m_sent(k, carried):
        m_copy(k).sent()
        return carried

    lax.fori_loop(1, S, m_sent, 0)
    for moved in links.copies:
        moved.sent()
    return links.used


def shards(
    R,
    S,
    tokens,
    lengths,
    parents,
    w_query,
    w_key,
    w_value,
    w_out,
    w_up,
    w_down,
    gain_attn,
    gain_ff,
    query_scale,
    bias_query,
    bias_value,
    bias_out,
    bias_up,
    bias_down,
    cotangent,
):
    L, D = tokens.shape
    SR = w_query.shape[0]
    HG = HEADS // S
    E = HG * HEAD_DIM
    CW = -(-3 * E // 128) * 128
    q, U, A, T = S // R, R // 2, R, S * L
    H = U if SR % (16 * U) == 0 else 1
    SRH = SR // H
    DH = D // 2
    NS = 8
    segments = lengths.shape[1]
    dims = types.SimpleNamespace(R=R, S=S, L=L, D=D, HG=HG, E=E, CW=CW, SR=SR, H=H, SRH=SRH, segments=segments)

    operands = dict(
        tokens=tokens, cotangent=cotangent, w_query=w_query, w_key=w_key, w_value=w_value,
        w_out=w_out, w_up=w_up, w_down=w_down, lengths=lengths, parents=parents,
        gain_attn=gain_attn, gain_ff=gain_ff, query_scale=query_scale, bias_query=bias_query,
        bias_value=bias_value, bias_out=bias_out, bias_up=bias_up, bias_down=bias_down,
    )
    outputs = dict(
        out=((L, D), BF16), gtok=((L, D), BF16), go=((3, SR, D), BF16),
        gall=((S, SR, CW), BF16), g_small=((NS, D), F32),
    )
    um = max(U - 1, 1)
    peers = q + U + A + (U * A if U * A <= 16 else 0)
    line_steps = A.bit_length() - 1
    scratch = dict(
        tok=((L, D), BF16), cot=((L, D), BF16), tabs=((8, 128), F32),
        wq=((D, CW), BF16), w3=((3, D, D), BF16), xa=((T, D), BF16),
        qkvf=((CW, L), F32), qpre=((E, T), F32), qt=((HG, 128, T), BF16),
        keys=((HG, T, 128), BF16), kt=((HG, HEAD_DIM, T), BF16),
        vals=((HG, T, 128), BF16), vt=((HG, HEAD_DIM, T), BF16),
        ot=((E, T), F32), otb=((E, T), BF16), lse=((HG, 8, T), F32), oa=((D, L), BF16),
        otok=((L, D), BF16), mid=((L, D), F32), ffin=((L, D), BF16), up=((L, D), F32),
        hid=((L, D), BF16), outb=((L, D), BF16),
        mg=((L, D), F32), og=((L, D), BF16), mgt=((D, L), BF16), dot_t=((E, T), BF16),
        small=((NS, D), F32), gp=((3, D, DH), BF16),
        rc=((3, A, q, SR, DH), BF16),
        cu=((A - 1, 3, SRH, DH), BF16), delta=((HG, 8, T), F32), dqkvt=((CW, T), BF16),
        dkt=((E, 2 * L), F32), dvt=((E, 2 * L), F32),
        gains=((8, D), F32), biascat=((8, CW), F32), qgain=((8, CW), F32), tab=((8, 128), F32),
        ags=((T // 2, D), BF16), arc=((T // 2, D), BF16),
        dtok=((L, CW), BF16),
        gq=((D, CW), BF16), cqu=((A - 1, q * SR, CW), BF16),
        sums=((line_steps + 4, NS, D), F32), landed=((line_steps + q + U, NS, D), F32),
        late=((5, 1, D), F32), late_landed=((peers, 1, D), F32),
    )
    if H == 1:
        scratch["ru"] = ((um, 3, SR, DH), BF16)
    held = [jax.ShapeDtypeStruct(*v) for k, v in scratch.items() if k not in ("ags", "arc")]
    dims.fits = sum(v.size * v.dtype.itemsize for v in held) <= VMEM_BYTES - (6 << 20)
    results = len(outputs)
    distant = ["out", "gtok"]
    if dims.fits:
        scratch.pop("ags")
        scratch.pop("arc")
    else:
        for name in [k for k in ("xa", "cu", "ru") if k in scratch]:
            outputs[name] = scratch.pop(name)
            distant.append(name)
        scratch.update(x_rows=((L, D), BF16), x_cols=((T, 256), BF16), c_rows=((SRH, DH), BF16))
    if U == 2:
        scratch.update(lent_tok=((L, D), BF16), lent_cot=((L, D), BF16))
    names = list(operands) + list(outputs) + list(scratch)
    names += ["send_sems", "recv_sems", "local_sems", "freed", "freed_again"]

    counted = [1024]

    def kernel(*refs):
        named = types.SimpleNamespace(**dict(zip(names, refs)))
        named.fg, named.dqt = named.up, named.ot
        named.ug, named.gtb = named.otok, named.ffin
        named.wqt = named.dqkvt.at[:, 0:D]
        if dims.fits:
            named.ags = named.xa.at[pl.ds(0, T // 2)]
            named.arc = named.xa.at[pl.ds(T // 2, T // 2)]
        counted[0] = layer_kernel(dims, named)

    whole = pl.BlockSpec(memory_space=pltpu.VMEM)
    far = ("tokens", "cotangent", "w_query", "w_key", "w_value", "w_out", "w_up", "w_down")
    def call(*operands):
        return pl.pallas_call(
        kernel,
        out_shape=[jax.ShapeDtypeStruct(*shape) for shape in outputs.values()],
        in_specs=[pl.BlockSpec(memory_space=pl.ANY) if k in far else whole for k in operands],
        out_specs=[pl.BlockSpec(memory_space=pl.ANY) if k in distant else whole for k in outputs],
        scratch_shapes=[pltpu.VMEM(*shape) for shape in scratch.values()]
        + [pltpu.SemaphoreType.DMA((counted[0],))] * 2
        + [pltpu.SemaphoreType.DMA((8,))]
        + [pltpu.SemaphoreType.REGULAR] * 2,
        compiler_params=pltpu.CompilerParams(
            collective_id=0, has_side_effects=True, vmem_limit_bytes=VMEM_BYTES
        ),
    )(*operands)

    jax.eval_shape(call, *operands.values())
    made = call(*operands.values())
    out, gtok, go, gall, g_small = made[:results]

    def finish(out, gtok, go, gall, sums, scale, *refs):
        outs, vectors, held, sems = refs[0:8], refs[8:16], refs[16:26], refs[26]
        came = [out, gtok, gall, go]
        loads = [pltpu.make_async_copy(came[n], held[n], sems.at[n]) for n in range(4)]
        left = [held[0], held[1], *held[4:10]]
        stores = [pltpu.make_async_copy(left[n], outs[n], sems.at[4 + n]) for n in range(8)]
        for n in (2, 3, 0, 1):
            loads[n].start()
        for n, at in ((0, 0), (1, 1), (3, 6), (4, 7), (5, 2), (6, 3), (7, 4)):
            vectors[n][...] = sums[at : at + 1, :].reshape(D)
        terms = sum(sums[5:6, hd * HEAD_DIM : (hd + 1) * HEAD_DIM] for hd in range(HG))
        gate = jax.nn.sigmoid(scale[...].reshape(1, HEAD_DIM)) * (query_base / math.sqrt(HEAD_DIM))
        vectors[2][...] = (terms * gate).reshape(HEAD_DIM)
        loads[2].wait()
        for n in range(3):
            for g2 in range(S):
                mine = held[2][g2, :, n * E : (n + 1) * E]
                held[4 + n][:, g2 * E : (g2 + 1) * E] = mine.astype(F32)
            stores[2 + n].start()
        loads[3].wait()
        for w in range(3):
            held[7 + w][...] = held[3][w].astype(F32)
            stores[5 + w].start()
        for n in range(2):
            loads[n].wait()
            stores[n].start()
        for copy in stores:
            copy.wait()

    distant = pl.BlockSpec(memory_space=pl.ANY)
    final = [((L, D), BF16)] * 2 + [((SR, D), F32)] * 6 + [((D,), F32)] * 8
    final[10] = ((HEAD_DIM,), F32)
    held = [((L, D), BF16)] * 2 + [((S, SR, CW), BF16), ((3, SR, D), BF16)] + [((SR, D), F32)] * 6
    return pl.pallas_call(
        finish,
        out_shape=[jax.ShapeDtypeStruct(*shape) for shape in final],
        in_specs=[distant] * 4 + [whole] * 2,
        out_specs=[distant] * 8 + [whole] * 8,
        scratch_shapes=[pltpu.VMEM(*shape) for shape in held] + [pltpu.SemaphoreType.DMA((12,))],
        compiler_params=pltpu.CompilerParams(vmem_limit_bytes=VMEM_BYTES),
    )(out, gtok, go, gall, g_small, query_scale)


def solution(mesh):
    rows, line, copied = P(("rep", "shard"), None), P("shard", None), P()
    in_specs = (rows, P("rep", None), P("rep", None)) + (line,) * 6 + (copied,) * 8 + (rows,)
    out_specs = (rows, rows) + (line,) * 6 + (copied,) * 8
    body = functools.partial(shards, mesh.shape["rep"], mesh.shape["shard"])
    return jax.shard_map(
        body, mesh=mesh, in_specs=in_specs, out_specs=out_specs, check_vma=False
    )
```
